128 devices in a mesh: gx: 4 (over y), yz: 32 (over x, z, core).
Axes of the slice: x: 4, y: 4, z: 4, core: 2. Of those that a mesh axis runs over, the one named last changes fastest.
Arguments:
- adjoint_seed: float32 [216, 16, 128, 128], P(None, 'gx', 'yz'), may hold values from -6 to 6
- elem_scale: float32 [16, 128, 128], P('gx', 'yz'), may hold values from 1 to 3
- face_coef: float32 [3, 16, 128, 128], P(None, 'gx', 'yz'), may hold values from 0.25 to 1
- fine_block: float32 [216, 216], replicated, may hold values from -0.4375 to 0.4375
- fine_smoother: float32 [216, 216], replicated, may hold values from -0.0546875 to 0.0546875
- mid_block: float32 [64, 64], replicated, may hold values from -0.75 to 0.75
- coarse_block: float32 [8, 8], replicated, may hold values from -4 to 4
- prolong_mid: float32 [216, 64], replicated, may hold values from -0.75 to 0.75
- prolong_low: float32 [64, 8], replicated, may hold values from -2 to 2
- noise_map: float32 [216, 216], replicated, may hold values from -0.4375 to 0.4375
- increments: float32 [16, 128, 128], P('gx', 'yz'), may hold values from -3 to 3
Outputs:
- adjoint_solution: float32 [216, 16, 128, 128], P(None, 'gx', 'yz')
- adjoint_prev: float32 [216, 16, 128, 128], P(None, 'gx', 'yz')
The draws below stay inside these ranges and needn't reach their ends.
All inputs are finite; a program needn't handle non-finite values.
Results may differ from the reference program's by a relative error of at most 0.0001.
Values sent between devices are 32-bit elements; how exact they have to be, the bound alone decides.
No kernel may reach another device: no remote copies, remote signals or barrier semaphores. Data moves between devices by JAX's collectives and lax.ppermute only.
A program may use at most 128 MiB of HBM per device.

```python
import math
import jax
import jax.numpy as jnp
from jax import lax

NF = 6
NM = 4
NC = 2
QF = 216
QM = 64
QC = 8
SWEEPS = 2
COARSE_SWEEPS = 6
NX = 16
NY = 128
NZ = 128


def level_of(key, extent, cuts, low, largest):
    level = 1.0
    for dim, blocks in cuts:
        draws = jax.random.uniform(jax.random.fold_in(jax.random.fold_in(key, 6), dim), (blocks,), jnp.float32, low / len(cuts), largest / len(cuts))
        level = level * jnp.repeat(jnp.exp(draws), extent[dim] // blocks).reshape((-1,) + (1,) * (len(extent) - 1 - dim))
    return level


def gaussian(rng, shape, scale, bound, cuts=(), held_as=jnp.bfloat16):
    entries = scale * jax.random.normal(rng, shape, jnp.float32)
    if cuts:
        entries = entries * level_of(rng, shape, cuts, -0.22, 0.18)
    return jnp.clip(entries, -bound, bound).astype(held_as)


def setup_inputs(seed: int = 0) -> dict:
    key_of = jax.random.split(jax.random.key(seed), 12)
    adjoint_seed = gaussian(key_of[0], (QF, NX, NY, NZ), 1.0, 6.0, ((1, 4), (2, 32)), jnp.float32)
    elem_scale = jnp.clip(jnp.exp(math.log(3.0) - 1.0986123 * jax.random.uniform(key_of[1], (NX, NY, NZ), jnp.float32) ** level_of(key_of[1], (NX, NY, NZ), ((0, 4), (1, 32)), -0.2, 0.2)), 1.0, 3.0)
    face_coef = jnp.clip(jnp.exp(math.log(1.0) - 1.3862944 * jax.random.uniform(key_of[2], (3, NX, NY, NZ), jnp.float32) ** level_of(key_of[2], (3, NX, NY, NZ), ((1, 4), (2, 32)), -0.2, 0.2)), 0.25, 1.0)
    fine_block = gaussian(key_of[3], (QF, QF), QF ** -0.5, 0.4375, (), jnp.float32)
    fine_smoother = gaussian(key_of[4], (QF, QF), (64 * QF) ** -0.5, 0.0546875, (), jnp.float32)
    mid_block = gaussian(key_of[5], (QM, QM), QM ** -0.5, 0.75, (), jnp.float32)
    coarse_block = gaussian(key_of[6], (QC, QC), 2 ** -0.5, 4.0, (), jnp.float32)
    prolong_mid = gaussian(key_of[7], (QF, QM), QM ** -0.5, 0.75, (), jnp.float32)
    prolong_low = gaussian(key_of[8], (QM, QC), QC ** -0.5, 2.0, (), jnp.float32)
    noise_map = gaussian(key_of[9], (QF, QF), QF ** -0.5, 0.4375, (), jnp.float32)
    increments = gaussian(key_of[10], (NX, NY, NZ), 0.5, 3.0, ((0, 4), (1, 32)), jnp.float32)
    return {"adjoint_seed": adjoint_seed, "elem_scale": elem_scale, "face_coef": face_coef, "fine_block": fine_block, "fine_smoother": fine_smoother, "mid_block": mid_block, "coarse_block": coarse_block, "prolong_mid": prolong_mid, "prolong_low": prolong_low, "noise_map": noise_map, "increments": increments}


precise = lax.Precision.HIGHEST
upwind = 0.9
downwind = 0.3


def transpose_apply(matrix, values):
    flattened = values.reshape((values.shape[0], -1))
    result = jnp.einsum("ji,jm->im", matrix, flattened, precision=precise)
    return result.reshape((matrix.shape[1],) + values.shape[1:])


def forward_apply(matrix, values):
    flattened = values.reshape((values.shape[0], -1))
    result = jnp.einsum("ij,jm->im", matrix, flattened, precision=precise)
    return result.reshape((matrix.shape[0],) + values.shape[1:])


def neighbour_terms(nodal, order_nodes, direction):
    element_dim = 2 + direction
    upper_layer = jnp.take(nodal, order_nodes - 1, axis=direction)
    lower_layer = jnp.take(nodal, 0, axis=direction)
    length = upper_layer.shape[element_dim]
    zero_slab = jnp.zeros_like(lax.slice_in_dim(upper_layer, 0, 1, axis=element_dim))
    from_lower = jnp.concatenate([zero_slab, lax.slice_in_dim(upper_layer, 0, length - 1, axis=element_dim)], axis=element_dim)
    from_upper = jnp.concatenate([lax.slice_in_dim(lower_layer, 1, length, axis=element_dim), zero_slab], axis=element_dim)
    return from_lower, from_upper


def assemble(values, matrix, scales, coefficients, order_nodes, neighbours):
    nodal_shape = (order_nodes, order_nodes, order_nodes) + values.shape[1:]
    result = (scales * (4.0 * values + transpose_apply(matrix, values))).reshape(nodal_shape)
    for direction in range(3):
        from_lower, from_upper = neighbours[direction]
        lower_spot = tuple(0 if place == direction else slice(None) for place in range(3))
        upper_spot = tuple(order_nodes - 1 if place == direction else slice(None) for place in range(3))
        result = result.at[lower_spot].add(-(coefficients[direction] * (upwind * from_lower)))
        result = result.at[upper_spot].add(-(coefficients[direction] * (downwind * from_upper)))
    return result.reshape(values.shape)


def adjoint_op(values, matrix, scales, coefficients, order_nodes):
    nodal = values.reshape((order_nodes, order_nodes, order_nodes) + values.shape[1:])
    neighbours = [neighbour_terms(nodal, order_nodes, direction) for direction in range(3)]
    return assemble(values, matrix, scales, coefficients, order_nodes, neighbours)


def fine_sweep(current, target, matrix, smoother, scales, coefficients):
    scaled = (target - adjoint_op(current, matrix, scales, coefficients, NF)) / scales
    return current + 0.25 * scaled + transpose_apply(smoother, scaled)


def point_sweep(current, target, matrix, scales, coefficients, order_nodes):
    return current + 0.2 * (target - adjoint_op(current, matrix, scales, coefficients, order_nodes)) / scales


def reference(adjoint_seed, elem_scale, face_coef, fine_block, fine_smoother, mid_block, coarse_block, prolong_mid, prolong_low, noise_map, increments):
    fine_field = jnp.zeros_like(adjoint_seed)
    for sweep_index in range(SWEEPS):
        fine_field = fine_sweep(fine_field, adjoint_seed, fine_block, fine_smoother, elem_scale, face_coef)
    rest_mid = transpose_apply(prolong_mid, adjoint_seed - adjoint_op(fine_field, fine_block, elem_scale, face_coef, NF))
    middle = jnp.zeros_like(rest_mid)
    for sweep_index in range(SWEEPS):
        middle = point_sweep(middle, rest_mid, mid_block, elem_scale, face_coef, NM)
    rest_low = transpose_apply(prolong_low, rest_mid - adjoint_op(middle, mid_block, elem_scale, face_coef, NM))
    coarse = jnp.zeros_like(rest_low)
    for sweep_index in range(COARSE_SWEEPS):
        coarse = point_sweep(coarse, rest_low, coarse_block, elem_scale, face_coef, NC)
    middle = middle + forward_apply(prolong_low, coarse)
    for sweep_index in range(SWEEPS):
        middle = point_sweep(middle, rest_mid, mid_block, elem_scale, face_coef, NM)
    fine_field = fine_field + forward_apply(prolong_mid, middle)
    for sweep_index in range(SWEEPS):
        fine_field = fine_sweep(fine_field, adjoint_seed, fine_block, fine_smoother, elem_scale, face_coef)
    adjoint_prev = fine_field + increments * transpose_apply(noise_map, fine_field)
    return fine_field, adjoint_prev
```

```python
import numpy as np
import jax
import jax.numpy as jnp
from jax import lax
from jax.sharding import PartitionSpec as P
from jax.experimental import pallas as pl
from jax.experimental.pallas import tpu as pltpu

NF = 6
QF = 216
SF = 240
QM = 64
QC = 8
COLS = 16
LANES = COLS * 128
F32 = jnp.float32
BF16 = jnp.bfloat16


def fine_slots():
    slots = []
    for i in range(6):
        slots += [(i, 0, k) for k in range(6)] + [None] * 2
        slots += [(i, 5, k) for k in range(6)] + [None] * 2
        slots += [(i, j, 0) for j in range(1, 5)] + [(i, j, 5) for j in range(1, 5)]
        slots += [(i, j, k) for j in range(1, 5) for k in range(1, 5)]
    return slots


def slot_matrix():
    to_slot = np.zeros((SF, QF), np.float32)
    for slot, node in enumerate(fine_slots()):
        if node is not None:
            to_slot[slot, (node[0] * 6 + node[1]) * 6 + node[2]] = 1.0
    return to_slot


def call(kernel, outs, scratch=(), smem=()):
    def run(*operands):
        specs = [
            pl.BlockSpec(memory_space=pltpu.SMEM if n in smem else pltpu.VMEM)
            for n in range(len(operands))
        ]
        return pl.pallas_call(
            kernel,
            out_shape=tuple(jax.ShapeDtypeStruct(s, d) for s, d in outs),
            in_specs=specs,
            out_specs=tuple(pl.BlockSpec(memory_space=pltpu.VMEM) for _ in outs),
            scratch_shapes=list(scratch),
            compiler_params=pltpu.CompilerParams(vmem_limit_bytes=32 * 1024 * 1024),
        )(*operands)

    return run


def dot(a, b):
    return lax.dot_general(a, b, (((1,), (0,)), ((), ())), preferred_element_type=F32)


def dot_nt(a, b):
    return lax.dot_general(a, b, (((1,), (1,)), ((), ())), preferred_element_type=F32)


def halves(values):
    high = values.astype(BF16)
    return high, (values - high.astype(F32)).astype(BF16)


def lane_roll(values, shift):
    return jnp.concatenate(
        [
            pltpu.roll(values[:, c * 128 : (c + 1) * 128], shift % 128, 1)
            for c in range(values.shape[1] // 128)
        ],
        axis=1,
    )


def sub_roll(values, shift):
    return pltpu.roll(values, shift % values.shape[0], 0)


def sublane(shape):
    return lax.broadcasted_iota(jnp.int32, shape, 0)


def x_from_lower(edge, values):
    return jnp.concatenate([edge, values[:, :1536]], axis=1)


def x_from_upper(values, edge):
    return jnp.concatenate([values[:, 512:], edge], axis=1)


def y_from_lower(edge, values):
    parts = []
    for x in range(4):
        parts += [edge[:, x * 128 : x * 128 + 128], values[:, x * 512 : x * 512 + 384]]
    return jnp.concatenate(parts, axis=1)


def y_from_upper(values, edge):
    parts = []
    for x in range(4):
        parts += [values[:, x * 512 + 128 : x * 512 + 512], edge[:, x * 128 : x * 128 + 128]]
    return jnp.concatenate(parts, axis=1)


def y_column(values, y):
    return jnp.concatenate(
        [values[:, x * 512 + y * 128 : x * 512 + y * 128 + 128] for x in range(4)], axis=1
    )


def even(idx_ref, axis):
    return idx_ref[axis] % 2 == 0


def prep_kernel(to_slot, fine, smooth, noise, mid, pmid, plow, kf, sf, nf, pmt, pm, km, plt):
    slot = to_slot[...]

    def eye(n, width=None):
        shape = (n, width or n)
        row = lax.broadcasted_iota(jnp.int32, shape, 0)
        col = lax.broadcasted_iota(jnp.int32, shape, 1)
        return row, col

    def one_hot(n):
        row, col = eye(n)
        return jnp.where(row == col, 1.0, 0.0).astype(BF16)

    def wide(out, rows, high, low):
        gap = jnp.zeros((rows, 16), BF16)
        out[:, 0:256] = jnp.concatenate([high, gap], axis=1)
        out[:, 256:512] = jnp.concatenate([high, gap], axis=1)
        out[:, 512:768] = jnp.concatenate([low, gap], axis=1)

    def narrow(out, high, low):
        row, col = eye(64, 128)
        twice = jnp.where((row == col) | (row == col - 64), 1.0, 0.0).astype(BF16)
        once = jnp.where(row == col, 1.0, 0.0).astype(BF16)
        out[:, 0:128] = dot(high, twice).astype(BF16)
        out[:, 128:256] = dot(low, once).astype(BF16)

    for source, out in ((fine, kf), (smooth, sf)):
        parts = [
            dot_nt(dot_nt(slot, part).astype(BF16), slot).astype(BF16)
            for part in halves(source[...])
        ]
        wide(out, SF, *parts)
    turn = one_hot(QF)
    wide(
        nf,
        QF,
        *[
            dot_nt(dot_nt(turn, part).astype(BF16), slot).astype(BF16)
            for part in halves(noise[...])
        ],
    )
    turn = one_hot(QM)
    high, low = halves(pmid[...])
    wide(
        pmt,
        QM,
        *[dot_nt(dot_nt(turn, part).astype(BF16), slot).astype(BF16) for part in (high, low)],
    )
    narrow(pm, *[dot(slot, part).astype(BF16) for part in (high, low)])
    narrow(km, *[dot_nt(turn, part).astype(BF16) for part in halves(mid[...])])
    row, col = eye(16, 8)
    turn = jnp.where(row == col, 1.0, 0.0).astype(BF16)
    narrow(plt, *[dot_nt(turn, part).astype(BF16) for part in halves(plow[...])])


def split_fine(values, x_ref, lanes):
    high, low = halves(values)
    x_ref[0:SF, lanes] = high
    x_ref[256 : 256 + SF, lanes] = low


def clear_fine(x_ref):
    x_ref[SF:256, :] = jnp.zeros((256 - SF, LANES), BF16)
    x_ref[256 + SF : 512, :] = jnp.zeros((256 - SF, LANES), BF16)


def fine_product(w_ref, x_ref, lanes):
    return dot(w_ref[:, 0:512], x_ref[:, lanes]) + dot(w_ref[:, 512:768], x_ref[0:256, lanes])


def mid_product(w_ref, values, x_ref):
    high, low = halves(values)
    x_ref[0:64, :] = high
    x_ref[64:128, :] = low
    x_ref[128:192, :] = high
    x_ref[192:256, :] = jnp.zeros((64, LANES), BF16)
    return dot(w_ref[...], x_ref[...])


def chunk(n):
    return slice(n * 512, n * 512 + 512)


def fine_sends(u_ref, idx, s1, s2, s3, s4):
    x_even, y_even = even(idx, 0), even(idx, 1)
    upper, lower = u_ref[200:240, 1536:2048], u_ref[0:40, 0:512]
    s1[...] = jnp.where(x_even, upper, lower)
    s2[...] = jnp.where(x_even, lower, upper)
    for i in range(6):
        upper = y_column(u_ref[40 * i + 8 : 40 * i + 16, :], 3)
        lower = y_column(u_ref[40 * i : 40 * i + 8, :], 0)
        s3[8 * i : 8 * i + 8, :] = jnp.where(y_even, upper, lower)
        s4[8 * i : 8 * i + 8, :] = jnp.where(y_even, lower, upper)


def fine_defect(u_ref, g_ref, csr, idx, r1, r2, r3, r4, kf, x_ref, t_ref):
    for n in range(4):
        u = u_ref[:, chunk(n)]
        split_fine(u, x_ref, chunk(n))
        t_ref[:, chunk(n)] = g_ref[:, chunk(n)] - 4.0 * u - fine_product(kf, x_ref, chunk(n))
    x_even, y_even = even(idx, 0), even(idx, 1)
    below = jnp.where(x_even, r2[...], r1[...])
    above = jnp.where(x_even, r1[...], r2[...])
    t_ref[0:40, :] += csr[0:1, :] * x_from_lower(below, u_ref[200:240, :])
    t_ref[200:240, :] += csr[1:2, :] * x_from_upper(u_ref[0:40, :], above)
    row = sublane((8, LANES))
    for i in range(6):
        base = 40 * i
        first, last, sides = (u_ref[base + 8 * n : base + 8 * n + 8, :] for n in range(3))
        edge = slice(8 * i, 8 * i + 8)
        below = jnp.where(y_even, r4[edge, :], r3[edge, :])
        above = jnp.where(y_even, r3[edge, :], r4[edge, :])
        t0 = csr[2:3, :] * y_from_lower(below, last)
        t1 = csr[3:4, :] * y_from_upper(first, above)
        for n, tile, extra in ((0, first, t0), (1, last, t1)):
            lower = csr[4:5, :] * sub_roll(lane_roll(tile, 1), 3)
            upper = csr[5:6, :] * sub_roll(lane_roll(tile, -1), 5)
            t_ref[base + 8 * n : base + 8 * n + 8, :] += (
                extra + jnp.where(row == 0, lower, 0.0) + jnp.where(row == 5, upper, 0.0)
            )
        lower = csr[4:5, :] * sub_roll(lane_roll(sides, 1), 4)
        upper = csr[5:6, :] * sub_roll(lane_roll(sides, -1), 4)
        t_ref[base + 16 : base + 24, :] += jnp.where(row < 4, lower, upper)


def fine_update(u_ref, out_ref, sf, x_ref, t_ref):
    for n in range(4):
        t = t_ref[:, chunk(n)]
        split_fine(t, x_ref, chunk(n))
        out_ref[:, chunk(n)] = u_ref[:, chunk(n)] + 0.25 * t + fine_product(sf, x_ref, chunk(n))


def first_kernel(seed, scale, coef, to_slot, sf, idx, g, u1, cs, csr, s1, s2, s3, s4, x_ref):
    over = 1.0 / scale[...]
    cs[...] = jnp.concatenate([coef[16 * d : 16 * d + 16, :] * over for d in range(3)], axis=0)
    csr[...] = jnp.zeros((8, LANES), F32)
    lane = lax.broadcasted_iota(jnp.int32, (1, 128), 1)
    for c in range(COLS):
        x, y = c // 4, c % 4
        lanes = slice(c * 128, c * 128 + 128)
        for d in range(3):
            value = cs[16 * d + c : 16 * d + c + 1, :]
            low, high = 0.9 * value, 0.3 * value
            if d == 0 and x == 0:
                low = jnp.where(idx[0] == 0, 0.0, low)
            if d == 0 and x == 3:
                high = jnp.where(idx[0] == idx[2] - 1, 0.0, high)
            if d == 1 and y == 0:
                low = jnp.where(idx[1] == 0, 0.0, low)
            if d == 1 and y == 3:
                high = jnp.where(idx[1] == idx[3] - 1, 0.0, high)
            if d == 2:
                low = jnp.where(lane == 0, 0.0, low)
                high = jnp.where(lane == 127, 0.0, high)
            csr[2 * d : 2 * d + 1, lanes] = low
            csr[2 * d + 1 : 2 * d + 2, lanes] = high
    clear_fine(x_ref)
    x_ref[QF:SF, :] = jnp.zeros((SF - QF, LANES), BF16)
    x_ref[256 + QF : 256 + SF, :] = jnp.zeros((SF - QF, LANES), BF16)
    slot = to_slot[...]
    for c in range(COLS):
        lanes = slice(c * 128, c * 128 + 128)
        values = seed[pl.ds(c, QF, stride=COLS), :] * over[c : c + 1, :]
        high, low = halves(values)
        rest = (values - high.astype(F32) - low.astype(F32)).astype(BF16)
        g[:, lanes] = dot(slot, high) + dot(slot, low) + dot(slot, rest)
    for n in range(4):
        values = g[:, chunk(n)]
        split_fine(values, x_ref, chunk(n))
        u1[:, chunk(n)] = 0.25 * values + fine_product(sf, x_ref, chunk(n))
    fine_sends(u1, idx, s1, s2, s3, s4)


def sweep_kernel(u, g, csr, idx, r1, r2, r3, r4, kf, sf, out, s1, s2, s3, s4, x_ref, t_ref):
    clear_fine(x_ref)
    fine_defect(u, g, csr, idx, r1, r2, r3, r4, kf, x_ref, t_ref)
    fine_update(u, out, sf, x_ref, t_ref)
    fine_sends(out, idx, s1, s2, s3, s4)


def restrict_kernel(u, g, csr, idx, r1, r2, r3, r4, kf, pmt, gm, m1, s1, s2, s3, s4, x_ref, t_ref):
    clear_fine(x_ref)
    fine_defect(u, g, csr, idx, r1, r2, r3, r4, kf, x_ref, t_ref)
    for n in range(4):
        split_fine(t_ref[:, chunk(n)], x_ref, chunk(n))
        value = fine_product(pmt, x_ref, chunk(n))
        gm[:, chunk(n)] = value
        m1[:, chunk(n)] = 0.2 * value
    mid_sends(m1, idx, s1, s2, s3, s4)


def last_kernel(u, g, csr, idx, r1, r2, r3, r4, kf, sf, nf, from_slot, inc, out, prev, x_ref, t_ref, w_ref):
    clear_fine(x_ref)
    fine_defect(u, g, csr, idx, r1, r2, r3, r4, kf, x_ref, t_ref)
    fine_update(u, w_ref, sf, x_ref, t_ref)
    slot = from_slot[...]
    for n in range(4):
        values = w_ref[:, chunk(n)]
        split_fine(values, x_ref, chunk(n))
        high, low = halves(values)
        rest = (values - high.astype(F32) - low.astype(F32)).astype(BF16)
        natural = dot(slot, high) + dot(slot, low) + dot(slot, rest)
        noise = fine_product(nf, x_ref, chunk(n))
        for y in range(4):
            c = 4 * n + y
            lanes = slice(y * 128, y * 128 + 128)
            out[pl.ds(c, QF, stride=COLS), :] = natural[:, lanes]
            prev[pl.ds(c, QF, stride=COLS), :] = (
                natural[:, lanes] + inc[c : c + 1, :] * noise[:, lanes]
            )


def mid_sends(m_ref, idx, s1, s2, s3, s4):
    x_even, y_even = even(idx, 0), even(idx, 1)
    upper, lower = m_ref[48:64, 1536:2048], m_ref[0:16, 0:512]
    s1[...] = jnp.where(x_even, upper, lower)
    s2[...] = jnp.where(x_even, lower, upper)
    for i in range(4):
        upper = y_column(m_ref[16 * i + 8 : 16 * i + 16, :], 3)
        lower = y_column(m_ref[16 * i : 16 * i + 8, :], 0)
        s3[8 * i : 8 * i + 8, :] = jnp.where(y_even, upper, lower)
        s4[8 * i : 8 * i + 8, :] = jnp.where(y_even, lower, upper)


def mid_edges(idx, r1, r2, r3, r4):
    x_even, y_even = even(idx, 0), even(idx, 1)
    return (
        jnp.where(x_even, r2[...], r1[...]),
        jnp.where(x_even, r1[...], r2[...]),
        jnp.where(y_even, r4[...], r3[...]),
        jnp.where(y_even, r3[...], r4[...]),
    )


def mid_defect(m_ref, g_ref, csr, edges, km, x_ref, t_ref):
    below_x, above_x, below_y, above_y = edges
    m = m_ref[...]
    t_ref[...] = g_ref[...] - 4.0 * m - mid_product(km, m, x_ref)
    t_ref[0:16, :] += csr[0:1, :] * x_from_lower(below_x, m_ref[48:64, :])
    t_ref[48:64, :] += csr[1:2, :] * x_from_upper(m_ref[0:16, :], above_x)
    row = sublane((8, LANES))
    for i in range(4):
        base = 16 * i
        first, last = m_ref[base : base + 8, :], m_ref[base + 8 : base + 16, :]
        edge = slice(8 * i, 8 * i + 8)
        extra0 = csr[2:3, :] * sub_roll(y_from_lower(below_y[edge, :], last), 4)
        extra1 = csr[3:4, :] * sub_roll(y_from_upper(first, above_y[edge, :]), 4)
        for n, tile, extra in (
            (0, first, jnp.where(row < 4, extra0, 0.0)),
            (1, last, jnp.where(row >= 4, extra1, 0.0)),
        ):
            lower = csr[4:5, :] * sub_roll(lane_roll(tile, 1), 5)
            upper = csr[5:6, :] * sub_roll(lane_roll(tile, -1), 3)
            t_ref[base + 8 * n : base + 8 * n + 8, :] += (
                extra + jnp.where(row % 4 == 0, lower, 0.0) + jnp.where(row % 4 == 3, upper, 0.0)
            )


def mid_kernel(m, g, csr, idx, r1, r2, r3, r4, km, out, s1, s2, s3, s4, x_ref, t_ref):
    mid_defect(m, g, csr, mid_edges(idx, r1, r2, r3, r4), km, x_ref, t_ref)
    out[...] = m[...] + 0.2 * t_ref[...]
    mid_sends(out, idx, s1, s2, s3, s4)


def low_kernel(m, g, csr, cs, idx, r1, r2, r3, r4, km, plt, pay, x_ref, t_ref):
    mid_defect(m, g, csr, mid_edges(idx, r1, r2, r3, r4), km, x_ref, t_ref)
    value = mid_product(plt, t_ref[...], x_ref)
    for c in range(COLS):
        pay[pl.ds(c, QC, stride=COLS), :] = value[0:8, c * 128 : c * 128 + 128]
    pay[QC * COLS : (QC + 3) * COLS, :] = cs[...]


def lift_kernel(m, csr, idx, r1, r2, r3, r4, km, pm, g, u, out, s1, s2, s3, s4, x_ref, t_ref):
    mid_defect(m, g, csr, mid_edges(idx, r1, r2, r3, r4), km, x_ref, t_ref)
    t_ref[...] = m[...] + 0.2 * t_ref[...]
    high, low = halves(t_ref[...])
    x_ref[0:64, :] = high
    x_ref[64:128, :] = low
    x_ref[128:192, :] = high
    for n in range(4):
        out[:, chunk(n)] = u[:, chunk(n)] + dot(pm[...], x_ref[:, chunk(n)])
    fine_sends(out, idx, s1, s2, s3, s4)


WX = 12
WROWS = WX * 16


def place(window, fields, blocks, idx):
    own, r1, r2, y3, y4 = blocks
    x_even, y_even = even(idx, 0), even(idx, 1)
    count = own.shape[0]
    zero = jnp.zeros((4, 128), F32)
    for d in range(fields):
        for x in range(4):
            rows = pl.ds(d * COLS + x * 4, 4)
            first = (own[rows, :], r1[rows, :], r2[rows, :])
            side = []
            for ref in (y3, y4):
                side.append(
                    tuple(ref[pl.ds(n * count + d * COLS + x * 4, 4), :] for n in range(3))
                )
            below = tuple(jnp.where(y_even, b, a) for a, b in zip(*side))
            above = tuple(jnp.where(y_even, a, b) for a, b in zip(*side))
            for offset, (mine, one, two) in ((0, below), (4, first), (8, above)):
                left = jnp.where(x_even, two, one)
                right = jnp.where(x_even, one, two)
                for plane, value in ((x, left), (4 + x, mine), (8 + x, right)):
                    window[d, pl.ds(plane * 16 + offset, 4), :] = value
            for plane in (x, 4 + x, 8 + x):
                window[d, pl.ds(plane * 16 + 12, 4), :] = zero


def coarse_sweep(c_ref, out_ref, g_ref, coef, kc, first, last):
    def step(plane, carry):
        here = pl.ds(pl.multiple_of(plane * 16, 16), 16)
        before = pl.ds(pl.multiple_of(plane * 16 - 16, 16), 16)
        after = pl.ds(pl.multiple_of(plane * 16 + 16, 16), 16)
        c = [c_ref[d, here, :] for d in range(QC)]
        weights = [coef[n, here, :] for n in range(6)]
        for d in range(QC):
            t = g_ref[d, here, :] - 4.0 * c[d]
            for j in range(QC):
                t = t - kc[j, d] * c[j]
            if d & 4:
                t = t + weights[1] * c_ref[d - 4, after, :]
            else:
                t = t + weights[0] * c_ref[d + 4, before, :]
            if d & 2:
                t = t + weights[3] * sub_roll(c[d - 2], -1)
            else:
                t = t + weights[2] * sub_roll(c[d + 2], 1)
            if d & 1:
                t = t + weights[5] * pltpu.roll(c[d - 1], 127, 1)
            else:
                t = t + weights[4] * pltpu.roll(c[d + 1], 1, 1)
            out_ref[d, here, :] = c[d] + 0.2 * t
        return carry

    lax.fori_loop(first, last, step, 0)


def coarse_kernel(own, r1, r2, y3, y4, kc, idx, g, coef, pay, window, one, two):
    place(window, QC + 3, (own, r1, r2, y3, y4), idx)
    g[...] = window[0:QC]
    lane = lax.broadcasted_iota(jnp.int32, (WROWS, 128), 1)
    row = lax.broadcasted_iota(jnp.int32, (WROWS, 128), 0)
    plane, y = row // 16, row % 16 - 4
    csx, csy, csz = (window[QC + d] for d in range(3))
    coef[0] = jnp.where((plane == 4) & (idx[0] == 0), 0.0, 0.9 * csx)
    coef[1] = jnp.where((plane == 7) & (idx[0] == idx[2] - 1), 0.0, 0.3 * csx)
    coef[2] = jnp.where((y == 0) & (idx[1] == 0), 0.0, 0.9 * csy)
    coef[3] = jnp.where((y == 3) & (idx[1] == idx[3] - 1), 0.0, 0.3 * csy)
    coef[4] = jnp.where(lane == 0, 0.0, 0.9 * csz)
    coef[5] = jnp.where(lane == 127, 0.0, 0.3 * csz)
    one[...] = 0.2 * g[...]
    coarse_sweep(one, two, g, coef, kc, 1, 11)
    coarse_sweep(two, one, g, coef, kc, 2, 10)
    coarse_sweep(one, two, g, coef, kc, 3, 9)
    coarse_sweep(two, one, g, coef, kc, 4, 8)
    for d in range(QC):
        for x in range(4):
            pay[pl.ds(d * COLS + x * 4, 4), :] = one[d, pl.ds((4 + x) * 16 + 4, 4), :]


def correct_kernel(
    own, r1, r2, y3, y4, kc, idx, g, coef, plow, m, gm, csr, q1, q2, q3, q4, km,
    out, s1, s2, s3, s4, window, one, x_ref, t_ref, m_ref, spread,
):
    place(window, QC, (own, r1, r2, y3, y4), idx)
    coarse_sweep(window, one, g, coef, kc, 3, 9)
    for d in range(QC):
        spread[d] = jnp.broadcast_to(plow[:, d : d + 1], (QM, 128))

    def lifted(x, y, rows):
        total = None
        for d in range(QC):
            part = spread[d, rows, :] * one[d, pl.ds((4 + x) * 16 + 4 + y, 1), :]
            total = part if total is None else total + part
        return total

    whole = slice(0, QM)
    for c in range(COLS):
        lanes = slice(c * 128, c * 128 + 128)
        m_ref[:, lanes] = m[:, lanes] + lifted(c // 4, c % 4, whole)
    below_x, above_x, below_y, above_y = mid_edges(idx, q1, q2, q3, q4)
    below_x = below_x + jnp.concatenate([lifted(-1, y, slice(48, 64)) for y in range(4)], axis=1)
    above_x = above_x + jnp.concatenate([lifted(4, y, slice(0, 16)) for y in range(4)], axis=1)
    below_rows, above_rows = [], []
    for i in range(4):
        last, first = slice(16 * i + 8, 16 * i + 16), slice(16 * i, 16 * i + 8)
        below_rows.append(jnp.concatenate([lifted(x, -1, last) for x in range(4)], axis=1))
        above_rows.append(jnp.concatenate([lifted(x, 4, first) for x in range(4)], axis=1))
    below_y = below_y + jnp.concatenate(below_rows, axis=0)
    above_y = above_y + jnp.concatenate(above_rows, axis=0)
    mid_defect(m_ref, gm, csr, (below_x, above_x, below_y, above_y), km, x_ref, t_ref)
    out[...] = m_ref[...] + 0.2 * t_ref[...]
    mid_sends(out, idx, s1, s2, s3, s4)


def swap(values, axis, odd):
    count = lax.axis_size(axis)
    pairs = [(i, (((i + odd) ^ 1) - odd) % count) for i in range(count)]
    return lax.ppermute(values, axis, pairs)


def exchange(sends):
    s1, s2, s3, s4 = sends
    return swap(s1, "gx", 0), swap(s2, "gx", 1), swap(s3, "yz", 0), swap(s4, "yz", 1)


def exchange_blocks(own):
    r1, r2 = swap(own, "gx", 0), swap(own, "gx", 1)
    three = jnp.concatenate([own, r1, r2], axis=0)
    return own, r1, r2, swap(three, "yz", 0), swap(three, "yz", 1)


def body(seed, scale, coef, fine, smooth, mid, coarse, pmid, plow, noise, inc):
    idx = jnp.stack(
        [
            lax.axis_index("gx"),
            lax.axis_index("yz"),
            jnp.int32(lax.axis_size("gx")),
            jnp.int32(lax.axis_size("yz")),
        ]
    ).astype(jnp.int32)
    rows = seed.reshape(QF * COLS, 128)
    scale = scale.reshape(COLS, 128)
    coef = coef.reshape(3 * COLS, 128)
    inc = inc.reshape(COLS, 128)
    slots = slot_matrix()
    to_slot, from_slot = jnp.asarray(slots, BF16), jnp.asarray(slots.T, BF16)

    kf, sf, nf, pmt, pm, km, plt = call(
        prep_kernel,
        [
            ((SF, 768), BF16),
            ((SF, 768), BF16),
            ((QF, 768), BF16),
            ((QM, 768), BF16),
            ((SF, 256), BF16),
            ((QM, 256), BF16),
            ((16, 256), BF16),
        ],
    )(to_slot, fine, smooth, noise, mid, pmid, plow)

    fine_field = ((SF, LANES), F32)
    fine_faces = [((40, 512), F32)] * 2 + [((48, 512), F32)] * 2
    mid_field = ((QM, LANES), F32)
    mid_faces = [((16, 512), F32)] * 2 + [((32, 512), F32)] * 2
    xf, tf = pltpu.VMEM((512, LANES), BF16), pltpu.VMEM((SF, LANES), F32)
    xm, tm = pltpu.VMEM((256, LANES), BF16), pltpu.VMEM((QM, LANES), F32)

    g, u, cs, csr, *sends = call(
        first_kernel,
        [fine_field, fine_field, ((3 * COLS, 128), F32), ((8, LANES), F32)] + fine_faces,
        [xf],
        (5,),
    )(rows, scale, coef, to_slot, sf, idx)

    sweep = call(sweep_kernel, [fine_field] + fine_faces, [xf, tf], (3,))
    u, *sends = sweep(u, g, csr, idx, *exchange(sends), kf, sf)
    gm, m, *sends = call(restrict_kernel, [mid_field, mid_field] + mid_faces, [xf, tf], (3,))(
        u, g, csr, idx, *exchange(sends), kf, pmt
    )
    m, *sends = call(mid_kernel, [mid_field] + mid_faces, [xm, tm], (3,))(
        m, gm, csr, idx, *exchange(sends), km
    )
    edges = exchange(sends)
    (pay,) = call(low_kernel, [(((QC + 3) * COLS, 128), F32)], [xm, tm], (4,))(
        m, gm, csr, cs, idx, *edges, km, plt
    )
    window = ((QC, WROWS, 128), F32)
    gw, coefw, pay = call(
        coarse_kernel,
        [window, ((6, WROWS, 128), F32), ((QC * COLS, 128), F32)],
        [
            pltpu.VMEM((QC + 3, WROWS, 128), F32),
            pltpu.VMEM((QC, WROWS, 128), F32),
            pltpu.VMEM((QC, WROWS, 128), F32),
        ],
        (5, 6),
    )(*exchange_blocks(pay), coarse, idx)
    m, *sends = call(
        correct_kernel,
        [mid_field] + mid_faces,
        [
            pltpu.VMEM((QC, WROWS, 128), F32),
            pltpu.VMEM((QC, WROWS, 128), F32),
            xm,
            tm,
            pltpu.VMEM((QM, LANES), F32),
            pltpu.VMEM((QC, QM, 128), F32),
        ],
        (5, 6),
    )(*exchange_blocks(pay), coarse, idx, gw, coefw, plow, m, gm, csr, *edges, km)
    u, *sends = call(lift_kernel, [fine_field] + fine_faces, [xm, tm], (2,))(
        m, csr, idx, *exchange(sends), km, pm, gm, u
    )
    u, *sends = sweep(u, g, csr, idx, *exchange(sends), kf, sf)
    out, prev = call(
        last_kernel,
        [((QF * COLS, 128), F32)] * 2,
        [xf, tf, pltpu.VMEM((SF, LANES), F32)],
        (3,),
    )(u, g, csr, idx, *exchange(sends), kf, sf, nf, from_slot, inc)
    shape = seed.shape
    return out.reshape(shape), prev.reshape(shape)


def solution(mesh):
    cell, field = P("gx", "yz", None), P(None, "gx", "yz", None)
    return jax.shard_map(
        body,
        mesh=mesh,
        in_specs=(field, cell, field) + (P(),) * 7 + (cell,),
        out_specs=(field, field),
        check_vma=False,
    )
```

```python
import numpy as np
import jax
import jax.numpy as jnp
from jax import lax
from jax.sharding import PartitionSpec as P
from jax.experimental import pallas as pl
from jax.experimental.pallas import tpu as pltpu

NF = 6
QF = 216
SF = 240
QM = 64
QC = 8
COLS = 16
LANES = COLS * 128
F32 = jnp.float32
BF16 = jnp.bfloat16


def fine_slots():
    slots = []
    for i in range(6):
        slots += [(i, 0, k) for k in range(6)] + [None] * 2
        slots += [(i, 5, k) for k in range(6)] + [None] * 2
        slots += [(i, j, 0) for j in range(1, 5)] + [(i, j, 5) for j in range(1, 5)]
        slots += [(i, j, k) for j in range(1, 5) for k in range(1, 5)]
    return slots


def slot_matrix():
    to_slot = np.zeros((SF, QF), np.float32)
    for slot, node in enumerate(fine_slots()):
        if node is not None:
            to_slot[slot, (node[0] * 6 + node[1]) * 6 + node[2]] = 1.0
    return to_slot


def call(kernel, outs, scratch=(), smem=(), hbm=(), cost=None):
    def run(*operands):
        specs = [
            pl.BlockSpec(
                memory_space=pltpu.SMEM if n in smem else pltpu.HBM if n in hbm else pltpu.VMEM
            )
            for n in range(len(operands))
        ]
        operands = [
            pltpu.with_memory_space_constraint(value, pltpu.HBM) if n in hbm else value
            for n, value in enumerate(operands)
        ]
        return pl.pallas_call(
            kernel,
            out_shape=tuple(jax.ShapeDtypeStruct(s, d) for s, d in outs),
            in_specs=specs,
            out_specs=tuple(pl.BlockSpec(memory_space=pltpu.VMEM) for _ in outs),
            scratch_shapes=list(scratch),
            compiler_params=pltpu.CompilerParams(vmem_limit_bytes=20 * 1024 * 1024),
            cost_estimate=cost,
        )(*operands)

    return run


def dot(a, b):
    return lax.dot_general(a, b, (((1,), (0,)), ((), ())), preferred_element_type=F32)


def dot_nt(a, b):
    return lax.dot_general(a, b, (((1,), (1,)), ((), ())), preferred_element_type=F32)


def halves(values):
    high = values.astype(BF16)
    return high, (values - high.astype(F32)).astype(BF16)


def lane_roll(values, shift):
    return jnp.concatenate(
        [
            pltpu.roll(values[:, c * 128 : (c + 1) * 128], shift % 128, 1)
            for c in range(values.shape[1] // 128)
        ],
        axis=1,
    )


def sub_roll(values, shift):
    return pltpu.roll(values, shift % values.shape[0], 0)


def sublane(shape):
    return lax.broadcasted_iota(jnp.int32, shape, 0)


def y_from_lower(values):
    parts, edge = [], jnp.zeros((values.shape[0], 128), F32)
    for x in range(4):
        parts += [edge, values[:, x * 512 : x * 512 + 384]]
    return jnp.concatenate(parts, axis=1)


def y_from_upper(values):
    parts, edge = [], jnp.zeros((values.shape[0], 128), F32)
    for x in range(4):
        parts += [values[:, x * 512 + 128 : x * 512 + 512], edge]
    return jnp.concatenate(parts, axis=1)


def y_column(values, y):
    return jnp.concatenate(
        [values[:, x * 512 + y * 128 : x * 512 + y * 128 + 128] for x in range(4)], axis=1
    )


def even(idx_ref, axis):
    return idx_ref[axis] % 2 == 0


def prepare(slot, fine, smooth, noise, mid, pmid_t, plow_t, kf, sf, nf, pmt, pm, km, plt, spread):
    def grid(rows, columns):
        return tuple(lax.broadcasted_iota(jnp.int32, (rows, columns), n) for n in range(2))

    def one_hot(n):
        row, col = grid(n, n)
        return jnp.where(row == col, 1.0, 0.0).astype(BF16)

    def wide(out, rows, high, low):
        gap = jnp.zeros((rows, 16), BF16)
        out[:, 0:256] = jnp.concatenate([high, gap], axis=1)
        out[:, 256:512] = jnp.concatenate([high, gap], axis=1)
        out[:, 512:768] = jnp.concatenate([low, gap], axis=1)

    def narrow(out, high, low):
        row, col = grid(64, 128)
        twice = jnp.where((row == col) | (row == col - 64), 1.0, 0.0).astype(BF16)
        once = jnp.where(row == col, 1.0, 0.0).astype(BF16)
        out[:, 0:128] = dot(high, twice).astype(BF16)
        out[:, 128:256] = dot(low, once).astype(BF16)

    def moved(left, part, right):
        return dot_nt(dot_nt(left, part).astype(BF16), right).astype(BF16)

    wide(sf, SF, *[moved(slot, part, slot) for part in halves(smooth)])
    wide(kf, SF, *[moved(slot, part, slot) for part in halves(fine)])
    turn = one_hot(QF)
    wide(nf, QF, *[moved(turn, part, slot) for part in halves(noise)])
    high, low = halves(pmid_t)
    wide(pmt, QM, *[dot_nt(part, slot).astype(BF16) for part in (high, low)])
    narrow(pm, *[dot_nt(slot, part).astype(BF16) for part in (high, low)])
    turn = one_hot(QM)
    narrow(km, *[dot_nt(turn, part).astype(BF16) for part in halves(mid)])
    high, low = halves(plow_t)
    rest = (plow_t - high.astype(F32) - low.astype(F32)).astype(BF16)
    gap = jnp.zeros((8, QM), BF16)
    narrow(plt, *[jnp.concatenate([part, gap], axis=0) for part in (high, low)])
    columns = dot_nt(turn, high) + dot_nt(turn, low) + dot_nt(turn, rest)
    for d in range(QC):
        spread[d] = jnp.broadcast_to(columns[:, d : d + 1], (QM, 128))


def split_fine(values, x_ref, lanes):
    high, low = halves(values)
    x_ref[0:SF, lanes] = high
    x_ref[256 : 256 + SF, lanes] = low


def clear_fine(x_ref):
    x_ref[SF:256, :] = jnp.zeros((256 - SF, LANES), BF16)
    x_ref[256 + SF : 512, :] = jnp.zeros((256 - SF, LANES), BF16)


def fine_product(w_ref, x_ref, lanes):
    return dot(w_ref[:, 0:512], x_ref[:, lanes]) + dot(w_ref[:, 512:768], x_ref[0:256, lanes])


def mid_product(w_ref, values, x_ref):
    high, low = halves(values)
    x_ref[0:64, :] = high
    x_ref[64:128, :] = low
    x_ref[128:192, :] = high
    x_ref[192:256, :] = jnp.zeros((64, LANES), BF16)
    return dot(w_ref[...], x_ref[...])


def chunk(n):
    return slice(n * 512, n * 512 + 512)


def fine_sends(u_ref, idx, s1, s2, s3, s4):
    x_even, y_even = even(idx, 0), even(idx, 1)
    upper, lower = u_ref[200:240, 1536:2048], u_ref[0:40, 0:512]
    s1[0:40, :] = jnp.where(x_even, upper, lower)
    s2[0:40, :] = jnp.where(x_even, lower, upper)
    for i in range(6):
        upper = y_column(u_ref[40 * i + 8 : 40 * i + 16, :], 3)
        lower = y_column(u_ref[40 * i : 40 * i + 8, :], 0)
        s3[8 * i : 8 * i + 8, :] = jnp.where(y_even, upper, lower)
        s4[8 * i : 8 * i + 8, :] = jnp.where(y_even, lower, upper)


def fine_local_kernel(u_ref, g_ref, csr, kf, t_ref, x_ref):
    clear_fine(x_ref)
    for n in range(4):
        u = u_ref[:, chunk(n)]
        split_fine(u, x_ref, chunk(n))
        t_ref[:, chunk(n)] = g_ref[:, chunk(n)] - 4.0 * u - fine_product(kf, x_ref, chunk(n))
    t_ref[0:40, 512:2048] += csr[0:1, 512:2048] * u_ref[200:240, 0:1536]
    t_ref[200:240, 0:1536] += csr[1:2, 0:1536] * u_ref[0:40, 512:2048]
    row = sublane((8, LANES))
    for i in range(6):
        base = 40 * i
        first, last, sides = (u_ref[base + 8 * n : base + 8 * n + 8, :] for n in range(3))
        t0 = csr[2:3, :] * y_from_lower(last)
        t1 = csr[3:4, :] * y_from_upper(first)
        for n, tile, extra in ((0, first, t0), (1, last, t1)):
            lower = csr[4:5, :] * sub_roll(lane_roll(tile, 1), 3)
            upper = csr[5:6, :] * sub_roll(lane_roll(tile, -1), 5)
            t_ref[base + 8 * n : base + 8 * n + 8, :] += (
                extra + jnp.where(row == 0, lower, 0.0) + jnp.where(row == 5, upper, 0.0)
            )
        lower = csr[4:5, :] * sub_roll(lane_roll(sides, 1), 4)
        upper = csr[5:6, :] * sub_roll(lane_roll(sides, -1), 4)
        t_ref[base + 16 : base + 24, :] += jnp.where(row < 4, lower, upper)


def fine_edges(n, t_in, csr, idx, r1, r2, r3, r4, t_ref):
    x_even, y_even = even(idx, 0), even(idx, 1)
    lanes = chunk(n)
    t_ref[:, lanes] = t_in[:, lanes]
    if n == 0:
        below = jnp.where(x_even, r2[0:40, :], r1[0:40, :])
        t_ref[0:40, lanes] += csr[0:1, lanes] * below
    if n == 3:
        above = jnp.where(x_even, r1[0:40, :], r2[0:40, :])
        t_ref[200:240, lanes] += csr[1:2, lanes] * above
    edge = slice(n * 128, n * 128 + 128)
    first, last = (slice(n * 512 + y * 128, n * 512 + y * 128 + 128) for y in (0, 3))
    for i in range(6):
        rows = slice(8 * i, 8 * i + 8)
        below = jnp.where(y_even, r4[rows, edge], r3[rows, edge])
        above = jnp.where(y_even, r3[rows, edge], r4[rows, edge])
        t_ref[40 * i : 40 * i + 8, first] += csr[2:3, first] * below
        t_ref[40 * i + 8 : 40 * i + 16, last] += csr[3:4, last] * above


def fine_update(u_ref, t_in, csr, idx, received, out_ref, sf, x_ref, t_ref):
    clear_fine(x_ref)
    for n in range(4):
        fine_edges(n, t_in, csr, idx, *received, t_ref)
        t = t_ref[:, chunk(n)]
        split_fine(t, x_ref, chunk(n))
        out_ref[:, chunk(n)] = u_ref[:, chunk(n)] + 0.25 * t + fine_product(sf, x_ref, chunk(n))


def first_kernel(
    seed_in, scale_in, coef_in, slot_in, smooth_in, fine_in, noise_in, mid_in, pmid_in, plow_in, idx,
    g, u1, csx, csr, s1, s2, s3, s4, kf, sf, nf, pmt, pm, km, plt, spread,
    x_ref, seed, scale, coef, slot, smooth, fine, noise, mid, pmid, plow, done,
):
    copies = {}
    for n, (name, source, target) in enumerate(
        (
            ("slot", slot_in, slot),
            ("smooth", smooth_in, smooth),
            ("fine", fine_in, fine),
            ("noise", noise_in, noise),
            ("pmid", pmid_in, pmid),
            ("plow", plow_in, plow),
            ("mid", mid_in, mid),
            ("scale", scale_in, scale),
            ("coef", coef_in, coef),
            ("seed", seed_in, seed),
        )
    ):
        copies[name] = pltpu.make_async_copy(source, target, done.at[n])
        copies[name].start()
    clear_fine(x_ref)
    x_ref[QF:SF, :] = jnp.zeros((SF - QF, LANES), BF16)
    x_ref[256 + QF : 256 + SF, :] = jnp.zeros((SF - QF, LANES), BF16)
    csr[...] = jnp.zeros((8, LANES), F32)
    csx[...] = jnp.zeros((16, 512), F32)
    for name in ("slot", "smooth", "fine", "noise", "pmid", "plow", "mid"):
        copies[name].wait()
    matrices = (ref[...] for ref in (slot, fine, smooth, noise, mid, pmid, plow))
    prepare(*matrices, kf, sf, nf, pmt, pm, km, plt, spread)
    copies["scale"].wait()
    copies["coef"].wait()
    over = 1.0 / scale[...]
    lane = lax.broadcasted_iota(jnp.int32, (1, 128), 1)
    for c in range(COLS):
        x, y = c // 4, c % 4
        lanes = slice(c * 128, c * 128 + 128)
        for d in range(3):
            value = coef[16 * d + c : 16 * d + c + 1, :] * over[c : c + 1, :]
            csx[4 * x + d : 4 * x + d + 1, y * 128 : y * 128 + 128] = value
            low, high = 0.9 * value, 0.3 * value
            if d == 0 and x == 0:
                low = jnp.where(idx[0] == 0, 0.0, low)
            if d == 0 and x == 3:
                high = jnp.where(idx[0] == idx[2] - 1, 0.0, high)
            if d == 1 and y == 0:
                low = jnp.where(idx[1] == 0, 0.0, low)
            if d == 1 and y == 3:
                high = jnp.where(idx[1] == idx[3] - 1, 0.0, high)
            if d == 2:
                low = jnp.where(lane == 0, 0.0, low)
                high = jnp.where(lane == 127, 0.0, high)
            csr[2 * d : 2 * d + 1, lanes] = low
            csr[2 * d + 1 : 2 * d + 2, lanes] = high
    copies["seed"].wait()
    for c in range(COLS):
        lanes = slice(c * 128, c * 128 + 128)
        values = seed[pl.ds(c, QF, stride=COLS), :] * over[c : c + 1, :]
        high, low = halves(values)
        rest = (values - high.astype(F32) - low.astype(F32)).astype(BF16)
        g[:, lanes] = dot(slot[...], high) + dot(slot[...], low) + dot(slot[...], rest)
    for n in range(4):
        values = g[:, chunk(n)]
        split_fine(values, x_ref, chunk(n))
        u1[:, chunk(n)] = 0.25 * values + fine_product(sf, x_ref, chunk(n))
    fine_sends(u1, idx, s1, s2, s3, s4)
    x_even = even(idx, 0)
    far, near = csx[4:16, :], csx[0:12, :]
    gap = jnp.zeros((4, 512), F32)
    s1[40:56, :] = jnp.concatenate([jnp.where(x_even, far, near), gap], axis=0)
    s2[40:56, :] = jnp.concatenate([jnp.where(x_even, near, far), gap], axis=0)


def spread_kernel(u, t_in, csr, idx, r1, r2, r3, r4, sf, csx, out, s1, s2, s3, s4, x_ref, t_ref):
    fine_update(u, t_in, csr, idx, (r1, r2, r3, r4), out, sf, x_ref, t_ref)
    fine_sends(out, idx, s1, s2, s3, s4)
    x_even, y_even = even(idx, 0), even(idx, 1)
    left = jnp.where(x_even, r2[40:56, :], r1[40:56, :])
    right = jnp.where(x_even, r1[40:56, :], r2[40:56, :])
    planes = jnp.concatenate([left[0:12], csx[...], right[0:12]], axis=0)
    gap = jnp.zeros((40, 128), F32)
    far, near = planes[:, 128:512], planes[:, 0:384]
    s3[48:88, :] = jnp.concatenate([jnp.where(y_even, far, near), gap], axis=1)
    s4[48:88, :] = jnp.concatenate([jnp.where(y_even, near, far), gap], axis=1)


def coefficient_kernel(idx, csx, r1, r2, r3, r4, coef):
    x_even, y_even = even(idx, 0), even(idx, 1)
    left = jnp.where(x_even, r2[40:56, :], r1[40:56, :])
    right = jnp.where(x_even, r1[40:56, :], r2[40:56, :])
    planes = jnp.concatenate([left[0:12], csx[...], right[0:12]], axis=0)
    below = jnp.where(y_even, r4[48:88, :], r3[48:88, :])
    above = jnp.where(y_even, r3[48:88, :], r4[48:88, :])
    first_x, last_x = idx[0] == 0, idx[0] == idx[2] - 1
    first_y, last_y = idx[1] == 0, idx[1] == idx[3] - 1
    lane = lax.broadcasted_iota(jnp.int32, (1, 128), 1)
    coef[...] = jnp.zeros((6, WROWS, 128), F32)
    for plane in range(WX):
        for y in range(-3, 7):
            source, at = (below, y + 3) if y < 0 else (planes, y) if y < 4 else (above, y - 4)
            row = slice(plane * 16 + 4 + y, plane * 16 + 5 + y)
            for d in range(3):
                value = source[4 * plane + d : 4 * plane + d + 1, at * 128 : at * 128 + 128]
                low, high = 0.9 * value, 0.3 * value
                if d == 0 and plane == 3:
                    low = jnp.where(first_x, 0.0, low)
                if d == 0 and plane == 6:
                    high = jnp.where(last_x, 0.0, high)
                if d == 1 and y == 0:
                    low = jnp.where(first_y, 0.0, low)
                if d == 1 and y == 3:
                    high = jnp.where(last_y, 0.0, high)
                if d == 2:
                    low = jnp.where(lane == 0, 0.0, low)
                    high = jnp.where(lane == 127, 0.0, high)
                coef[2 * d, row, :] = low
                coef[2 * d + 1, row, :] = high


def sweep_kernel(u, t_in, csr, idx, r1, r2, r3, r4, sf, out, s1, s2, s3, s4, x_ref, t_ref):
    fine_update(u, t_in, csr, idx, (r1, r2, r3, r4), out, sf, x_ref, t_ref)
    fine_sends(out, idx, s1, s2, s3, s4)


def restrict_kernel(t_in, csr, idx, r1, r2, r3, r4, pmt, gm, m1, s1, s2, s3, s4, x_ref, t_ref):
    clear_fine(x_ref)
    for n in range(4):
        fine_edges(n, t_in, csr, idx, r1, r2, r3, r4, t_ref)
        split_fine(t_ref[:, chunk(n)], x_ref, chunk(n))
        value = fine_product(pmt, x_ref, chunk(n))
        gm[:, chunk(n)] = value
        m1[:, chunk(n)] = 0.2 * value
    mid_sends(m1, idx, s1, s2, s3, s4)


def last_kernel(
    u, t_in, csr, idx, r1, r2, r3, r4, sf, nf, from_slot, inc, out, prev, x_ref, t_ref, w_ref
):
    fine_update(u, t_in, csr, idx, (r1, r2, r3, r4), w_ref, sf, x_ref, t_ref)
    slot = from_slot[...]
    for n in range(4):
        values = w_ref[:, chunk(n)]
        split_fine(values, x_ref, chunk(n))
        high, low = halves(values)
        rest = (values - high.astype(F32) - low.astype(F32)).astype(BF16)
        natural = dot(slot, high) + dot(slot, low) + dot(slot, rest)
        noise = fine_product(nf, x_ref, chunk(n))
        for y in range(4):
            c = 4 * n + y
            lanes = slice(y * 128, y * 128 + 128)
            out[pl.ds(c, QF, stride=COLS), :] = natural[:, lanes]
            prev[pl.ds(c, QF, stride=COLS), :] = (
                natural[:, lanes] + inc[c : c + 1, :] * noise[:, lanes]
            )


def mid_sends(m_ref, idx, s1, s2, s3, s4):
    x_even, y_even = even(idx, 0), even(idx, 1)
    upper, lower = m_ref[48:64, 1536:2048], m_ref[0:16, 0:512]
    s1[...] = jnp.where(x_even, upper, lower)
    s2[...] = jnp.where(x_even, lower, upper)
    for i in range(4):
        upper = y_column(m_ref[16 * i + 8 : 16 * i + 16, :], 3)
        lower = y_column(m_ref[16 * i : 16 * i + 8, :], 0)
        s3[8 * i : 8 * i + 8, :] = jnp.where(y_even, upper, lower)
        s4[8 * i : 8 * i + 8, :] = jnp.where(y_even, lower, upper)


def mid_edges(idx, r1, r2, r3, r4):
    x_even, y_even = even(idx, 0), even(idx, 1)
    return (
        jnp.where(x_even, r2[...], r1[...]),
        jnp.where(x_even, r1[...], r2[...]),
        jnp.where(y_even, r4[...], r3[...]),
        jnp.where(y_even, r3[...], r4[...]),
    )


def mid_local(m_ref, g_ref, csr, km, t_ref, x_ref):
    m = m_ref[...]
    t_ref[...] = g_ref[...] - 4.0 * m - mid_product(km, m, x_ref)
    t_ref[0:16, 512:2048] += csr[0:1, 512:2048] * m_ref[48:64, 0:1536]
    t_ref[48:64, 0:1536] += csr[1:2, 0:1536] * m_ref[0:16, 512:2048]
    row = sublane((8, LANES))
    for i in range(4):
        base = 16 * i
        first, last = m_ref[base : base + 8, :], m_ref[base + 8 : base + 16, :]
        extra0 = csr[2:3, :] * sub_roll(y_from_lower(last), 4)
        extra1 = csr[3:4, :] * sub_roll(y_from_upper(first), 4)
        for n, tile, extra in (
            (0, first, jnp.where(row < 4, extra0, 0.0)),
            (1, last, jnp.where(row >= 4, extra1, 0.0)),
        ):
            lower = csr[4:5, :] * sub_roll(lane_roll(tile, 1), 5)
            upper = csr[5:6, :] * sub_roll(lane_roll(tile, -1), 3)
            t_ref[base + 8 * n : base + 8 * n + 8, :] += (
                extra + jnp.where(row % 4 == 0, lower, 0.0) + jnp.where(row % 4 == 3, upper, 0.0)
            )


def mid_edge_terms(csr, edges, t_ref):
    below_x, above_x, below_y, above_y = edges
    t_ref[0:16, 0:512] += csr[0:1, 0:512] * below_x
    t_ref[48:64, 1536:2048] += csr[1:2, 1536:2048] * above_x
    row = sublane((8, 128))
    for i in range(4):
        rows = slice(8 * i, 8 * i + 8)
        for x in range(4):
            edge = slice(x * 128, x * 128 + 128)
            first, last = (slice(x * 512 + y * 128, x * 512 + y * 128 + 128) for y in (0, 3))
            below = csr[2:3, first] * sub_roll(below_y[rows, edge], 4)
            above = csr[3:4, last] * sub_roll(above_y[rows, edge], 4)
            t_ref[16 * i : 16 * i + 8, first] += jnp.where(row < 4, below, 0.0)
            t_ref[16 * i + 8 : 16 * i + 16, last] += jnp.where(row >= 4, above, 0.0)


def mid_local_kernel(m_ref, g_ref, csr, km, t_ref, x_ref):
    mid_local(m_ref, g_ref, csr, km, t_ref, x_ref)


def mid_kernel(m, t_in, csr, idx, r1, r2, r3, r4, out, s1, s2, s3, s4, t_ref):
    t_ref[...] = t_in[...]
    mid_edge_terms(csr, mid_edges(idx, r1, r2, r3, r4), t_ref)
    out[...] = m[...] + 0.2 * t_ref[...]
    mid_sends(out, idx, s1, s2, s3, s4)


def block_sends(pay, idx, s1, s2):
    x_even = even(idx, 0)
    far, near = pay[32:128, :], pay[0:96, :]
    s1[...] = jnp.where(x_even, far, near)
    s2[...] = jnp.where(x_even, near, far)


def row_kernel(idx, own, r1, r2, s3, s4):
    x_even, y_even = even(idx, 0), even(idx, 1)
    for plane in range(WX):
        tiles = []
        for y in range(4):
            if 3 <= plane < 7:
                at = QC * (4 * (plane - 3) + y)
                tiles.append(own[at : at + QC, :])
            else:
                at = QC * (4 * (plane % 7) + y)
                one, two = r1[at : at + QC, :], r2[at : at + QC, :]
                tiles.append(jnp.where(x_even == (plane < 3), two, one))
        for y in range(3):
            rows = slice(QC * (3 * plane + y), QC * (3 * plane + y) + QC)
            s3[rows, :] = jnp.where(y_even, tiles[y + 1], tiles[y])
            s4[rows, :] = jnp.where(y_even, tiles[y], tiles[y + 1])


def low_kernel(t_in, csr, idx, r1, r2, r3, r4, plt, pay, s1, s2, x_ref, t_ref):
    t_ref[...] = t_in[...]
    mid_edge_terms(csr, mid_edges(idx, r1, r2, r3, r4), t_ref)
    value = mid_product(plt, t_ref[...], x_ref)
    for c in range(COLS):
        pay[QC * c : QC * c + QC, :] = value[0:8, c * 128 : c * 128 + 128]
    block_sends(pay, idx, s1, s2)


def lift_kernel(m, t_in, csr, idx, r1, r2, r3, r4, pm, u, out, s1, s2, s3, s4, x_ref, t_ref):
    t_ref[...] = t_in[...]
    mid_edge_terms(csr, mid_edges(idx, r1, r2, r3, r4), t_ref)
    high, low = halves(m[...] + 0.2 * t_ref[...])
    x_ref[0:64, :] = high
    x_ref[64:128, :] = low
    x_ref[128:192, :] = high
    x_ref[192:256, :] = jnp.zeros((64, LANES), BF16)
    for n in range(4):
        out[:, chunk(n)] = u[:, chunk(n)] + dot(pm[...], x_ref[:, chunk(n)])
    fine_sends(out, idx, s1, s2, s3, s4)


WX = 10
WROWS = WX * 16


def place(window, own, r1, r2, r3, r4, idx):
    x_even, y_even = even(idx, 0), even(idx, 1)
    window[...] = jnp.zeros((QC * WROWS, 128), F32)

    def put(plane, y, tile):
        window[pl.ds(plane * 16 + 4 + y, QC, stride=WROWS), :] = tile

    for y in range(4):
        for x in range(4):
            c = 4 * x + y
            put(3 + x, y, own[QC * c : QC * c + QC, :])
        for x in range(3):
            rows = slice(QC * (4 * x + y), QC * (4 * x + y) + QC)
            put(x, y, jnp.where(x_even, r2[rows, :], r1[rows, :]))
            put(7 + x, y, jnp.where(x_even, r1[rows, :], r2[rows, :]))
    for plane in range(WX):
        for y in range(3):
            rows = slice(QC * (3 * plane + y), QC * (3 * plane + y) + QC)
            put(plane, y - 3, jnp.where(y_even, r4[rows, :], r3[rows, :]))
            put(plane, y + 4, jnp.where(y_even, r3[rows, :], r4[rows, :]))


def coarse_sweep(c_ref, out_ref, g_ref, coef, kc, first, last):
    def rows(d, plane):
        return pl.ds(pl.multiple_of(d * WROWS + plane * 16, 16), 16)

    def step(plane, carry):
        c = [c_ref[rows(d, plane), :] for d in range(QC)]
        weights = [coef[n, pl.ds(pl.multiple_of(plane * 16, 16), 16), :] for n in range(6)]
        for d in range(QC):
            t = g_ref[rows(d, plane), :] - 4.0 * c[d]
            for j in range(QC):
                t = t - kc[j, d] * c[j]
            if d & 4:
                t = t + weights[1] * c_ref[rows(d - 4, plane + 1), :]
            else:
                t = t + weights[0] * c_ref[rows(d + 4, plane - 1), :]
            if d & 2:
                t = t + weights[3] * sub_roll(c[d - 2], -1)
            else:
                t = t + weights[2] * sub_roll(c[d + 2], 1)
            if d & 1:
                t = t + weights[5] * pltpu.roll(c[d - 1], 127, 1)
            else:
                t = t + weights[4] * pltpu.roll(c[d + 1], 1, 1)
            out_ref[rows(d, plane), :] = c[d] + 0.2 * t
        return carry

    lax.fori_loop(first, last, step, 0)


def coarse_kernel(own, r1, r2, r3, r4, kc, idx, coef, g, pay, s1, s2, one, two):
    place(g, own, r1, r2, r3, r4, idx)
    one[...] = 0.2 * g[...]
    coarse_sweep(one, two, g, coef, kc, 1, 9)
    coarse_sweep(two, one, g, coef, kc, 2, 8)
    coarse_sweep(one, two, g, coef, kc, 3, 7)
    for c in range(COLS):
        row = (3 + c // 4) * 16 + 4 + c % 4
        pay[QC * c : QC * c + QC, :] = two[pl.ds(row, QC, stride=WROWS), :]
    block_sends(pay, idx, s1, s2)


def correct_kernel(
    own, r1, r2, r3, r4, kc, idx, g, coef, spread, m, gm, csr, q1, q2, q3, q4, km,
    out, s1, s2, s3, s4, one, two, x_ref, t_ref, m_ref,
):
    place(one, own, r1, r2, r3, r4, idx)
    coarse_sweep(one, two, g, coef, kc, 1, 9)
    coarse_sweep(two, one, g, coef, kc, 2, 8)

    def lifted(x, y, rows):
        total = None
        for d in range(QC):
            row = d * WROWS + (3 + x) * 16 + 4 + y
            part = spread[d, rows, :] * one[row : row + 1, :]
            total = part if total is None else total + part
        return total

    whole = slice(0, QM)
    for c in range(COLS):
        lanes = slice(c * 128, c * 128 + 128)
        m_ref[:, lanes] = m[:, lanes] + lifted(c // 4, c % 4, whole)
    below_x, above_x, below_y, above_y = mid_edges(idx, q1, q2, q3, q4)
    below_x = below_x + jnp.concatenate([lifted(-1, y, slice(48, 64)) for y in range(4)], axis=1)
    above_x = above_x + jnp.concatenate([lifted(4, y, slice(0, 16)) for y in range(4)], axis=1)
    below_rows, above_rows = [], []
    for i in range(4):
        last, first = slice(16 * i + 8, 16 * i + 16), slice(16 * i, 16 * i + 8)
        below_rows.append(jnp.concatenate([lifted(x, -1, last) for x in range(4)], axis=1))
        above_rows.append(jnp.concatenate([lifted(x, 4, first) for x in range(4)], axis=1))
    below_y = below_y + jnp.concatenate(below_rows, axis=0)
    above_y = above_y + jnp.concatenate(above_rows, axis=0)
    mid_local(m_ref, gm, csr, km, t_ref, x_ref)
    mid_edge_terms(csr, (below_x, above_x, below_y, above_y), t_ref)
    out[...] = m_ref[...] + 0.2 * t_ref[...]
    mid_sends(out, idx, s1, s2, s3, s4)


def swap(values, axis, odd):
    count = lax.axis_size(axis)
    pairs = [(i, (((i + odd) ^ 1) - odd) % count) for i in range(count)]
    return lax.ppermute(values, axis, pairs)


def exchange(sends):
    s1, s2, s3, s4 = sends
    return swap(s1, "gx", 0), swap(s2, "gx", 1), swap(s3, "yz", 0), swap(s4, "yz", 1)


def exchange_blocks(idx, own, s1, s2):
    r1, r2 = swap(s1, "gx", 0), swap(s2, "gx", 1)
    s3, s4 = call(row_kernel, [((QC * 3 * WX, 128), F32)] * 2, (), (0,))(idx, own, r1, r2)
    return own, r1, r2, swap(s3, "yz", 0), swap(s4, "yz", 1)


def body(seed, scale, coef, fine, smooth, mid, coarse, pmid, plow, noise, inc):
    idx = jnp.stack(
        [
            lax.axis_index("gx"),
            lax.axis_index("yz"),
            jnp.int32(lax.axis_size("gx")),
            jnp.int32(lax.axis_size("yz")),
        ]
    ).astype(jnp.int32)
    slots = slot_matrix()
    to_slot, from_slot = jnp.asarray(slots, BF16), jnp.asarray(slots.T, BF16)

    fine_field = ((SF, LANES), F32)
    fine_faces = [((40, 512), F32)] * 2 + [((48, 512), F32)] * 2
    mid_field = ((QM, LANES), F32)
    mid_faces = [((16, 512), F32)] * 2 + [((32, 512), F32)] * 2
    xf, tf = pltpu.VMEM((512, LANES), BF16), pltpu.VMEM((SF, LANES), F32)
    xm, tm = pltpu.VMEM((256, LANES), BF16), pltpu.VMEM((QM, LANES), F32)
    window = ((QC * WROWS, 128), F32)
    windows = [pltpu.VMEM((QC * WROWS, 128), F32)] * 2
    blocks = [((QC * COLS, 128), F32)] + [((QC * 12, 128), F32)] * 2

    operands = (
        seed.reshape(QF * COLS, 128),
        scale.reshape(COLS, 128),
        coef.reshape(3 * COLS, 128),
        to_slot,
        smooth,
        fine,
        noise,
        mid,
        pmid.T,
        plow.T,
    )
    g, u, csx, csr, s1, s2, s3, s4, kf, sf, nf, pmt, pm, km, plt, spread = call(
        first_kernel,
        [fine_field, fine_field, ((16, 512), F32), ((8, LANES), F32)]
        + [((56, 512), F32)] * 2
        + [((48, 512), F32)] * 2
        + [
            ((SF, 768), BF16),
            ((SF, 768), BF16),
            ((QF, 768), BF16),
            ((QM, 768), BF16),
            ((SF, 256), BF16),
            ((QM, 256), BF16),
            ((16, 256), BF16),
            ((QC, QM, 128), F32),
        ],
        [xf]
        + [pltpu.VMEM(operand.shape, operand.dtype) for operand in operands]
        + [pltpu.SemaphoreType.DMA((len(operands),))],
        (10,),
        range(10),
    )(*operands, idx)

    def fine_local(u):
        (t,) = call(fine_local_kernel, [fine_field], [xf])(u, g, csr, kf)
        return t

    def mid_local_part(m):
        (t,) = call(mid_local_kernel, [mid_field], [xm])(m, gm, csr, km)
        return t

    first = exchange((s1, s2, s3, s4))
    u, *sends = call(
        spread_kernel,
        [fine_field] + fine_faces[:2] + [((88, 512), F32)] * 2,
        [xf, tf],
        (3,),
    )(u, fine_local(u), csr, idx, *first, sf, csx)
    edges = exchange(sends)
    (coefw,) = call(coefficient_kernel, [((6, WROWS, 128), F32)], (), (0,))(
        idx, csx, first[0], first[1], edges[2], edges[3]
    )
    gm, m, *sends = call(restrict_kernel, [mid_field, mid_field] + mid_faces, [xf, tf], (2,))(
        fine_local(u), csr, idx, *edges, pmt
    )
    edges = exchange(sends)
    m, *sends = call(mid_kernel, [mid_field] + mid_faces, [tm], (3,))(
        m, mid_local_part(m), csr, idx, *edges
    )
    edges = exchange(sends)
    pay = call(low_kernel, blocks, [xm, tm], (2,))(mid_local_part(m), csr, idx, *edges, plt)
    gw, *pay = call(coarse_kernel, [window] + blocks, windows, (5, 6))(
        *exchange_blocks(idx, *pay), coarse, idx, coefw
    )
    m, *sends = call(
        correct_kernel,
        [mid_field] + mid_faces,
        windows + [xm, tm, pltpu.VMEM((QM, LANES), F32)],
        (5, 6),
    )(*exchange_blocks(idx, *pay), coarse, idx, gw, coefw, spread, m, gm, csr, *edges, km)
    edges = exchange(sends)
    u, *sends = call(lift_kernel, [fine_field] + fine_faces, [xm, tm], (3,))(
        m, mid_local_part(m), csr, idx, *edges, pm, u
    )
    edges = exchange(sends)
    u, *sends = call(sweep_kernel, [fine_field] + fine_faces, [xf, tf], (3,))(
        u, fine_local(u), csr, idx, *edges, sf
    )
    edges = exchange(sends)
    out, prev = call(
        last_kernel,
        [((QF * COLS, 128), F32)] * 2,
        [xf, tf, pltpu.VMEM((SF, LANES), F32)],
        (3,),
    )(u, fine_local(u), csr, idx, *edges, sf, nf, from_slot, inc.reshape(COLS, 128))
    shape = seed.shape
    return out.reshape(shape), prev.reshape(shape)


def solution(mesh):
    cell, field = P("gx", "yz", None), P(None, "gx", "yz", None)
    return jax.shard_map(
        body,
        mesh=mesh,
        in_specs=(field, cell, field) + (P(),) * 7 + (cell,),
        out_specs=(field, field),
        check_vma=False,
    )
```

```python
import numpy as np
import jax
import jax.numpy as jnp
from jax import lax
from jax.sharding import PartitionSpec as P
from jax.experimental import pallas as pl
from jax.experimental.pallas import tpu as pltpu

NF = 6
QF = 216
SF = 240
QM = 64
QC = 8
COLS = 16
LANES = COLS * 128
F32 = jnp.float32
BF16 = jnp.bfloat16


def fine_slots():
    slots = []
    for i in range(6):
        slots += [(i, 0, k) for k in range(6)] + [None] * 2
        slots += [(i, 5, k) for k in range(6)] + [None] * 2
        slots += [(i, j, 0) for j in range(1, 5)] + [(i, j, 5) for j in range(1, 5)]
        slots += [(i, j, k) for j in range(1, 5) for k in range(1, 5)]
    return slots


def slot_matrix():
    to_slot = np.zeros((SF, QF), np.float32)
    for slot, node in enumerate(fine_slots()):
        if node is not None:
            to_slot[slot, (node[0] * 6 + node[1]) * 6 + node[2]] = 1.0
    return to_slot


def call(kernel, outs, scratch=(), smem=(), hbm=(), cost=None):
    def run(*operands):
        specs = [
            pl.BlockSpec(
                memory_space=pltpu.SMEM if n in smem else pltpu.HBM if n in hbm else pltpu.VMEM
            )
            for n in range(len(operands))
        ]
        operands = [
            pltpu.with_memory_space_constraint(value, pltpu.HBM) if n in hbm else value
            for n, value in enumerate(operands)
        ]
        return pl.pallas_call(
            kernel,
            out_shape=tuple(jax.ShapeDtypeStruct(s, d) for s, d in outs),
            in_specs=specs,
            out_specs=tuple(pl.BlockSpec(memory_space=pltpu.VMEM) for _ in outs),
            scratch_shapes=list(scratch),
            compiler_params=pltpu.CompilerParams(vmem_limit_bytes=20 * 1024 * 1024),
            cost_estimate=cost,
        )(*operands)

    return run


def dot(a, b):
    return lax.dot_general(a, b, (((1,), (0,)), ((), ())), preferred_element_type=F32)


def dot_nt(a, b):
    return lax.dot_general(a, b, (((1,), (1,)), ((), ())), preferred_element_type=F32)


def halves(values):
    high = values.astype(BF16)
    return high, (values - high.astype(F32)).astype(BF16)


def lane_roll(values, shift):
    return jnp.concatenate(
        [
            pltpu.roll(values[:, c * 128 : (c + 1) * 128], shift % 128, 1)
            for c in range(values.shape[1] // 128)
        ],
        axis=1,
    )


def sub_roll(values, shift):
    return pltpu.roll(values, shift % values.shape[0], 0)


def sublane(shape):
    return lax.broadcasted_iota(jnp.int32, shape, 0)


def y_from_lower(values):
    parts, edge = [], jnp.zeros((values.shape[0], 128), F32)
    for x in range(4):
        parts += [edge, values[:, x * 512 : x * 512 + 384]]
    return jnp.concatenate(parts, axis=1)


def y_from_upper(values):
    parts, edge = [], jnp.zeros((values.shape[0], 128), F32)
    for x in range(4):
        parts += [values[:, x * 512 + 128 : x * 512 + 512], edge]
    return jnp.concatenate(parts, axis=1)


def y_column(values, y):
    return jnp.concatenate(
        [values[:, x * 512 + y * 128 : x * 512 + y * 128 + 128] for x in range(4)], axis=1
    )


def even(idx_ref, axis):
    return idx_ref[axis] % 2 == 0


def prepare(slot, fine, smooth, noise, mid, pmid_t, plow_t, kf, sf, nf, pmt, pm, km, plt, spread):
    def grid(rows, columns):
        return tuple(lax.broadcasted_iota(jnp.int32, (rows, columns), n) for n in range(2))

    def one_hot(n):
        row, col = grid(n, n)
        return jnp.where(row == col, 1.0, 0.0).astype(BF16)

    def wide(out, rows, high, low):
        gap = jnp.zeros((rows, 16), BF16)
        out[:, 0:256] = jnp.concatenate([high, gap], axis=1)
        out[:, 256:512] = jnp.concatenate([high, gap], axis=1)
        out[:, 512:768] = jnp.concatenate([low, gap], axis=1)

    def narrow(out, high, low):
        row, col = grid(64, 128)
        twice = jnp.where((row == col) | (row == col - 64), 1.0, 0.0).astype(BF16)
        once = jnp.where(row == col, 1.0, 0.0).astype(BF16)
        out[:, 0:128] = dot(high, twice).astype(BF16)
        out[:, 128:256] = dot(low, once).astype(BF16)

    def moved(left, part, right):
        return dot_nt(dot_nt(left, part).astype(BF16), right).astype(BF16)

    wide(sf, SF, *[moved(slot, part, slot) for part in halves(smooth)])
    wide(kf, SF, *[moved(slot, part, slot) for part in halves(fine)])
    turn = one_hot(QF)
    wide(nf, QF, *[moved(turn, part, slot) for part in halves(noise)])
    high, low = halves(pmid_t)
    wide(pmt, QM, *[dot_nt(part, slot).astype(BF16) for part in (high, low)])
    narrow(pm, *[dot_nt(slot, part).astype(BF16) for part in (high, low)])
    turn = one_hot(QM)
    narrow(km, *[dot_nt(turn, part).astype(BF16) for part in halves(mid)])
    high, low = halves(plow_t)
    rest = (plow_t - high.astype(F32) - low.astype(F32)).astype(BF16)
    gap = jnp.zeros((8, QM), BF16)
    narrow(plt, *[jnp.concatenate([part, gap], axis=0) for part in (high, low)])
    columns = dot_nt(turn, high) + dot_nt(turn, low) + dot_nt(turn, rest)
    for d in range(QC):
        spread[d] = jnp.broadcast_to(columns[:, d : d + 1], (QM, 128))


def split_fine(values, x_ref, lanes):
    high, low = halves(values)
    x_ref[0:SF, lanes] = high
    x_ref[256 : 256 + SF, lanes] = low


def clear_fine(x_ref):
    x_ref[SF:256, :] = jnp.zeros((256 - SF, LANES), BF16)
    x_ref[256 + SF : 512, :] = jnp.zeros((256 - SF, LANES), BF16)


def fine_product(w_ref, x_ref, lanes):
    return dot(w_ref[:, 0:512], x_ref[:, lanes]) + dot(w_ref[:, 512:768], x_ref[0:256, lanes])


def mid_product(w_ref, values, x_ref):
    high, low = halves(values)
    x_ref[0:64, :] = high
    x_ref[64:128, :] = low
    x_ref[128:192, :] = high
    x_ref[192:256, :] = jnp.zeros((64, LANES), BF16)
    return dot(w_ref[...], x_ref[...])


def chunk(n):
    return slice(n * 512, n * 512 + 512)


def fine_sends(u_ref, idx, s1, s2, s3, s4):
    x_even, y_even = even(idx, 0), even(idx, 1)
    upper, lower = u_ref[200:240, 1536:2048], u_ref[0:40, 0:512]
    s1[0:40, :] = jnp.where(x_even, upper, lower)
    s2[0:40, :] = jnp.where(x_even, lower, upper)
    for i in range(6):
        upper = y_column(u_ref[40 * i + 8 : 40 * i + 16, :], 3)
        lower = y_column(u_ref[40 * i : 40 * i + 8, :], 0)
        s3[8 * i : 8 * i + 8, :] = jnp.where(y_even, upper, lower)
        s4[8 * i : 8 * i + 8, :] = jnp.where(y_even, lower, upper)


def fine_local_kernel(u_ref, g_ref, csr, kf, t_ref, x_ref):
    clear_fine(x_ref)
    for n in range(4):
        u = u_ref[:, chunk(n)]
        split_fine(u, x_ref, chunk(n))
        t_ref[:, chunk(n)] = g_ref[:, chunk(n)] - 4.0 * u - fine_product(kf, x_ref, chunk(n))
    t_ref[0:40, 512:2048] += csr[0:1, 512:2048] * u_ref[200:240, 0:1536]
    t_ref[200:240, 0:1536] += csr[1:2, 0:1536] * u_ref[0:40, 512:2048]
    row = sublane((8, LANES))
    for i in range(6):
        base = 40 * i
        first, last, sides = (u_ref[base + 8 * n : base + 8 * n + 8, :] for n in range(3))
        t0 = csr[2:3, :] * y_from_lower(last)
        t1 = csr[3:4, :] * y_from_upper(first)
        for n, tile, extra in ((0, first, t0), (1, last, t1)):
            lower = csr[4:5, :] * sub_roll(lane_roll(tile, 1), 3)
            upper = csr[5:6, :] * sub_roll(lane_roll(tile, -1), 5)
            t_ref[base + 8 * n : base + 8 * n + 8, :] += (
                extra + jnp.where(row == 0, lower, 0.0) + jnp.where(row == 5, upper, 0.0)
            )
        lower = csr[4:5, :] * sub_roll(lane_roll(sides, 1), 4)
        upper = csr[5:6, :] * sub_roll(lane_roll(sides, -1), 4)
        t_ref[base + 16 : base + 24, :] += jnp.where(row < 4, lower, upper)


def fine_edges(n, t_in, csr, idx, r1, r2, r3, r4, t_ref):
    x_even, y_even = even(idx, 0), even(idx, 1)
    lanes = chunk(n)
    t_ref[:, lanes] = t_in[:, lanes]
    if n == 0:
        below = jnp.where(x_even, r2[0:40, :], r1[0:40, :])
        t_ref[0:40, lanes] += csr[0:1, lanes] * below
    if n == 3:
        above = jnp.where(x_even, r1[0:40, :], r2[0:40, :])
        t_ref[200:240, lanes] += csr[1:2, lanes] * above
    edge = slice(n * 128, n * 128 + 128)
    first, last = (slice(n * 512 + y * 128, n * 512 + y * 128 + 128) for y in (0, 3))
    for i in range(6):
        rows = slice(8 * i, 8 * i + 8)
        below = jnp.where(y_even, r4[rows, edge], r3[rows, edge])
        above = jnp.where(y_even, r3[rows, edge], r4[rows, edge])
        t_ref[40 * i : 40 * i + 8, first] += csr[2:3, first] * below
        t_ref[40 * i + 8 : 40 * i + 16, last] += csr[3:4, last] * above


def fine_update(u_ref, t_in, csr, idx, received, out_ref, sf, x_ref, t_ref):
    clear_fine(x_ref)
    for n in range(4):
        fine_edges(n, t_in, csr, idx, *received, t_ref)
        t = t_ref[:, chunk(n)]
        split_fine(t, x_ref, chunk(n))
        out_ref[:, chunk(n)] = u_ref[:, chunk(n)] + 0.25 * t + fine_product(sf, x_ref, chunk(n))


def first_kernel(
    seed_in, scale_in, coef_in, slot_in, smooth_in, fine_in, noise_in, mid_in, pmid_in, plow_in, idx,
    g, u1, csx, csr, s1, s2, s3, s4, kf, sf, nf, pmt, pm, km, plt, spread,
    x_ref, seed, scale, coef, slot, smooth, fine, noise, mid, pmid, plow, done,
):
    copies = {}
    for n, (name, source, target) in enumerate(
        (
            ("slot", slot_in, slot),
            ("smooth", smooth_in, smooth),
            ("fine", fine_in, fine),
            ("noise", noise_in, noise),
            ("pmid", pmid_in, pmid),
            ("plow", plow_in, plow),
            ("mid", mid_in, mid),
            ("scale", scale_in, scale),
            ("coef", coef_in, coef),
            ("seed", seed_in, seed),
        )
    ):
        copies[name] = pltpu.make_async_copy(source, target, done.at[n])
        copies[name].start()
    clear_fine(x_ref)
    x_ref[QF:SF, :] = jnp.zeros((SF - QF, LANES), BF16)
    x_ref[256 + QF : 256 + SF, :] = jnp.zeros((SF - QF, LANES), BF16)
    csr[...] = jnp.zeros((8, LANES), F32)
    csx[...] = jnp.zeros((16, 512), F32)
    for name in ("slot", "smooth", "fine", "noise", "pmid", "plow", "mid"):
        copies[name].wait()
    matrices = (ref[...] for ref in (slot, fine, smooth, noise, mid, pmid, plow))
    prepare(*matrices, kf, sf, nf, pmt, pm, km, plt, spread)
    copies["scale"].wait()
    copies["coef"].wait()
    over = 1.0 / scale[...]
    lane = lax.broadcasted_iota(jnp.int32, (1, 128), 1)
    for c in range(COLS):
        x, y = c // 4, c % 4
        lanes = slice(c * 128, c * 128 + 128)
        for d in range(3):
            value = coef[16 * d + c : 16 * d + c + 1, :] * over[c : c + 1, :]
            csx[4 * x + d : 4 * x + d + 1, y * 128 : y * 128 + 128] = value
            low, high = 0.9 * value, 0.3 * value
            if d == 0 and x == 0:
                low = jnp.where(idx[0] == 0, 0.0, low)
            if d == 0 and x == 3:
                high = jnp.where(idx[0] == idx[2] - 1, 0.0, high)
            if d == 1 and y == 0:
                low = jnp.where(idx[1] == 0, 0.0, low)
            if d == 1 and y == 3:
                high = jnp.where(idx[1] == idx[3] - 1, 0.0, high)
            if d == 2:
                low = jnp.where(lane == 0, 0.0, low)
                high = jnp.where(lane == 127, 0.0, high)
            csr[2 * d : 2 * d + 1, lanes] = low
            csr[2 * d + 1 : 2 * d + 2, lanes] = high
    copies["seed"].wait()
    for c in range(COLS):
        lanes = slice(c * 128, c * 128 + 128)
        values = seed[pl.ds(c, QF, stride=COLS), :] * over[c : c + 1, :]
        high, low = halves(values)
        rest = (values - high.astype(F32) - low.astype(F32)).astype(BF16)
        g[:, lanes] = dot(slot[...], high) + dot(slot[...], low) + dot(slot[...], rest)
    for n in range(4):
        values = g[:, chunk(n)]
        split_fine(values, x_ref, chunk(n))
        u1[:, chunk(n)] = 0.25 * values + fine_product(sf, x_ref, chunk(n))
    fine_sends(u1, idx, s1, s2, s3, s4)
    x_even = even(idx, 0)
    far, near = csx[4:16, :], csx[0:12, :]
    gap = jnp.zeros((4, 512), F32)
    s1[40:56, :] = jnp.concatenate([jnp.where(x_even, far, near), gap], axis=0)
    s2[40:56, :] = jnp.concatenate([jnp.where(x_even, near, far), gap], axis=0)


def spread_kernel(u, t_in, csr, idx, r1, r2, r3, r4, sf, csx, out, s1, s2, s3, s4, x_ref, t_ref):
    fine_update(u, t_in, csr, idx, (r1, r2, r3, r4), out, sf, x_ref, t_ref)
    fine_sends(out, idx, s1, s2, s3, s4)
    x_even, y_even = even(idx, 0), even(idx, 1)
    left = jnp.where(x_even, r2[40:56, :], r1[40:56, :])
    right = jnp.where(x_even, r1[40:56, :], r2[40:56, :])
    planes = jnp.concatenate([left[0:12], csx[...], right[0:12]], axis=0)
    gap = jnp.zeros((40, 128), F32)
    far, near = planes[:, 128:512], planes[:, 0:384]
    s3[48:88, :] = jnp.concatenate([jnp.where(y_even, far, near), gap], axis=1)
    s4[48:88, :] = jnp.concatenate([jnp.where(y_even, near, far), gap], axis=1)


def coefficient_kernel(idx, csx, r1, r2, r3, r4, coef):
    x_even, y_even = even(idx, 0), even(idx, 1)
    left = jnp.where(x_even, r2[40:56, :], r1[40:56, :])
    right = jnp.where(x_even, r1[40:56, :], r2[40:56, :])
    planes = jnp.concatenate([left[0:12], csx[...], right[0:12]], axis=0)
    below = jnp.where(y_even, r4[48:88, :], r3[48:88, :])
    above = jnp.where(y_even, r3[48:88, :], r4[48:88, :])
    first_x, last_x = idx[0] == 0, idx[0] == idx[2] - 1
    first_y, last_y = idx[1] == 0, idx[1] == idx[3] - 1
    lane = lax.broadcasted_iota(jnp.int32, (1, 128), 1)
    coef[...] = jnp.zeros((6, WROWS, 128), F32)
    for plane in range(WX):
        for y in range(-3, 7):
            source, at = (below, y + 3) if y < 0 else (planes, y) if y < 4 else (above, y - 4)
            row = slice(plane * 16 + 4 + y, plane * 16 + 5 + y)
            for d in range(3):
                value = source[4 * plane + d : 4 * plane + d + 1, at * 128 : at * 128 + 128]
                low, high = 0.9 * value, 0.3 * value
                if d == 0 and plane == 3:
                    low = jnp.where(first_x, 0.0, low)
                if d == 0 and plane == 6:
                    high = jnp.where(last_x, 0.0, high)
                if d == 1 and y == 0:
                    low = jnp.where(first_y, 0.0, low)
                if d == 1 and y == 3:
                    high = jnp.where(last_y, 0.0, high)
                if d == 2:
                    low = jnp.where(lane == 0, 0.0, low)
                    high = jnp.where(lane == 127, 0.0, high)
                coef[2 * d, row, :] = low
                coef[2 * d + 1, row, :] = high


def sweep_kernel(u, t_in, csr, idx, r1, r2, r3, r4, sf, out, s1, s2, s3, s4, x_ref, t_ref):
    fine_update(u, t_in, csr, idx, (r1, r2, r3, r4), out, sf, x_ref, t_ref)
    fine_sends(out, idx, s1, s2, s3, s4)


def restrict_kernel(t_in, csr, idx, r1, r2, r3, r4, pmt, gm, m1, s1, s2, s3, s4, x_ref, t_ref):
    clear_fine(x_ref)
    for n in range(4):
        fine_edges(n, t_in, csr, idx, r1, r2, r3, r4, t_ref)
        split_fine(t_ref[:, chunk(n)], x_ref, chunk(n))
        value = fine_product(pmt, x_ref, chunk(n))
        gm[:, chunk(n)] = value
        m1[:, chunk(n)] = 0.2 * value
    mid_sends(m1, idx, s1, s2, s3, s4)


def last_kernel(
    u, t_in, csr, idx, r1, r2, r3, r4, sf, nf, from_slot, inc, out, prev, x_ref, t_ref, w_ref
):
    fine_update(u, t_in, csr, idx, (r1, r2, r3, r4), w_ref, sf, x_ref, t_ref)
    slot = from_slot[...]
    for n in range(4):
        values = w_ref[:, chunk(n)]
        split_fine(values, x_ref, chunk(n))
        high, low = halves(values)
        rest = (values - high.astype(F32) - low.astype(F32)).astype(BF16)
        natural = dot(slot, high) + dot(slot, low) + dot(slot, rest)
        noise = fine_product(nf, x_ref, chunk(n))
        for y in range(4):
            c = 4 * n + y
            lanes = slice(y * 128, y * 128 + 128)
            out[pl.ds(c, QF, stride=COLS), :] = natural[:, lanes]
            prev[pl.ds(c, QF, stride=COLS), :] = (
                natural[:, lanes] + inc[c : c + 1, :] * noise[:, lanes]
            )


def mid_sends(m_ref, idx, s1, s2, s3, s4):
    x_even, y_even = even(idx, 0), even(idx, 1)
    upper, lower = m_ref[48:64, 1536:2048], m_ref[0:16, 0:512]
    s1[...] = jnp.where(x_even, upper, lower)
    s2[...] = jnp.where(x_even, lower, upper)
    for i in range(4):
        upper = y_column(m_ref[16 * i + 8 : 16 * i + 16, :], 3)
        lower = y_column(m_ref[16 * i : 16 * i + 8, :], 0)
        s3[8 * i : 8 * i + 8, :] = jnp.where(y_even, upper, lower)
        s4[8 * i : 8 * i + 8, :] = jnp.where(y_even, lower, upper)


def mid_edges(idx, r1, r2, r3, r4):
    x_even, y_even = even(idx, 0), even(idx, 1)
    return (
        jnp.where(x_even, r2[...], r1[...]),
        jnp.where(x_even, r1[...], r2[...]),
        jnp.where(y_even, r4[...], r3[...]),
        jnp.where(y_even, r3[...], r4[...]),
    )


def mid_local(m_ref, g_ref, csr, km, t_ref, x_ref):
    m = m_ref[...]
    t_ref[...] = g_ref[...] - 4.0 * m - mid_product(km, m, x_ref)
    t_ref[0:16, 512:2048] += csr[0:1, 512:2048] * m_ref[48:64, 0:1536]
    t_ref[48:64, 0:1536] += csr[1:2, 0:1536] * m_ref[0:16, 512:2048]
    row = sublane((8, LANES))
    for i in range(4):
        base = 16 * i
        first, last = m_ref[base : base + 8, :], m_ref[base + 8 : base + 16, :]
        extra0 = csr[2:3, :] * sub_roll(y_from_lower(last), 4)
        extra1 = csr[3:4, :] * sub_roll(y_from_upper(first), 4)
        for n, tile, extra in (
            (0, first, jnp.where(row < 4, extra0, 0.0)),
            (1, last, jnp.where(row >= 4, extra1, 0.0)),
        ):
            lower = csr[4:5, :] * sub_roll(lane_roll(tile, 1), 5)
            upper = csr[5:6, :] * sub_roll(lane_roll(tile, -1), 3)
            t_ref[base + 8 * n : base + 8 * n + 8, :] += (
                extra + jnp.where(row % 4 == 0, lower, 0.0) + jnp.where(row % 4 == 3, upper, 0.0)
            )


def mid_edge_terms(csr, edges, t_ref):
    below_x, above_x, below_y, above_y = edges
    t_ref[0:16, 0:512] += csr[0:1, 0:512] * below_x
    t_ref[48:64, 1536:2048] += csr[1:2, 1536:2048] * above_x
    row = sublane((8, 128))
    for i in range(4):
        rows = slice(8 * i, 8 * i + 8)
        for x in range(4):
            edge = slice(x * 128, x * 128 + 128)
            first, last = (slice(x * 512 + y * 128, x * 512 + y * 128 + 128) for y in (0, 3))
            below = csr[2:3, first] * sub_roll(below_y[rows, edge], 4)
            above = csr[3:4, last] * sub_roll(above_y[rows, edge], 4)
            t_ref[16 * i : 16 * i + 8, first] += jnp.where(row < 4, below, 0.0)
            t_ref[16 * i + 8 : 16 * i + 16, last] += jnp.where(row >= 4, above, 0.0)


def mid_local_kernel(m_ref, g_ref, csr, km, t_ref, x_ref):
    mid_local(m_ref, g_ref, csr, km, t_ref, x_ref)


def mid_kernel(m, t_in, csr, idx, r1, r2, r3, r4, out, s1, s2, s3, s4, t_ref):
    t_ref[...] = t_in[...]
    mid_edge_terms(csr, mid_edges(idx, r1, r2, r3, r4), t_ref)
    out[...] = m[...] + 0.2 * t_ref[...]
    mid_sends(out, idx, s1, s2, s3, s4)


def block_sends(pay, idx, s1, s2):
    x_even = even(idx, 0)
    far, near = pay[32:128, :], pay[0:96, :]
    s1[...] = jnp.where(x_even, far, near)
    s2[...] = jnp.where(x_even, near, far)


def row_kernel(idx, own, r1, r2, s3, s4):
    x_even, y_even = even(idx, 0), even(idx, 1)
    for plane in range(WX):
        tiles = []
        for y in range(4):
            if 3 <= plane < 7:
                at = QC * (4 * (plane - 3) + y)
                tiles.append(own[at : at + QC, :])
            else:
                at = QC * (4 * (plane % 7) + y)
                one, two = r1[at : at + QC, :], r2[at : at + QC, :]
                tiles.append(jnp.where(x_even == (plane < 3), two, one))
        for y in range(3):
            rows = slice(QC * (3 * plane + y), QC * (3 * plane + y) + QC)
            s3[rows, :] = jnp.where(y_even, tiles[y + 1], tiles[y])
            s4[rows, :] = jnp.where(y_even, tiles[y], tiles[y + 1])


def low_kernel(t_in, csr, idx, r1, r2, r3, r4, plt, pay, s1, s2, x_ref, t_ref):
    t_ref[...] = t_in[...]
    mid_edge_terms(csr, mid_edges(idx, r1, r2, r3, r4), t_ref)
    value = mid_product(plt, t_ref[...], x_ref)
    for c in range(COLS):
        pay[QC * c : QC * c + QC, :] = value[0:8, c * 128 : c * 128 + 128]
    block_sends(pay, idx, s1, s2)


def lift_kernel(m, t_in, csr, idx, r1, r2, r3, r4, pm, u, out, s1, s2, s3, s4, x_ref, t_ref):
    t_ref[...] = t_in[...]
    mid_edge_terms(csr, mid_edges(idx, r1, r2, r3, r4), t_ref)
    high, low = halves(m[...] + 0.2 * t_ref[...])
    x_ref[0:64, :] = high
    x_ref[64:128, :] = low
    x_ref[128:192, :] = high
    x_ref[192:256, :] = jnp.zeros((64, LANES), BF16)
    for n in range(4):
        out[:, chunk(n)] = u[:, chunk(n)] + dot(pm[...], x_ref[:, chunk(n)])
    fine_sends(out, idx, s1, s2, s3, s4)


WX = 10
WROWS = WX * 16


def place(window, own, r1, r2, r3, r4, idx):
    x_even, y_even = even(idx, 0), even(idx, 1)
    window[...] = jnp.zeros((QC * WROWS, 128), F32)

    def put(plane, y, tile):
        window[pl.ds(plane * 16 + 4 + y, QC, stride=WROWS), :] = tile

    for y in range(4):
        for x in range(4):
            c = 4 * x + y
            put(3 + x, y, own[QC * c : QC * c + QC, :])
        for x in range(3):
            rows = slice(QC * (4 * x + y), QC * (4 * x + y) + QC)
            put(x, y, jnp.where(x_even, r2[rows, :], r1[rows, :]))
            put(7 + x, y, jnp.where(x_even, r1[rows, :], r2[rows, :]))
    for plane in range(WX):
        for y in range(3):
            rows = slice(QC * (3 * plane + y), QC * (3 * plane + y) + QC)
            put(plane, y - 3, jnp.where(y_even, r4[rows, :], r3[rows, :]))
            put(plane, y + 4, jnp.where(y_even, r3[rows, :], r4[rows, :]))


def coarse_sweep(c_ref, out_ref, g_ref, coef, kc, first, last):
    def rows(d, plane):
        return pl.ds(pl.multiple_of(d * WROWS + plane * 16, 16), 16)

    def step(plane, carry):
        c = [c_ref[rows(d, plane), :] for d in range(QC)]
        weights = [coef[n, pl.ds(pl.multiple_of(plane * 16, 16), 16), :] for n in range(6)]
        for d in range(QC):
            t = g_ref[rows(d, plane), :] - 4.0 * c[d]
            for j in range(QC):
                t = t - kc[j, d] * c[j]
            if d & 4:
                t = t + weights[1] * c_ref[rows(d - 4, plane + 1), :]
            else:
                t = t + weights[0] * c_ref[rows(d + 4, plane - 1), :]
            if d & 2:
                t = t + weights[3] * sub_roll(c[d - 2], -1)
            else:
                t = t + weights[2] * sub_roll(c[d + 2], 1)
            if d & 1:
                t = t + weights[5] * pltpu.roll(c[d - 1], 127, 1)
            else:
                t = t + weights[4] * pltpu.roll(c[d + 1], 1, 1)
            out_ref[rows(d, plane), :] = c[d] + 0.2 * t
        return carry

    lax.fori_loop(first, last, step, 0)


def coarse_kernel(own, r1, r2, r3, r4, kc, idx, coef, g, pay, s1, s2, one, two):
    place(g, own, r1, r2, r3, r4, idx)
    one[...] = 0.2 * g[...]
    coarse_sweep(one, two, g, coef, kc, 1, 9)
    coarse_sweep(two, one, g, coef, kc, 2, 8)
    coarse_sweep(one, two, g, coef, kc, 3, 7)
    for c in range(COLS):
        row = (3 + c // 4) * 16 + 4 + c % 4
        pay[QC * c : QC * c + QC, :] = two[pl.ds(row, QC, stride=WROWS), :]
    block_sends(pay, idx, s1, s2)


def correct_kernel(
    own, r1, r2, r3, r4, kc, idx, g, coef, spread, m, gm, csr, q1, q2, q3, q4, km,
    out, s1, s2, s3, s4, one, two, x_ref, t_ref, m_ref,
):
    place(one, own, r1, r2, r3, r4, idx)
    coarse_sweep(one, two, g, coef, kc, 1, 9)
    coarse_sweep(two, one, g, coef, kc, 2, 8)

    def lifted(x, y, rows):
        total = None
        for d in range(QC):
            row = d * WROWS + (3 + x) * 16 + 4 + y
            part = spread[d, rows, :] * one[row : row + 1, :]
            total = part if total is None else total + part
        return total

    whole = slice(0, QM)
    for c in range(COLS):
        lanes = slice(c * 128, c * 128 + 128)
        m_ref[:, lanes] = m[:, lanes] + lifted(c // 4, c % 4, whole)
    below_x, above_x, below_y, above_y = mid_edges(idx, q1, q2, q3, q4)
    below_x = below_x + jnp.concatenate([lifted(-1, y, slice(48, 64)) for y in range(4)], axis=1)
    above_x = above_x + jnp.concatenate([lifted(4, y, slice(0, 16)) for y in range(4)], axis=1)
    below_rows, above_rows = [], []
    for i in range(4):
        last, first = slice(16 * i + 8, 16 * i + 16), slice(16 * i, 16 * i + 8)
        below_rows.append(jnp.concatenate([lifted(x, -1, last) for x in range(4)], axis=1))
        above_rows.append(jnp.concatenate([lifted(x, 4, first) for x in range(4)], axis=1))
    below_y = below_y + jnp.concatenate(below_rows, axis=0)
    above_y = above_y + jnp.concatenate(above_rows, axis=0)
    mid_local(m_ref, gm, csr, km, t_ref, x_ref)
    mid_edge_terms(csr, (below_x, above_x, below_y, above_y), t_ref)
    out[...] = m_ref[...] + 0.2 * t_ref[...]
    mid_sends(out, idx, s1, s2, s3, s4)


def partners(step):
    nx, ny = lax.axis_size("gx"), lax.axis_size("yz")
    pairs = []
    for a in range(nx):
        for b in range(ny):
            to = (a, b)
            if step < 2:
                at = ((a + step) ^ 1) - step
                to = (at, b) if 0 <= at < nx else (a, b ^ 1)
            else:
                at = ((b + step - 2) ^ 1) - (step - 2)
                to = (a, at) if 0 <= at < ny else (a ^ 1, b)
            pairs.append((a * ny + b, to[0] * ny + to[1]))
    return pairs


def swap(values, step):
    return lax.ppermute(values, ("gx", "yz"), partners(step))


def exchange(sends):
    s1, s2, s3, s4 = sends
    r2, r1, r4, r3 = swap(s2, 1), swap(s1, 0), swap(s4, 3), swap(s3, 2)
    return r1, r2, r3, r4


def exchange_blocks(idx, own, s1, s2):
    r2, r1 = swap(s2, 1), swap(s1, 0)
    s3, s4 = call(row_kernel, [((QC * 3 * WX, 128), F32)] * 2, (), (0,))(idx, own, r1, r2)
    r4, r3 = swap(s4, 3), swap(s3, 2)
    return own, r1, r2, r3, r4


def body(seed, scale, coef, fine, smooth, mid, coarse, pmid, plow, noise, inc):
    idx = jnp.stack(
        [
            lax.axis_index("gx"),
            lax.axis_index("yz"),
            jnp.int32(lax.axis_size("gx")),
            jnp.int32(lax.axis_size("yz")),
        ]
    ).astype(jnp.int32)
    slots = slot_matrix()
    to_slot, from_slot = jnp.asarray(slots, BF16), jnp.asarray(slots.T, BF16)

    fine_field = ((SF, LANES), F32)
    fine_faces = [((40, 512), F32)] * 2 + [((48, 512), F32)] * 2
    mid_field = ((QM, LANES), F32)
    mid_faces = [((16, 512), F32)] * 2 + [((32, 512), F32)] * 2
    xf, tf = pltpu.VMEM((512, LANES), BF16), pltpu.VMEM((SF, LANES), F32)
    xm, tm = pltpu.VMEM((256, LANES), BF16), pltpu.VMEM((QM, LANES), F32)
    window = ((QC * WROWS, 128), F32)
    windows = [pltpu.VMEM((QC * WROWS, 128), F32)] * 2
    blocks = [((QC * COLS, 128), F32)] + [((QC * 12, 128), F32)] * 2

    operands = (
        seed.reshape(QF * COLS, 128),
        scale.reshape(COLS, 128),
        coef.reshape(3 * COLS, 128),
        to_slot,
        smooth,
        fine,
        noise,
        mid,
        pmid.T,
        plow.T,
    )
    g, u, csx, csr, s1, s2, s3, s4, kf, sf, nf, pmt, pm, km, plt, spread = call(
        first_kernel,
        [fine_field, fine_field, ((16, 512), F32), ((8, LANES), F32)]
        + [((56, 512), F32)] * 2
        + [((48, 512), F32)] * 2
        + [
            ((SF, 768), BF16),
            ((SF, 768), BF16),
            ((QF, 768), BF16),
            ((QM, 768), BF16),
            ((SF, 256), BF16),
            ((QM, 256), BF16),
            ((16, 256), BF16),
            ((QC, QM, 128), F32),
        ],
        [xf]
        + [pltpu.VMEM(operand.shape, operand.dtype) for operand in operands]
        + [pltpu.SemaphoreType.DMA((len(operands),))],
        (10,),
        range(10),
    )(*operands, idx)

    def fine_local(u):
        (t,) = call(fine_local_kernel, [fine_field], [xf])(u, g, csr, kf)
        return t

    def mid_local_part(m):
        (t,) = call(mid_local_kernel, [mid_field], [xm])(m, gm, csr, km)
        return t

    first = exchange((s1, s2, s3, s4))
    u, *sends = call(
        spread_kernel,
        [fine_field] + fine_faces[:2] + [((88, 512), F32)] * 2,
        [xf, tf],
        (3,),
    )(u, fine_local(u), csr, idx, *first, sf, csx)
    edges = exchange(sends)
    (coefw,) = call(coefficient_kernel, [((6, WROWS, 128), F32)], (), (0,))(
        idx, csx, first[0], first[1], edges[2], edges[3]
    )
    gm, m, *sends = call(restrict_kernel, [mid_field, mid_field] + mid_faces, [xf, tf], (2,))(
        fine_local(u), csr, idx, *edges, pmt
    )
    edges = exchange(sends)
    m, *sends = call(mid_kernel, [mid_field] + mid_faces, [tm], (3,))(
        m, mid_local_part(m), csr, idx, *edges
    )
    edges = exchange(sends)
    pay = call(low_kernel, blocks, [xm, tm], (2,))(mid_local_part(m), csr, idx, *edges, plt)
    gw, *pay = call(coarse_kernel, [window] + blocks, windows, (5, 6))(
        *exchange_blocks(idx, *pay), coarse, idx, coefw
    )
    m, *sends = call(
        correct_kernel,
        [mid_field] + mid_faces,
        windows + [xm, tm, pltpu.VMEM((QM, LANES), F32)],
        (5, 6),
    )(*exchange_blocks(idx, *pay), coarse, idx, gw, coefw, spread, m, gm, csr, *edges, km)
    edges = exchange(sends)
    u, *sends = call(lift_kernel, [fine_field] + fine_faces, [xm, tm], (3,))(
        m, mid_local_part(m), csr, idx, *edges, pm, u
    )
    edges = exchange(sends)
    u, *sends = call(sweep_kernel, [fine_field] + fine_faces, [xf, tf], (3,))(
        u, fine_local(u), csr, idx, *edges, sf
    )
    edges = exchange(sends)
    out, prev = call(
        last_kernel,
        [((QF * COLS, 128), F32)] * 2,
        [xf, tf, pltpu.VMEM((SF, LANES), F32)],
        (3,),
    )(u, fine_local(u), csr, idx, *edges, sf, nf, from_slot, inc.reshape(COLS, 128))
    shape = seed.shape
    return out.reshape(shape), prev.reshape(shape)


def solution(mesh):
    cell, field = P("gx", "yz", None), P(None, "gx", "yz", None)
    return jax.shard_map(
        body,
        mesh=mesh,
        in_specs=(field, cell, field) + (P(),) * 7 + (cell,),
        out_specs=(field, field),
        check_vma=False,
    )
```

```python
import numpy as np
import jax
import jax.numpy as jnp
from jax import lax
from jax.sharding import PartitionSpec as P
from jax.experimental import pallas as pl
from jax.experimental.pallas import tpu as pltpu

NF = 6
QF = 216
SF = 240
QM = 64
QC = 8
COLS = 16
LANES = COLS * 128
F32 = jnp.float32
BF16 = jnp.bfloat16


def fine_slots():
    slots = []
    for i in range(6):
        slots += [(i, 0, k) for k in range(6)] + [None] * 2
        slots += [(i, 5, k) for k in range(6)] + [None] * 2
        slots += [(i, j, 0) for j in range(1, 5)] + [(i, j, 5) for j in range(1, 5)]
        slots += [(i, j, k) for j in range(1, 5) for k in range(1, 5)]
    return slots


def slot_matrix():
    to_slot = np.zeros((SF, QF), np.float32)
    for slot, node in enumerate(fine_slots()):
        if node is not None:
            to_slot[slot, (node[0] * 6 + node[1]) * 6 + node[2]] = 1.0
    return to_slot


def call(kernel, outs, scratch=(), smem=(), hbm=(), hbm_outs=False):
    def run(*operands):
        specs = [
            pl.BlockSpec(
                memory_space=pltpu.SMEM if n in smem else pltpu.HBM if n in hbm else pltpu.VMEM
            )
            for n in range(len(operands))
        ]
        operands = [
            pltpu.with_memory_space_constraint(value, pltpu.HBM) if n in hbm else value
            for n, value in enumerate(operands)
        ]
        return pl.pallas_call(
            kernel,
            out_shape=tuple(jax.ShapeDtypeStruct(s, d) for s, d in outs),
            in_specs=specs,
            out_specs=tuple(
                pl.BlockSpec(memory_space=pltpu.HBM if hbm_outs else pltpu.VMEM) for _ in outs
            ),
            scratch_shapes=list(scratch),
            compiler_params=pltpu.CompilerParams(vmem_limit_bytes=20 * 1024 * 1024),
        )(*operands)

    return run


def dot(a, b):
    return lax.dot_general(a, b, (((1,), (0,)), ((), ())), preferred_element_type=F32)


def dot_nt(a, b):
    return lax.dot_general(a, b, (((1,), (1,)), ((), ())), preferred_element_type=F32)


def halves(values):
    high = values.astype(BF16)
    return high, (values - high.astype(F32)).astype(BF16)


def lane_roll(values, shift):
    return jnp.concatenate(
        [
            pltpu.roll(values[:, c * 128 : (c + 1) * 128], shift % 128, 1)
            for c in range(values.shape[1] // 128)
        ],
        axis=1,
    )


def sub_roll(values, shift):
    return pltpu.roll(values, shift % values.shape[0], 0)


def sublane(shape):
    return lax.broadcasted_iota(jnp.int32, shape, 0)


def y_from_lower(values):
    parts, edge = [], jnp.zeros((values.shape[0], 128), F32)
    for x in range(4):
        parts += [edge, values[:, x * 512 : x * 512 + 384]]
    return jnp.concatenate(parts, axis=1)


def y_from_upper(values):
    parts, edge = [], jnp.zeros((values.shape[0], 128), F32)
    for x in range(4):
        parts += [values[:, x * 512 + 128 : x * 512 + 512], edge]
    return jnp.concatenate(parts, axis=1)


def y_column(values, y):
    return jnp.concatenate(
        [values[:, x * 512 + y * 128 : x * 512 + y * 128 + 128] for x in range(4)], axis=1
    )


def even(idx_ref, axis):
    return idx_ref[axis] % 2 == 0


def grid(rows, columns):
    return tuple(lax.broadcasted_iota(jnp.int32, (rows, columns), n) for n in range(2))


def one_hot(n):
    row, col = grid(n, n)
    return jnp.where(row == col, 1.0, 0.0).astype(BF16)


def wide(out, rows, high, low):
    gap = jnp.zeros((rows, 16), BF16)
    out[:, 0:256] = jnp.concatenate([high, gap], axis=1)
    out[:, 256:512] = jnp.concatenate([high, gap], axis=1)
    out[:, 512:768] = jnp.concatenate([low, gap], axis=1)


def narrow(out, high, low):
    row, col = grid(64, 128)
    twice = jnp.where((row == col) | (row == col - 64), 1.0, 0.0).astype(BF16)
    once = jnp.where(row == col, 1.0, 0.0).astype(BF16)
    out[:, 0:128] = dot(high, twice).astype(BF16)
    out[:, 128:256] = dot(low, once).astype(BF16)


def turned(left, part):
    return dot_nt(left, part).astype(BF16)


def prepare(slot, fine, mid, pmid_t, plow_t, kf, pmt, km, plt):
    wide(kf, SF, *[turned(turned(slot, part), slot) for part in halves(fine)])
    wide(pmt, QM, *[turned(part, slot) for part in halves(pmid_t)])
    turn = one_hot(QM)
    narrow(km, *[turned(turn, part) for part in halves(mid)])
    gap = jnp.zeros((8, QM), BF16)
    narrow(plt, *[jnp.concatenate([part, gap], axis=0) for part in halves(plow_t)])


def late_kernel(slot, noise, pmid_t, plow_t, nf, pm, spread):
    turn = one_hot(QF)
    wide(nf, QF, *[turned(turned(turn, part), slot[...]) for part in halves(noise[...])])
    narrow(pm, *[turned(slot[...], part) for part in halves(pmid_t[...])])
    turn = one_hot(QM)
    values = plow_t[...]
    high, low = halves(values)
    rest = (values - high.astype(F32) - low.astype(F32)).astype(BF16)
    columns = dot_nt(turn, high) + dot_nt(turn, low) + dot_nt(turn, rest)
    for d in range(QC):
        spread[d] = jnp.broadcast_to(columns[:, d : d + 1], (QM, 128))


def split_fine(values, x_ref, lanes):
    high, low = halves(values)
    x_ref[0:SF, lanes] = high
    x_ref[256 : 256 + SF, lanes] = low


def clear_fine(x_ref):
    x_ref[SF:256, :] = jnp.zeros((256 - SF, LANES), BF16)
    x_ref[256 + SF : 512, :] = jnp.zeros((256 - SF, LANES), BF16)


def split_product(w_ref, values):
    high, low = halves(values)
    w = w_ref[:, 0:SF]
    return dot(w, high) + dot(w, low) + dot(w_ref[:, 512 : 512 + SF], high)


def fine_product(w_ref, x_ref, lanes):
    return dot(w_ref[:, 0:512], x_ref[:, lanes]) + dot(w_ref[:, 512:768], x_ref[0:256, lanes])


def mid_product(w_ref, values, x_ref):
    high, low = halves(values)
    x_ref[0:64, :] = high
    x_ref[64:128, :] = low
    x_ref[128:192, :] = high
    x_ref[192:256, :] = jnp.zeros((64, LANES), BF16)
    return dot(w_ref[...], x_ref[...])


def chunk(n):
    return slice(n * 512, n * 512 + 512)


def fine_sends(u_ref, idx, s1, s2, s3, s4):
    x_even, y_even = even(idx, 0), even(idx, 1)
    upper, lower = u_ref[200:240, 1536:2048], u_ref[0:40, 0:512]
    s1[0:40, :] = jnp.where(x_even, upper, lower)
    s2[0:40, :] = jnp.where(x_even, lower, upper)
    for i in range(6):
        upper = y_column(u_ref[40 * i + 8 : 40 * i + 16, :], 3)
        lower = y_column(u_ref[40 * i : 40 * i + 8, :], 0)
        s3[8 * i : 8 * i + 8, :] = jnp.where(y_even, upper, lower)
        s4[8 * i : 8 * i + 8, :] = jnp.where(y_even, lower, upper)


def fine_local_kernel(u_ref, g_ref, csr, kf, t_ref, x_ref):
    clear_fine(x_ref)
    for n in range(4):
        u = u_ref[:, chunk(n)]
        split_fine(u, x_ref, chunk(n))
        t_ref[:, chunk(n)] = g_ref[:, chunk(n)] - 4.0 * u - fine_product(kf, x_ref, chunk(n))
    t_ref[0:40, 512:2048] += csr[0:1, 512:2048] * u_ref[200:240, 0:1536]
    t_ref[200:240, 0:1536] += csr[1:2, 0:1536] * u_ref[0:40, 512:2048]
    row = sublane((8, LANES))
    for i in range(6):
        base = 40 * i
        first, last, sides = (u_ref[base + 8 * n : base + 8 * n + 8, :] for n in range(3))
        t0 = csr[2:3, :] * y_from_lower(last)
        t1 = csr[3:4, :] * y_from_upper(first)
        for n, tile, extra in ((0, first, t0), (1, last, t1)):
            lower = csr[4:5, :] * sub_roll(lane_roll(tile, 1), 3)
            upper = csr[5:6, :] * sub_roll(lane_roll(tile, -1), 5)
            t_ref[base + 8 * n : base + 8 * n + 8, :] += (
                extra + jnp.where(row == 0, lower, 0.0) + jnp.where(row == 5, upper, 0.0)
            )
        lower = csr[4:5, :] * sub_roll(lane_roll(sides, 1), 4)
        upper = csr[5:6, :] * sub_roll(lane_roll(sides, -1), 4)
        t_ref[base + 16 : base + 24, :] += jnp.where(row < 4, lower, upper)


def fine_edges(n, t_in, csr, idx, r1, r2, r3, r4):
    x_even, y_even = even(idx, 0), even(idx, 1)
    columns = []
    for y in range(4):
        lanes = slice(n * 512 + y * 128, n * 512 + y * 128 + 128)
        side, edge = slice(y * 128, y * 128 + 128), slice(n * 128, n * 128 + 128)
        tiles = []
        for r in range(SF // 8):
            tile = t_in[8 * r : 8 * r + 8, lanes]
            if n == 0 and r < 5:
                rows = slice(8 * r, 8 * r + 8)
                tile = tile + csr[0:1, lanes] * jnp.where(x_even, r2[rows, side], r1[rows, side])
            if n == 3 and r >= 25:
                rows = slice(8 * r - 200, 8 * r - 192)
                tile = tile + csr[1:2, lanes] * jnp.where(x_even, r1[rows, side], r2[rows, side])
            rows = slice(r // 5 * 8, r // 5 * 8 + 8)
            if y == 0 and r % 5 == 0:
                tile = tile + csr[2:3, lanes] * jnp.where(y_even, r4[rows, edge], r3[rows, edge])
            if y == 3 and r % 5 == 1:
                tile = tile + csr[3:4, lanes] * jnp.where(y_even, r3[rows, edge], r4[rows, edge])
            tiles.append(tile)
        columns.append(jnp.concatenate(tiles, axis=0))
    return jnp.concatenate(columns, axis=1)


def fine_update(u_ref, t_in, csr, idx, received, out_ref, sf):
    for n in range(4):
        t = fine_edges(n, t_in, csr, idx, *received)
        out_ref[:, chunk(n)] = u_ref[:, chunk(n)] + split_product(sf, t)


def first_kernel(
    seed_in, scale_in, coef_in, slot_in, smooth_in, fine_in, mid_in, pmid_in, plow_in, idx,
    g, u1, csx, csr, s1, s2, s3, s4, kf, sf, pmt, km, plt,
    seed, scale, coef, slot, smooth, fine, mid, pmid, plow, done,
):
    copies = {}
    for n, (name, source, target) in enumerate(
        (
            ("scale", scale_in, scale),
            ("coef", coef_in, coef),
            ("slot", slot_in, slot),
            ("smooth", smooth_in, smooth),
            ("fine", fine_in, fine),
            ("pmid", pmid_in, pmid),
            ("plow", plow_in, plow),
            ("mid", mid_in, mid),
            ("seed", seed_in, seed),
        )
    ):
        copies[name] = pltpu.make_async_copy(source, target, done.at[n])
        copies[name].start()
    csr[6:8, :] = jnp.zeros((2, LANES), F32)
    csx[...] = jnp.zeros((16, 512), F32)
    copies["scale"].wait()
    copies["coef"].wait()
    over = 1.0 / scale[...]
    lane = lax.broadcasted_iota(jnp.int32, (COLS, 128), 1)
    column = lax.broadcasted_iota(jnp.int32, (COLS, 128), 0)
    for d in range(3):
        value = coef[16 * d : 16 * d + 16, :] * over
        low, high = 0.9 * value, 0.3 * value
        if d == 0:
            low = jnp.where((column < 4) & (idx[0] == 0), 0.0, low)
            high = jnp.where((column >= 12) & (idx[0] == idx[2] - 1), 0.0, high)
        if d == 1:
            low = jnp.where((column % 4 == 0) & (idx[1] == 0), 0.0, low)
            high = jnp.where((column % 4 == 3) & (idx[1] == idx[3] - 1), 0.0, high)
        if d == 2:
            low = jnp.where(lane == 0, 0.0, low)
            high = jnp.where(lane == 127, 0.0, high)
        for c in range(COLS):
            x, y = c // 4, c % 4
            lanes = slice(c * 128, c * 128 + 128)
            csx[4 * x + d : 4 * x + d + 1, y * 128 : y * 128 + 128] = value[c : c + 1, :]
            csr[2 * d : 2 * d + 1, lanes] = low[c : c + 1, :]
            csr[2 * d + 1 : 2 * d + 2, lanes] = high[c : c + 1, :]
    x_even = even(idx, 0)
    far, near = csx[4:16, :], csx[0:12, :]
    gap = jnp.zeros((4, 512), F32)
    s1[40:56, :] = jnp.concatenate([jnp.where(x_even, far, near), gap], axis=0)
    s2[40:56, :] = jnp.concatenate([jnp.where(x_even, near, far), gap], axis=0)
    for name in ("slot", "smooth", "fine", "pmid", "plow", "mid"):
        copies[name].wait()
    row, col = grid(QF, QF)
    first = [
        turned(slot[...], part)
        for part in halves(smooth[...] + jnp.where(row == col, 0.25, 0.0))
    ]
    wide(sf, SF, *[turned(part, slot[...]) for part in first])
    prepare(slot[...], fine[...], mid[...], pmid[...], plow[...], kf, pmt, km, plt)
    copies["seed"].wait()
    both = jnp.concatenate([first[0], slot[...]], axis=0)
    for n in range(4):
        values = jnp.concatenate(
            [
                seed[pl.ds(c, QF, stride=COLS), :] * over[c : c + 1, :]
                for c in range(4 * n, 4 * n + 4)
            ],
            axis=1,
        )
        high, low = halves(values)
        result = dot(both, high) + dot(both, low)
        g[:, chunk(n)] = result[SF:, :]
        u1[:, chunk(n)] = result[:SF, :] + dot(first[1], high)
    fine_sends(u1, idx, s1, s2, s3, s4)


def spread_kernel(u, t_in, csr, idx, r1, r2, r3, r4, sf, csx, out, s1, s2, s3, s4):
    fine_update(u, t_in, csr, idx, (r1, r2, r3, r4), out, sf)
    fine_sends(out, idx, s1, s2, s3, s4)
    x_even, y_even = even(idx, 0), even(idx, 1)
    left = jnp.where(x_even, r2[40:56, :], r1[40:56, :])
    right = jnp.where(x_even, r1[40:56, :], r2[40:56, :])
    planes = jnp.concatenate([left[0:12], csx[...], right[0:12]], axis=0)
    gap = jnp.zeros((40, 128), F32)
    far, near = planes[:, 128:512], planes[:, 0:384]
    s3[48:88, :] = jnp.concatenate([jnp.where(y_even, far, near), gap], axis=1)
    s4[48:88, :] = jnp.concatenate([jnp.where(y_even, near, far), gap], axis=1)


def coefficient_kernel(idx, csx, r1, r2, r3, r4, coef):
    x_even, y_even = even(idx, 0), even(idx, 1)
    left = jnp.where(x_even, r2[40:56, :], r1[40:56, :])
    right = jnp.where(x_even, r1[40:56, :], r2[40:56, :])
    planes = jnp.concatenate([left[0:12], csx[...], right[0:12]], axis=0)
    below = jnp.where(y_even, r4[48:88, :], r3[48:88, :])
    above = jnp.where(y_even, r3[48:88, :], r4[48:88, :])
    first_x, last_x = idx[0] == 0, idx[0] == idx[2] - 1
    first_y, last_y = idx[1] == 0, idx[1] == idx[3] - 1
    lane = lax.broadcasted_iota(jnp.int32, (1, 128), 1)
    coef[...] = jnp.zeros((6, WROWS, 128), F32)
    for plane in range(WX):
        for y in range(-3, 7):
            source, at = (below, y + 3) if y < 0 else (planes, y) if y < 4 else (above, y - 4)
            row = slice(plane * 16 + 4 + y, plane * 16 + 5 + y)
            for d in range(3):
                value = source[4 * plane + d : 4 * plane + d + 1, at * 128 : at * 128 + 128]
                low, high = 0.9 * value, 0.3 * value
                if d == 0 and plane == 3:
                    low = jnp.where(first_x, 0.0, low)
                if d == 0 and plane == 6:
                    high = jnp.where(last_x, 0.0, high)
                if d == 1 and y == 0:
                    low = jnp.where(first_y, 0.0, low)
                if d == 1 and y == 3:
                    high = jnp.where(last_y, 0.0, high)
                if d == 2:
                    low = jnp.where(lane == 0, 0.0, low)
                    high = jnp.where(lane == 127, 0.0, high)
                coef[2 * d, row, :] = low
                coef[2 * d + 1, row, :] = high


def sweep_kernel(u, t_in, csr, idx, r1, r2, r3, r4, sf, out, s1, s2, s3, s4):
    fine_update(u, t_in, csr, idx, (r1, r2, r3, r4), out, sf)
    fine_sends(out, idx, s1, s2, s3, s4)


def restrict_kernel(t_in, csr, idx, r1, r2, r3, r4, pmt, gm, m1, s1, s2, s3, s4):
    for n in range(4):
        value = split_product(pmt, fine_edges(n, t_in, csr, idx, r1, r2, r3, r4))
        gm[:, chunk(n)] = value
        m1[:, chunk(n)] = 0.2 * value
    mid_sends(m1, idx, s1, s2, s3, s4)


def last_kernel(
    u, t_in, csr, idx, r1, r2, r3, r4, sf, nf, from_slot, inc, out, prev,
    u_ref, natural, out_rows, prev_rows, done,
):
    fine_update(u, t_in, csr, idx, (r1, r2, r3, r4), u_ref, sf)
    slot = from_slot[...]
    for n in range(4):
        high, low = halves(u_ref[:, chunk(n)])
        natural[:, chunk(n)] = dot(slot, high) + dot(slot, low)
        for c in range(4 * n, 4 * n + 4):
            out_rows[pl.ds(c, QF, stride=COLS), :] = natural[:, c * 128 : c * 128 + 128]
    first = pltpu.make_async_copy(out_rows, out, done.at[0])
    first.start()
    for n in range(4):
        noise = split_product(nf, u_ref[:, chunk(n)])
        for y in range(4):
            c = 4 * n + y
            prev_rows[pl.ds(c, QF, stride=COLS), :] = (
                natural[:, c * 128 : c * 128 + 128]
                + inc[c : c + 1, :] * noise[:, y * 128 : y * 128 + 128]
            )
    second = pltpu.make_async_copy(prev_rows, prev, done.at[1])
    second.start()
    first.wait()
    second.wait()


def mid_sends(m_ref, idx, s1, s2, s3, s4):
    x_even, y_even = even(idx, 0), even(idx, 1)
    upper, lower = m_ref[48:64, 1536:2048], m_ref[0:16, 0:512]
    s1[...] = jnp.where(x_even, upper, lower)
    s2[...] = jnp.where(x_even, lower, upper)
    for i in range(4):
        upper = y_column(m_ref[16 * i + 8 : 16 * i + 16, :], 3)
        lower = y_column(m_ref[16 * i : 16 * i + 8, :], 0)
        s3[8 * i : 8 * i + 8, :] = jnp.where(y_even, upper, lower)
        s4[8 * i : 8 * i + 8, :] = jnp.where(y_even, lower, upper)


def mid_edges(idx, r1, r2, r3, r4):
    x_even, y_even = even(idx, 0), even(idx, 1)
    return (
        jnp.where(x_even, r2[...], r1[...]),
        jnp.where(x_even, r1[...], r2[...]),
        jnp.where(y_even, r4[...], r3[...]),
        jnp.where(y_even, r3[...], r4[...]),
    )


def mid_local(m_ref, g_ref, csr, km, t_ref, x_ref):
    m = m_ref[...]
    t_ref[...] = g_ref[...] - 4.0 * m - mid_product(km, m, x_ref)
    t_ref[0:16, 512:2048] += csr[0:1, 512:2048] * m_ref[48:64, 0:1536]
    t_ref[48:64, 0:1536] += csr[1:2, 0:1536] * m_ref[0:16, 512:2048]
    row = sublane((8, LANES))
    for i in range(4):
        base = 16 * i
        first, last = m_ref[base : base + 8, :], m_ref[base + 8 : base + 16, :]
        extra0 = csr[2:3, :] * sub_roll(y_from_lower(last), 4)
        extra1 = csr[3:4, :] * sub_roll(y_from_upper(first), 4)
        for n, tile, extra in (
            (0, first, jnp.where(row < 4, extra0, 0.0)),
            (1, last, jnp.where(row >= 4, extra1, 0.0)),
        ):
            lower = csr[4:5, :] * sub_roll(lane_roll(tile, 1), 5)
            upper = csr[5:6, :] * sub_roll(lane_roll(tile, -1), 3)
            t_ref[base + 8 * n : base + 8 * n + 8, :] += (
                extra + jnp.where(row % 4 == 0, lower, 0.0) + jnp.where(row % 4 == 3, upper, 0.0)
            )


def mid_edge_terms(csr, edges, t_ref):
    below_x, above_x, below_y, above_y = edges
    t_ref[0:16, 0:512] += csr[0:1, 0:512] * below_x
    t_ref[48:64, 1536:2048] += csr[1:2, 1536:2048] * above_x
    row = sublane((8, 128))
    for i in range(4):
        rows = slice(8 * i, 8 * i + 8)
        for x in range(4):
            edge = slice(x * 128, x * 128 + 128)
            first, last = (slice(x * 512 + y * 128, x * 512 + y * 128 + 128) for y in (0, 3))
            below = csr[2:3, first] * sub_roll(below_y[rows, edge], 4)
            above = csr[3:4, last] * sub_roll(above_y[rows, edge], 4)
            t_ref[16 * i : 16 * i + 8, first] += jnp.where(row < 4, below, 0.0)
            t_ref[16 * i + 8 : 16 * i + 16, last] += jnp.where(row >= 4, above, 0.0)


def mid_local_kernel(m_ref, g_ref, csr, km, t_ref, x_ref):
    mid_local(m_ref, g_ref, csr, km, t_ref, x_ref)


def mid_kernel(m, t_in, csr, idx, r1, r2, r3, r4, out, s1, s2, s3, s4, t_ref):
    t_ref[...] = t_in[...]
    mid_edge_terms(csr, mid_edges(idx, r1, r2, r3, r4), t_ref)
    out[...] = m[...] + 0.2 * t_ref[...]
    mid_sends(out, idx, s1, s2, s3, s4)


def block_sends(pay, idx, s1, s2):
    x_even = even(idx, 0)
    far, near = pay[32:128, :], pay[0:96, :]
    s1[...] = jnp.where(x_even, far, near)
    s2[...] = jnp.where(x_even, near, far)


def row_kernel(idx, own, r1, r2, s3, s4):
    x_even, y_even = even(idx, 0), even(idx, 1)
    for plane in range(WX):
        tiles = []
        for y in range(4):
            if 3 <= plane < 7:
                at = QC * (4 * (plane - 3) + y)
                tiles.append(own[at : at + QC, :])
            else:
                at = QC * (4 * (plane % 7) + y)
                one, two = r1[at : at + QC, :], r2[at : at + QC, :]
                tiles.append(jnp.where(x_even == (plane < 3), two, one))
        for y in range(3):
            rows = slice(QC * (3 * plane + y), QC * (3 * plane + y) + QC)
            s3[rows, :] = jnp.where(y_even, tiles[y + 1], tiles[y])
            s4[rows, :] = jnp.where(y_even, tiles[y], tiles[y + 1])


def low_kernel(t_in, csr, idx, r1, r2, r3, r4, plt, pay, s1, s2, x_ref, t_ref):
    t_ref[...] = t_in[...]
    mid_edge_terms(csr, mid_edges(idx, r1, r2, r3, r4), t_ref)
    value = mid_product(plt, t_ref[...], x_ref)
    for c in range(COLS):
        pay[QC * c : QC * c + QC, :] = value[0:8, c * 128 : c * 128 + 128]
    block_sends(pay, idx, s1, s2)


def lift_kernel(m, t_in, csr, idx, r1, r2, r3, r4, pm, u, out, s1, s2, s3, s4, x_ref, t_ref):
    t_ref[...] = t_in[...]
    mid_edge_terms(csr, mid_edges(idx, r1, r2, r3, r4), t_ref)
    high, low = halves(m[...] + 0.2 * t_ref[...])
    x_ref[0:64, :] = high
    x_ref[64:128, :] = low
    x_ref[128:192, :] = high
    x_ref[192:256, :] = jnp.zeros((64, LANES), BF16)
    for n in range(4):
        out[:, chunk(n)] = u[:, chunk(n)] + dot(pm[...], x_ref[:, chunk(n)])
    fine_sends(out, idx, s1, s2, s3, s4)


WX = 10
WROWS = WX * 16


def place(window, own, r1, r2, r3, r4, idx):
    x_even, y_even = even(idx, 0), even(idx, 1)
    window[...] = jnp.zeros((QC * WROWS, 128), F32)

    def put(plane, y, tile):
        window[pl.ds(plane * 16 + 4 + y, QC, stride=WROWS), :] = tile

    for y in range(4):
        for x in range(4):
            c = 4 * x + y
            put(3 + x, y, own[QC * c : QC * c + QC, :])
        for x in range(3):
            rows = slice(QC * (4 * x + y), QC * (4 * x + y) + QC)
            put(x, y, jnp.where(x_even, r2[rows, :], r1[rows, :]))
            put(7 + x, y, jnp.where(x_even, r1[rows, :], r2[rows, :]))
    for plane in range(WX):
        for y in range(3):
            rows = slice(QC * (3 * plane + y), QC * (3 * plane + y) + QC)
            put(plane, y - 3, jnp.where(y_even, r4[rows, :], r3[rows, :]))
            put(plane, y + 4, jnp.where(y_even, r3[rows, :], r4[rows, :]))


def coarse_sweep(c_ref, out_ref, g_ref, coef, kc, first, last):
    def rows(d, plane):
        return pl.ds(d * WROWS + plane * 16, 16)

    def step(plane):
        c = [c_ref[rows(d, plane), :] for d in range(QC)]
        weights = [coef[n, pl.ds(plane * 16, 16), :] for n in range(6)]
        for d in range(QC):
            t = g_ref[rows(d, plane), :] - 4.0 * c[d]
            for j in range(QC):
                t = t - kc[j, d] * c[j]
            if d & 4:
                t = t + weights[1] * c_ref[rows(d - 4, plane + 1), :]
            else:
                t = t + weights[0] * c_ref[rows(d + 4, plane - 1), :]
            if d & 2:
                t = t + weights[3] * sub_roll(c[d - 2], -1)
            else:
                t = t + weights[2] * sub_roll(c[d + 2], 1)
            if d & 1:
                t = t + weights[5] * pltpu.roll(c[d - 1], 127, 1)
            else:
                t = t + weights[4] * pltpu.roll(c[d + 1], 1, 1)
            out_ref[rows(d, plane), :] = c[d] + 0.2 * t

    for plane in range(first, last):
        step(plane)


def coarse_kernel(own, r1, r2, r3, r4, kc, idx, coef, g, pay, s1, s2, one, two):
    place(g, own, r1, r2, r3, r4, idx)
    one[...] = 0.2 * g[...]
    coarse_sweep(one, two, g, coef, kc, 1, 9)
    coarse_sweep(two, one, g, coef, kc, 2, 8)
    coarse_sweep(one, two, g, coef, kc, 3, 7)
    for c in range(COLS):
        row = (3 + c // 4) * 16 + 4 + c % 4
        pay[QC * c : QC * c + QC, :] = two[pl.ds(row, QC, stride=WROWS), :]
    block_sends(pay, idx, s1, s2)


def correct_kernel(
    own, r1, r2, r3, r4, kc, idx, g, coef, spread, m, gm, csr, q1, q2, q3, q4, km,
    out, s1, s2, s3, s4, one, two, x_ref, t_ref, m_ref,
):
    place(one, own, r1, r2, r3, r4, idx)
    coarse_sweep(one, two, g, coef, kc, 1, 9)
    coarse_sweep(two, one, g, coef, kc, 2, 8)

    def lifted(x, y, rows):
        total = None
        for d in range(QC):
            row = d * WROWS + (3 + x) * 16 + 4 + y
            part = spread[d, rows, :] * one[row : row + 1, :]
            total = part if total is None else total + part
        return total

    whole = slice(0, QM)
    for c in range(COLS):
        lanes = slice(c * 128, c * 128 + 128)
        m_ref[:, lanes] = m[:, lanes] + lifted(c // 4, c % 4, whole)
    below_x, above_x, below_y, above_y = mid_edges(idx, q1, q2, q3, q4)
    below_x = below_x + jnp.concatenate([lifted(-1, y, slice(48, 64)) for y in range(4)], axis=1)
    above_x = above_x + jnp.concatenate([lifted(4, y, slice(0, 16)) for y in range(4)], axis=1)
    below_rows, above_rows = [], []
    for i in range(4):
        last, first = slice(16 * i + 8, 16 * i + 16), slice(16 * i, 16 * i + 8)
        below_rows.append(jnp.concatenate([lifted(x, -1, last) for x in range(4)], axis=1))
        above_rows.append(jnp.concatenate([lifted(x, 4, first) for x in range(4)], axis=1))
    below_y = below_y + jnp.concatenate(below_rows, axis=0)
    above_y = above_y + jnp.concatenate(above_rows, axis=0)
    mid_local(m_ref, gm, csr, km, t_ref, x_ref)
    mid_edge_terms(csr, (below_x, above_x, below_y, above_y), t_ref)
    out[...] = m_ref[...] + 0.2 * t_ref[...]
    mid_sends(out, idx, s1, s2, s3, s4)


def partners(step):
    nx, ny = lax.axis_size("gx"), lax.axis_size("yz")
    pairs = []
    for a in range(nx):
        for b in range(ny):
            to = (a, b)
            if step < 2:
                at = ((a + step) ^ 1) - step
                to = (at, b) if 0 <= at < nx else (a, b ^ 1)
            else:
                at = ((b + step - 2) ^ 1) - (step - 2)
                to = (a, at) if 0 <= at < ny else (a ^ 1, b)
            pairs.append((a * ny + b, to[0] * ny + to[1]))
    return pairs


def swap(values, step):
    return lax.ppermute(values, ("gx", "yz"), partners(step))


def exchange(sends):
    s1, s2, s3, s4 = sends
    r2, r1, r4, r3 = swap(s2, 1), swap(s1, 0), swap(s4, 3), swap(s3, 2)
    return r1, r2, r3, r4


def exchange_blocks(idx, own, s1, s2):
    r2, r1 = swap(s2, 1), swap(s1, 0)
    s3, s4 = call(row_kernel, [((QC * 3 * WX, 128), F32)] * 2, (), (0,))(idx, own, r1, r2)
    r4, r3 = swap(s4, 3), swap(s3, 2)
    return own, r1, r2, r3, r4


def body(seed, scale, coef, fine, smooth, mid, coarse, pmid, plow, noise, inc):
    idx = jnp.stack(
        [
            lax.axis_index("gx"),
            lax.axis_index("yz"),
            jnp.int32(lax.axis_size("gx")),
            jnp.int32(lax.axis_size("yz")),
        ]
    ).astype(jnp.int32)
    slots = slot_matrix()
    to_slot, from_slot = jnp.asarray(slots, BF16), jnp.asarray(slots.T, BF16)

    fine_field = ((SF, LANES), F32)
    fine_faces = [((40, 512), F32)] * 2 + [((48, 512), F32)] * 2
    mid_field = ((QM, LANES), F32)
    mid_faces = [((16, 512), F32)] * 2 + [((32, 512), F32)] * 2
    xf = pltpu.VMEM((512, LANES), BF16)
    xm, tm = pltpu.VMEM((256, LANES), BF16), pltpu.VMEM((QM, LANES), F32)
    window = ((QC * WROWS, 128), F32)
    windows = [pltpu.VMEM((QC * WROWS, 128), F32)] * 2
    blocks = [((QC * COLS, 128), F32)] + [((QC * 12, 128), F32)] * 2

    operands = (
        seed.reshape(QF * COLS, 128),
        scale.reshape(COLS, 128),
        coef.reshape(3 * COLS, 128),
        to_slot,
        smooth,
        fine,
        mid,
        pmid.T,
        plow.T,
    )
    g, u, csx, csr, s1, s2, s3, s4, kf, sf, pmt, km, plt = call(
        first_kernel,
        [fine_field, fine_field, ((16, 512), F32), ((8, LANES), F32)]
        + [((56, 512), F32)] * 2
        + [((48, 512), F32)] * 2
        + [
            ((SF, 768), BF16),
            ((SF, 768), BF16),
            ((QM, 768), BF16),
            ((QM, 256), BF16),
            ((16, 256), BF16),
        ],
        [pltpu.VMEM(operand.shape, operand.dtype) for operand in operands]
        + [pltpu.SemaphoreType.DMA((len(operands),))],
        (9,),
        range(9),
    )(*operands, idx)
    nf, pm, spread = call(
        late_kernel, [((QF, 768), BF16), ((SF, 256), BF16), ((QC, QM, 128), F32)]
    )(to_slot, noise, pmid.T, plow.T)

    def fine_local(u):
        (t,) = call(fine_local_kernel, [fine_field], [xf])(u, g, csr, kf)
        return t

    def mid_local_part(m):
        (t,) = call(mid_local_kernel, [mid_field], [xm])(m, gm, csr, km)
        return t

    first = exchange((s1, s2, s3, s4))
    u, *sends = call(
        spread_kernel,
        [fine_field] + fine_faces[:2] + [((88, 512), F32)] * 2,
        (),
        (3,),
    )(u, fine_local(u), csr, idx, *first, sf, csx)
    edges = exchange(sends)
    (coefw,) = call(coefficient_kernel, [((6, WROWS, 128), F32)], (), (0,))(
        idx, csx, first[0], first[1], edges[2], edges[3]
    )
    gm, m, *sends = call(restrict_kernel, [mid_field, mid_field] + mid_faces, (), (2,))(
        fine_local(u), csr, idx, *edges, pmt
    )
    edges = exchange(sends)
    m, *sends = call(mid_kernel, [mid_field] + mid_faces, [tm], (3,))(
        m, mid_local_part(m), csr, idx, *edges
    )
    edges = exchange(sends)
    pay = call(low_kernel, blocks, [xm, tm], (2,))(mid_local_part(m), csr, idx, *edges, plt)
    gw, *pay = call(coarse_kernel, [window] + blocks, windows, (5, 6))(
        *exchange_blocks(idx, *pay), coarse, idx, coefw
    )
    m, *sends = call(
        correct_kernel,
        [mid_field] + mid_faces,
        windows + [xm, tm, pltpu.VMEM((QM, LANES), F32)],
        (5, 6),
    )(*exchange_blocks(idx, *pay), coarse, idx, gw, coefw, spread, m, gm, csr, *edges, km)
    edges = exchange(sends)
    u, *sends = call(lift_kernel, [fine_field] + fine_faces, [xm, tm], (3,))(
        m, mid_local_part(m), csr, idx, *edges, pm, u
    )
    edges = exchange(sends)
    u, *sends = call(sweep_kernel, [fine_field] + fine_faces, (), (3,))(
        u, fine_local(u), csr, idx, *edges, sf
    )
    edges = exchange(sends)
    out, prev = call(
        last_kernel,
        [((QF * COLS, 128), F32)] * 2,
        [
            pltpu.VMEM((SF, LANES), F32),
            pltpu.VMEM((QF, LANES), F32),
            pltpu.VMEM((QF * COLS, 128), F32),
            pltpu.VMEM((QF * COLS, 128), F32),
            pltpu.SemaphoreType.DMA((2,)),
        ],
        (3,),
        hbm_outs=True,
    )(u, fine_local(u), csr, idx, *edges, sf, nf, from_slot, inc.reshape(COLS, 128))
    shape = seed.shape
    return out.reshape(shape), prev.reshape(shape)


def solution(mesh):
    cell, field = P("gx", "yz", None), P(None, "gx", "yz", None)
    return jax.shard_map(
        body,
        mesh=mesh,
        in_specs=(field, cell, field) + (P(),) * 7 + (cell,),
        out_specs=(field, field),
        check_vma=False,
    )
```

```python
import numpy as np
import jax
import jax.numpy as jnp
from jax import lax
from jax.sharding import PartitionSpec as P
from jax.experimental import pallas as pl
from jax.experimental.pallas import tpu as pltpu

NF = 6
QF = 216
SF = 240
QM = 64
QC = 8
COLS = 16
LANES = COLS * 128
F32 = jnp.float32
BF16 = jnp.bfloat16


def fine_slots():
    slots = []
    for i in range(6):
        slots += [(i, 0, k) for k in range(6)] + [None] * 2
        slots += [(i, 5, k) for k in range(6)] + [None] * 2
        slots += [(i, j, 0) for j in range(1, 5)] + [(i, j, 5) for j in range(1, 5)]
        slots += [(i, j, k) for j in range(1, 5) for k in range(1, 5)]
    return slots


def slot_matrix():
    to_slot = np.zeros((SF, QF), np.float32)
    for slot, node in enumerate(fine_slots()):
        if node is not None:
            to_slot[slot, (node[0] * 6 + node[1]) * 6 + node[2]] = 1.0
    return to_slot


def call(kernel, outs, scratch=(), smem=(), hbm=(), hbm_outs=False):
    def run(*operands):
        specs = [
            pl.BlockSpec(
                memory_space=pltpu.SMEM if n in smem else pltpu.HBM if n in hbm else pltpu.VMEM
            )
            for n in range(len(operands))
        ]
        operands = [
            pltpu.with_memory_space_constraint(value, pltpu.HBM) if n in hbm else value
            for n, value in enumerate(operands)
        ]
        return pl.pallas_call(
            kernel,
            out_shape=tuple(jax.ShapeDtypeStruct(s, d) for s, d in outs),
            in_specs=specs,
            out_specs=tuple(
                pl.BlockSpec(memory_space=pltpu.HBM if hbm_outs else pltpu.VMEM) for _ in outs
            ),
            scratch_shapes=list(scratch),
            compiler_params=pltpu.CompilerParams(vmem_limit_bytes=20 * 1024 * 1024),
        )(*operands)

    return run


def dot(a, b):
    return lax.dot_general(a, b, (((1,), (0,)), ((), ())), preferred_element_type=F32)


def dot_nt(a, b):
    return lax.dot_general(a, b, (((1,), (1,)), ((), ())), preferred_element_type=F32)


def halves(values):
    high = values.astype(BF16)
    return high, (values - high.astype(F32)).astype(BF16)


def lane_roll(values, shift):
    return jnp.concatenate(
        [
            pltpu.roll(values[:, c * 128 : (c + 1) * 128], shift % 128, 1)
            for c in range(values.shape[1] // 128)
        ],
        axis=1,
    )


def sub_roll(values, shift):
    return pltpu.roll(values, shift % values.shape[0], 0)


def sublane(shape):
    return lax.broadcasted_iota(jnp.int32, shape, 0)


def y_from_lower(values):
    parts, edge = [], jnp.zeros((values.shape[0], 128), F32)
    for x in range(4):
        parts += [edge, values[:, x * 512 : x * 512 + 384]]
    return jnp.concatenate(parts, axis=1)


def y_from_upper(values):
    parts, edge = [], jnp.zeros((values.shape[0], 128), F32)
    for x in range(4):
        parts += [values[:, x * 512 + 128 : x * 512 + 512], edge]
    return jnp.concatenate(parts, axis=1)


def y_column(values, y):
    return jnp.concatenate(
        [values[:, x * 512 + y * 128 : x * 512 + y * 128 + 128] for x in range(4)], axis=1
    )


def even(idx_ref, axis):
    return idx_ref[axis] % 2 == 0


def grid(rows, columns):
    return tuple(lax.broadcasted_iota(jnp.int32, (rows, columns), n) for n in range(2))


def one_hot(n):
    row, col = grid(n, n)
    return jnp.where(row == col, 1.0, 0.0).astype(BF16)


def wide(out, rows, high, low):
    gap = jnp.zeros((rows, 16), BF16)
    out[:, 0:256] = jnp.concatenate([high, gap], axis=1)
    out[:, 256:512] = jnp.concatenate([high, gap], axis=1)
    out[:, 512:768] = jnp.concatenate([low, gap], axis=1)


def narrow(out, high, low):
    row, col = grid(64, 128)
    twice = jnp.where((row == col) | (row == col - 64), 1.0, 0.0).astype(BF16)
    once = jnp.where(row == col, 1.0, 0.0).astype(BF16)
    out[:, 0:128] = dot(high, twice).astype(BF16)
    out[:, 128:256] = dot(low, once).astype(BF16)


def turned(left, part):
    return dot_nt(left, part).astype(BF16)


def prepare(slot, fine, mid, pmid_t, plow_t, kf, pmt, km, plt, plv):
    wide(kf, SF, *[turned(turned(slot, part), slot) for part in halves(fine)])
    wide(pmt, QM, *[turned(part, slot) for part in halves(pmid_t)])
    turn = one_hot(QM)
    narrow(km, *[turned(turn, part) for part in halves(mid)])
    gap = jnp.zeros((8, QM), BF16)
    narrow(plt, *[jnp.concatenate([part, gap], axis=0) for part in halves(plow_t)])
    row, col = grid(QM, QM)
    moves = (
        col == row + 48,
        col == row - 48,
        (col == row + 12) & (row // 4 % 4 == 0),
        (col == row - 12) & (row // 4 % 4 == 3),
    )
    moves = [jnp.where(move, 1.0, 0.0).astype(BF16) for move in moves]
    narrow(
        plv,
        *[
            jnp.concatenate([dot(part, move).astype(BF16) for move in moves], axis=0)
            for part in halves(plow_t)
        ],
    )


def late_kernel(slot, noise, pmid_t, plow_t, nf, pm, spread):
    turn = one_hot(QF)
    wide(nf, QF, *[turned(turned(turn, part), slot[...]) for part in halves(noise[...])])
    narrow(pm, *[turned(slot[...], part) for part in halves(pmid_t[...])])
    turn = one_hot(QM)
    values = plow_t[...]
    high, low = halves(values)
    rest = (values - high.astype(F32) - low.astype(F32)).astype(BF16)
    columns = dot_nt(turn, high) + dot_nt(turn, low) + dot_nt(turn, rest)
    for d in range(QC):
        spread[d] = jnp.broadcast_to(columns[:, d : d + 1], (QM, 128))


def split_fine(values, x_ref, lanes):
    high, low = halves(values)
    x_ref[0:SF, lanes] = high
    x_ref[256 : 256 + SF, lanes] = low


def clear_fine(x_ref):
    x_ref[SF:256, :] = jnp.zeros((256 - SF, LANES), BF16)
    x_ref[256 + SF : 512, :] = jnp.zeros((256 - SF, LANES), BF16)


def split_product(w_ref, values):
    high, low = halves(values)
    w = w_ref[:, 0:SF]
    return dot(w, high) + dot(w, low) + dot(w_ref[:, 512 : 512 + SF], high)


def fine_product(w_ref, x_ref, lanes):
    return dot(w_ref[:, 0:512], x_ref[:, lanes]) + dot(w_ref[:, 512:768], x_ref[0:256, lanes])


def mid_product(w_ref, values, x_ref):
    high, low = halves(values)
    x_ref[0:64, :] = high
    x_ref[64:128, :] = low
    x_ref[128:192, :] = high
    x_ref[192:256, :] = jnp.zeros((64, LANES), BF16)
    return dot(w_ref[...], x_ref[...])


def chunk(n):
    return slice(n * 512, n * 512 + 512)


def fine_sends(u_ref, idx, s1, s2, s3, s4):
    x_even, y_even = even(idx, 0), even(idx, 1)
    upper, lower = u_ref[200:240, 1536:2048], u_ref[0:40, 0:512]
    s1[0:40, :] = jnp.where(x_even, upper, lower)
    s2[0:40, :] = jnp.where(x_even, lower, upper)
    for i in range(6):
        upper = y_column(u_ref[40 * i + 8 : 40 * i + 16, :], 3)
        lower = y_column(u_ref[40 * i : 40 * i + 8, :], 0)
        s3[8 * i : 8 * i + 8, :] = jnp.where(y_even, upper, lower)
        s4[8 * i : 8 * i + 8, :] = jnp.where(y_even, lower, upper)


def fine_local_kernel(u_ref, g_ref, csr, kf, t_ref, x_ref):
    clear_fine(x_ref)
    for n in range(4):
        u = u_ref[:, chunk(n)]
        split_fine(u, x_ref, chunk(n))
        t_ref[:, chunk(n)] = g_ref[:, chunk(n)] - 4.0 * u - fine_product(kf, x_ref, chunk(n))
    t_ref[0:40, 512:2048] += csr[0:1, 512:2048] * u_ref[200:240, 0:1536]
    t_ref[200:240, 0:1536] += csr[1:2, 0:1536] * u_ref[0:40, 512:2048]
    row = sublane((8, LANES))
    for i in range(6):
        base = 40 * i
        first, last, sides = (u_ref[base + 8 * n : base + 8 * n + 8, :] for n in range(3))
        t0 = csr[2:3, :] * y_from_lower(last)
        t1 = csr[3:4, :] * y_from_upper(first)
        for n, tile, extra in ((0, first, t0), (1, last, t1)):
            lower = csr[4:5, :] * sub_roll(lane_roll(tile, 1), 3)
            upper = csr[5:6, :] * sub_roll(lane_roll(tile, -1), 5)
            t_ref[base + 8 * n : base + 8 * n + 8, :] += (
                extra + jnp.where(row == 0, lower, 0.0) + jnp.where(row == 5, upper, 0.0)
            )
        lower = csr[4:5, :] * sub_roll(lane_roll(sides, 1), 4)
        upper = csr[5:6, :] * sub_roll(lane_roll(sides, -1), 4)
        t_ref[base + 16 : base + 24, :] += jnp.where(row < 4, lower, upper)


def fine_edges(n, t_in, csr, idx, r1, r2, r3, r4):
    x_even, y_even = even(idx, 0), even(idx, 1)
    columns = []
    for y in range(4):
        lanes = slice(n * 512 + y * 128, n * 512 + y * 128 + 128)
        side, edge = slice(y * 128, y * 128 + 128), slice(n * 128, n * 128 + 128)
        tiles = []
        for r in range(SF // 8):
            tile = t_in[8 * r : 8 * r + 8, lanes]
            if n == 0 and r < 5:
                rows = slice(8 * r, 8 * r + 8)
                tile = tile + csr[0:1, lanes] * jnp.where(x_even, r2[rows, side], r1[rows, side])
            if n == 3 and r >= 25:
                rows = slice(8 * r - 200, 8 * r - 192)
                tile = tile + csr[1:2, lanes] * jnp.where(x_even, r1[rows, side], r2[rows, side])
            rows = slice(r // 5 * 8, r // 5 * 8 + 8)
            if y == 0 and r % 5 == 0:
                tile = tile + csr[2:3, lanes] * jnp.where(y_even, r4[rows, edge], r3[rows, edge])
            if y == 3 and r % 5 == 1:
                tile = tile + csr[3:4, lanes] * jnp.where(y_even, r3[rows, edge], r4[rows, edge])
            tiles.append(tile)
        columns.append(jnp.concatenate(tiles, axis=0))
    return jnp.concatenate(columns, axis=1)


def fine_update(u_ref, t_in, csr, idx, received, out_ref, sf):
    for n in range(4):
        t = fine_edges(n, t_in, csr, idx, *received)
        out_ref[:, chunk(n)] = u_ref[:, chunk(n)] + split_product(sf, t)


def first_kernel(
    seed_in, scale_in, coef_in, slot_in, smooth_in, fine_in, mid_in, pmid_in, plow_in, idx,
    g, u1, csx, csr, s1, s2, s3, s4, kf, sf, pmt, km, plt, plv,
    seed, scale, coef, slot, smooth, fine, mid, pmid, plow, done,
):
    copies = {}
    for n, (name, source, target) in enumerate(
        (
            ("scale", scale_in, scale),
            ("coef", coef_in, coef),
            ("slot", slot_in, slot),
            ("smooth", smooth_in, smooth),
            ("fine", fine_in, fine),
            ("pmid", pmid_in, pmid),
            ("plow", plow_in, plow),
            ("mid", mid_in, mid),
            ("seed", seed_in, seed),
        )
    ):
        copies[name] = pltpu.make_async_copy(source, target, done.at[n])
        copies[name].start()
    csr[6:8, :] = jnp.zeros((2, LANES), F32)
    csx[...] = jnp.zeros((16, 512), F32)
    copies["scale"].wait()
    copies["coef"].wait()
    over = 1.0 / scale[...]
    lane = lax.broadcasted_iota(jnp.int32, (COLS, 128), 1)
    column = lax.broadcasted_iota(jnp.int32, (COLS, 128), 0)
    for d in range(3):
        value = coef[16 * d : 16 * d + 16, :] * over
        low, high = 0.9 * value, 0.3 * value
        if d == 0:
            low = jnp.where((column < 4) & (idx[0] == 0), 0.0, low)
            high = jnp.where((column >= 12) & (idx[0] == idx[2] - 1), 0.0, high)
        if d == 1:
            low = jnp.where((column % 4 == 0) & (idx[1] == 0), 0.0, low)
            high = jnp.where((column % 4 == 3) & (idx[1] == idx[3] - 1), 0.0, high)
        if d == 2:
            low = jnp.where(lane == 0, 0.0, low)
            high = jnp.where(lane == 127, 0.0, high)
        for c in range(COLS):
            x, y = c // 4, c % 4
            lanes = slice(c * 128, c * 128 + 128)
            csx[4 * x + d : 4 * x + d + 1, y * 128 : y * 128 + 128] = value[c : c + 1, :]
            csr[2 * d : 2 * d + 1, lanes] = low[c : c + 1, :]
            csr[2 * d + 1 : 2 * d + 2, lanes] = high[c : c + 1, :]
    x_even = even(idx, 0)
    far, near = csx[4:16, :], csx[0:12, :]
    gap = jnp.zeros((4, 512), F32)
    s1[40:56, :] = jnp.concatenate([jnp.where(x_even, far, near), gap], axis=0)
    s2[40:56, :] = jnp.concatenate([jnp.where(x_even, near, far), gap], axis=0)
    for name in ("slot", "smooth", "fine", "pmid", "plow", "mid"):
        copies[name].wait()
    row, col = grid(QF, QF)
    first = [
        turned(slot[...], part)
        for part in halves(smooth[...] + jnp.where(row == col, 0.25, 0.0))
    ]
    wide(sf, SF, *[turned(part, slot[...]) for part in first])
    prepare(slot[...], fine[...], mid[...], pmid[...], plow[...], kf, pmt, km, plt, plv)
    copies["seed"].wait()
    both = jnp.concatenate([first[0], slot[...]], axis=0)
    for n in range(4):
        values = jnp.concatenate(
            [
                seed[pl.ds(c, QF, stride=COLS), :] * over[c : c + 1, :]
                for c in range(4 * n, 4 * n + 4)
            ],
            axis=1,
        )
        high, low = halves(values)
        result = dot(both, high) + dot(both, low)
        g[:, chunk(n)] = result[SF:, :]
        u1[:, chunk(n)] = result[:SF, :] + dot(first[1], high)
    fine_sends(u1, idx, s1, s2, s3, s4)


def spread_kernel(u, t_in, csr, idx, r1, r2, r3, r4, sf, csx, out, s1, s2, s3, s4):
    fine_update(u, t_in, csr, idx, (r1, r2, r3, r4), out, sf)
    fine_sends(out, idx, s1, s2, s3, s4)
    x_even, y_even = even(idx, 0), even(idx, 1)
    left = jnp.where(x_even, r2[40:56, :], r1[40:56, :])
    right = jnp.where(x_even, r1[40:56, :], r2[40:56, :])
    planes = jnp.concatenate([left[0:12], csx[...], right[0:12]], axis=0)
    gap = jnp.zeros((40, 128), F32)
    far, near = planes[:, 128:512], planes[:, 0:384]
    s3[48:88, :] = jnp.concatenate([jnp.where(y_even, far, near), gap], axis=1)
    s4[48:88, :] = jnp.concatenate([jnp.where(y_even, near, far), gap], axis=1)


def coefficient_kernel(idx, csx, r1, r2, r3, r4, coef):
    x_even, y_even = even(idx, 0), even(idx, 1)
    left = jnp.where(x_even, r2[40:56, :], r1[40:56, :])
    right = jnp.where(x_even, r1[40:56, :], r2[40:56, :])
    planes = jnp.concatenate([left[0:12], csx[...], right[0:12]], axis=0)
    below = jnp.where(y_even, r4[48:88, :], r3[48:88, :])
    above = jnp.where(y_even, r3[48:88, :], r4[48:88, :])
    first_x, last_x = idx[0] == 0, idx[0] == idx[2] - 1
    first_y, last_y = idx[1] == 0, idx[1] == idx[3] - 1
    lane = lax.broadcasted_iota(jnp.int32, (1, 128), 1)
    coef[...] = jnp.zeros((6, WROWS, 128), F32)
    for plane in range(WX):
        for y in range(-3, 7):
            source, at = (below, y + 3) if y < 0 else (planes, y) if y < 4 else (above, y - 4)
            row = slice(plane * 16 + 4 + y, plane * 16 + 5 + y)
            for d in range(3):
                value = source[4 * plane + d : 4 * plane + d + 1, at * 128 : at * 128 + 128]
                low, high = 0.9 * value, 0.3 * value
                if d == 0 and plane == 3:
                    low = jnp.where(first_x, 0.0, low)
                if d == 0 and plane == 6:
                    high = jnp.where(last_x, 0.0, high)
                if d == 1 and y == 0:
                    low = jnp.where(first_y, 0.0, low)
                if d == 1 and y == 3:
                    high = jnp.where(last_y, 0.0, high)
                if d == 2:
                    low = jnp.where(lane == 0, 0.0, low)
                    high = jnp.where(lane == 127, 0.0, high)
                coef[2 * d, row, :] = low
                coef[2 * d + 1, row, :] = high


def sweep_kernel(u, t_in, csr, idx, r1, r2, r3, r4, sf, out, s1, s2, s3, s4):
    fine_update(u, t_in, csr, idx, (r1, r2, r3, r4), out, sf)
    fine_sends(out, idx, s1, s2, s3, s4)


def restrict_kernel(t_in, csr, idx, r1, r2, r3, r4, pmt, gm, m1, s1, s2, s3, s4):
    for n in range(4):
        value = split_product(pmt, fine_edges(n, t_in, csr, idx, r1, r2, r3, r4))
        gm[:, chunk(n)] = value
        m1[:, chunk(n)] = 0.2 * value
    mid_sends(m1, idx, s1, s2, s3, s4)


def last_kernel(
    u, t_in, csr, idx, r1, r2, r3, r4, sf, nf, from_slot, inc, out, prev,
    u_ref, natural, out_rows, prev_rows, done,
):
    fine_update(u, t_in, csr, idx, (r1, r2, r3, r4), u_ref, sf)
    slot = from_slot[...]
    for n in range(4):
        high, low = halves(u_ref[:, chunk(n)])
        natural[:, chunk(n)] = dot(slot, high) + dot(slot, low)
        for c in range(4 * n, 4 * n + 4):
            out_rows[pl.ds(c, QF, stride=COLS), :] = natural[:, c * 128 : c * 128 + 128]
    first = pltpu.make_async_copy(out_rows, out, done.at[0])
    first.start()
    for n in range(4):
        noise = split_product(nf, u_ref[:, chunk(n)])
        for y in range(4):
            c = 4 * n + y
            prev_rows[pl.ds(c, QF, stride=COLS), :] = (
                natural[:, c * 128 : c * 128 + 128]
                + inc[c : c + 1, :] * noise[:, y * 128 : y * 128 + 128]
            )
    second = pltpu.make_async_copy(prev_rows, prev, done.at[1])
    second.start()
    first.wait()
    second.wait()


def mid_sends(m_ref, idx, s1, s2, s3, s4):
    x_even, y_even = even(idx, 0), even(idx, 1)
    upper, lower = m_ref[48:64, 1536:2048], m_ref[0:16, 0:512]
    s1[...] = jnp.where(x_even, upper, lower)
    s2[...] = jnp.where(x_even, lower, upper)
    for i in range(4):
        upper = y_column(m_ref[16 * i + 8 : 16 * i + 16, :], 3)
        lower = y_column(m_ref[16 * i : 16 * i + 8, :], 0)
        s3[8 * i : 8 * i + 8, :] = jnp.where(y_even, upper, lower)
        s4[8 * i : 8 * i + 8, :] = jnp.where(y_even, lower, upper)


def mid_edges(idx, r1, r2, r3, r4):
    x_even, y_even = even(idx, 0), even(idx, 1)
    return (
        jnp.where(x_even, r2[...], r1[...]),
        jnp.where(x_even, r1[...], r2[...]),
        jnp.where(y_even, r4[...], r3[...]),
        jnp.where(y_even, r3[...], r4[...]),
    )


def mid_local(m_ref, g_ref, csr, km, t_ref, x_ref):
    m = m_ref[...]
    t_ref[...] = g_ref[...] - 4.0 * m - mid_product(km, m, x_ref)
    t_ref[0:16, 512:2048] += csr[0:1, 512:2048] * m_ref[48:64, 0:1536]
    t_ref[48:64, 0:1536] += csr[1:2, 0:1536] * m_ref[0:16, 512:2048]
    row = sublane((8, LANES))
    for i in range(4):
        base = 16 * i
        first, last = m_ref[base : base + 8, :], m_ref[base + 8 : base + 16, :]
        extra0 = csr[2:3, :] * sub_roll(y_from_lower(last), 4)
        extra1 = csr[3:4, :] * sub_roll(y_from_upper(first), 4)
        for n, tile, extra in (
            (0, first, jnp.where(row < 4, extra0, 0.0)),
            (1, last, jnp.where(row >= 4, extra1, 0.0)),
        ):
            lower = csr[4:5, :] * sub_roll(lane_roll(tile, 1), 5)
            upper = csr[5:6, :] * sub_roll(lane_roll(tile, -1), 3)
            t_ref[base + 8 * n : base + 8 * n + 8, :] += (
                extra + jnp.where(row % 4 == 0, lower, 0.0) + jnp.where(row % 4 == 3, upper, 0.0)
            )


def mid_edge_terms(csr, edges, t_ref):
    below_x, above_x, below_y, above_y = edges
    t_ref[0:16, 0:512] += csr[0:1, 0:512] * below_x
    t_ref[48:64, 1536:2048] += csr[1:2, 1536:2048] * above_x
    row = sublane((8, 128))
    for i in range(4):
        rows = slice(8 * i, 8 * i + 8)
        for x in range(4):
            edge = slice(x * 128, x * 128 + 128)
            first, last = (slice(x * 512 + y * 128, x * 512 + y * 128 + 128) for y in (0, 3))
            below = csr[2:3, first] * sub_roll(below_y[rows, edge], 4)
            above = csr[3:4, last] * sub_roll(above_y[rows, edge], 4)
            t_ref[16 * i : 16 * i + 8, first] += jnp.where(row < 4, below, 0.0)
            t_ref[16 * i + 8 : 16 * i + 16, last] += jnp.where(row >= 4, above, 0.0)


def mid_local_kernel(m_ref, g_ref, csr, km, t_ref, x_ref):
    mid_local(m_ref, g_ref, csr, km, t_ref, x_ref)


def far_near(idx, far, near, s1, s2):
    x_even = even(idx, 0)
    s1[...] = jnp.where(x_even, far, near)
    s2[...] = jnp.where(x_even, near, far)


def smooth_kernel(
    m, t_in, csr, idx, r1, r2, r3, r4, gm, km, plt, plv, out, own, s1, s2, x_ref, t_ref
):
    t_ref[...] = t_in[...]
    mid_edge_terms(csr, mid_edges(idx, r1, r2, r3, r4), t_ref)
    out[...] = m[...] + 0.2 * t_ref[...]
    mid_local(out, gm, csr, km, t_ref, x_ref)
    faces = dot(plv[...], x_ref[...])
    value = mid_product(plt, t_ref[...], x_ref)
    for c in range(COLS):
        own[QC * c : QC * c + QC, :] = value[0:8, c * 128 : c * 128 + 128]
    for n in range(4):
        upper, lower = slice((12 + n) * 128, (13 + n) * 128), slice(n * 128, n * 128 + 128)
        own[128 + 8 * n : 136 + 8 * n, :] = faces[0:8, upper]
        own[160 + 8 * n : 168 + 8 * n, :] = faces[8:16, lower]
        upper = slice((4 * n + 3) * 128, (4 * n + 4) * 128)
        lower = slice(4 * n * 128, (4 * n + 1) * 128)
        own[192 + 8 * n : 200 + 8 * n, :] = faces[16:24, upper]
        own[224 + 8 * n : 232 + 8 * n, :] = faces[24:32, lower]
    far = (own[32:128, :], own[128:160, :], own[200:224, :], own[232:256, :])
    near = (own[0:96, :], own[160:192, :], own[192:216, :], own[224:248, :])
    far_near(idx, jnp.concatenate(far, axis=0), jnp.concatenate(near, axis=0), s1, s2)


WX = 10
WROWS = WX * 16
REACH = [(p, d) for p in range(WX) for d in range(1, 4 - max(0, 3 - p, p - 6))]


def window_row(plane, y):
    return plane * 16 + 4 + y


def tile(ref, n):
    return ref[QC * n : QC * n + QC, :]


def window_tiles(idx, own, r1, r2):
    x_even = even(idx, 0)
    planes = []
    for plane in range(WX):
        if 3 <= plane < 7:
            planes.append([tile(own, 4 * (plane - 3) + y) for y in range(4)])
        else:
            n = 4 * (plane % 7)
            left = plane < 3
            planes.append(
                [
                    jnp.where(x_even == left, tile(r2, n + y), tile(r1, n + y))
                    for y in range(4)
                ]
            )
    return planes


def row_sends(idx, planes, s3, s4):
    y_even = even(idx, 1)
    for n, (p, d) in enumerate(REACH):
        far, near = planes[p][4 - d], planes[p][d - 1]
        s3[QC * n : QC * n + QC, :] = jnp.where(y_even, far, near)
        s4[QC * n : QC * n + QC, :] = jnp.where(y_even, near, far)


def row_kernel(idx, own, r1, r2, coef, s3, s4, whole):
    x_even, y_even = even(idx, 0), even(idx, 1)
    planes = window_tiles(idx, own, r1, r2)

    def left(n):
        return jnp.where(x_even, tile(r2, n), tile(r1, n))

    def right(n):
        return jnp.where(x_even, tile(r1, n), tile(r2, n))

    def weight(n, plane, y):
        row = window_row(plane, y)
        return coef[n, row : row + 1, :]

    for y in range(4):
        planes[3][y] = planes[3][y] + weight(0, 3, y) * left(12 + y)
        planes[6][y] = planes[6][y] + weight(1, 6, y) * right(12 + y)
        planes[2][y] = planes[2][y] + weight(1, 2, y) * tile(own, 20 + y)
        planes[7][y] = planes[7][y] + weight(0, 7, y) * tile(own, 16 + y)
    row_sends(idx, planes, s3, s4)
    for p in range(WX):
        for y in range(4):
            n = 4 * p + y
            whole[QC * n : QC * n + QC, :] = planes[p][y]
        if p < 3:
            upper, lower = left(16 + p), left(19 + p)
        elif p < 7:
            upper, lower = tile(own, 24 + p - 3), tile(own, 28 + p - 3)
        else:
            upper, lower = right(16 + p - 7), right(19 + p - 7)
        whole[320 + QC * p : 328 + QC * p, :] = upper
        whole[400 + QC * p : 408 + QC * p, :] = lower
        at = QC * (len(REACH) + p)
        s3[at : at + QC, :] = jnp.where(y_even, upper, lower)
        s4[at : at + QC, :] = jnp.where(y_even, lower, upper)


def half_rows(first, second, upper):
    low = sublane(first.shape) < 4
    if upper:
        return jnp.where(low, sub_roll(first, 4), second)
    return jnp.where(low, first, sub_roll(second, 4))


def second_row_kernel(idx, own, r1, r2, m, s3, s4):
    y_even = even(idx, 1)
    row_sends(idx, window_tiles(idx, own, r1, r2), s3, s4)
    at = QC * len(REACH)
    for x in range(4):
        for pair in range(2):
            base = 32 * pair
            up, low = (
                slice((4 * x + y) * 128, (4 * x + y) * 128 + 128) for y in (3, 0)
            )
            upper = half_rows(m[base + 8 : base + 16, up], m[base + 24 : base + 32, up], True)
            lower = half_rows(m[base : base + 8, low], m[base + 16 : base + 24, low], False)
            s3[at : at + 8, :] = jnp.where(y_even, upper, lower)
            s4[at : at + 8, :] = jnp.where(y_even, lower, upper)
            at += 8


def second_edges(idx, r1, r2, r3, r4):
    x_even, y_even = even(idx, 0), even(idx, 1)

    def x_face(ref):
        return jnp.concatenate([ref[96 + 16 * y : 112 + 16 * y, :] for y in range(4)], axis=1)

    def y_face(ref, upper):
        base = QC * len(REACH)
        rows = []
        for i in range(4):
            parts = []
            for x in range(4):
                at = base + 16 * x + 8 * (i // 2)
                part = ref[at : at + 8, :]
                parts.append(sub_roll(part, 4) if (i % 2 == 0) == upper else part)
            rows.append(jnp.concatenate(parts, axis=1))
        return jnp.concatenate(rows, axis=0)

    return (
        jnp.where(x_even, x_face(r2), x_face(r1)),
        jnp.where(x_even, x_face(r1), x_face(r2)),
        jnp.where(y_even, y_face(r4, True), y_face(r3, True)),
        jnp.where(y_even, y_face(r3, False), y_face(r4, False)),
    )


def lift_kernel(m, t_in, csr, idx, r1, r2, r3, r4, pm, u, out, s1, s2, s3, s4, x_ref, t_ref):
    t_ref[...] = t_in[...]
    mid_edge_terms(csr, mid_edges(idx, r1, r2, r3, r4), t_ref)
    high, low = halves(m[...] + 0.2 * t_ref[...])
    x_ref[0:64, :] = high
    x_ref[64:128, :] = low
    x_ref[128:192, :] = high
    x_ref[192:256, :] = jnp.zeros((64, LANES), BF16)
    for n in range(4):
        out[:, chunk(n)] = u[:, chunk(n)] + dot(pm[...], x_ref[:, chunk(n)])
    fine_sends(out, idx, s1, s2, s3, s4)


def place_first(window, whole, r3, r4, coef, idx):
    y_even = even(idx, 1)
    window[...] = jnp.zeros((QC * WROWS, 128), F32)

    def put(plane, y, value):
        window[pl.ds(window_row(plane, y), QC, stride=WROWS), :] = value

    def below(n):
        return jnp.where(y_even, tile(r4, n), tile(r3, n))

    def above(n):
        return jnp.where(y_even, tile(r3, n), tile(r4, n))

    def weight(n, plane, y):
        row = window_row(plane, y)
        return coef[n, row : row + 1, :]

    count = len(REACH)
    for p in range(WX):
        for y in range(4):
            value = tile(whole, 4 * p + y)
            if y == 0:
                value = value + weight(2, p, 0) * below(count + p)
            if y == 3:
                value = value + weight(3, p, 3) * above(count + p)
            put(p, y, value)
    for n, (p, d) in enumerate(REACH):
        lower, upper = below(n), above(n)
        if d == 1:
            lower = lower + weight(3, p, -1) * tile(whole, 50 + p)
            upper = upper + weight(2, p, 4) * tile(whole, 40 + p)
        put(p, -d, lower)
        put(p, 3 + d, upper)


def place_second(window, own, r1, r2, r3, r4, idx):
    y_even = even(idx, 1)
    window[...] = jnp.zeros((QC * WROWS, 128), F32)

    def put(plane, y, value):
        window[pl.ds(window_row(plane, y), QC, stride=WROWS), :] = value

    planes = window_tiles(idx, own, r1, r2)
    for p in range(WX):
        for y in range(4):
            put(p, y, planes[p][y])
    for n, (p, d) in enumerate(REACH):
        put(p, -d, jnp.where(y_even, tile(r4, n), tile(r3, n)))
        put(p, 3 + d, jnp.where(y_even, tile(r3, n), tile(r4, n)))


def coarse_sweep(c_ref, out_ref, g_ref, coef, kc, first, last):
    def rows(d, plane):
        return pl.ds(d * WROWS + plane * 16, 16)

    def step(plane):
        c = [c_ref[rows(d, plane), :] for d in range(QC)]
        weights = [coef[n, pl.ds(plane * 16, 16), :] for n in range(6)]
        for d in range(QC):
            t = g_ref[rows(d, plane), :] - 4.0 * c[d]
            for j in range(QC):
                t = t - kc[j, d] * c[j]
            if d & 4:
                t = t + weights[1] * c_ref[rows(d - 4, plane + 1), :]
            else:
                t = t + weights[0] * c_ref[rows(d + 4, plane - 1), :]
            if d & 2:
                t = t + weights[3] * sub_roll(c[d - 2], -1)
            else:
                t = t + weights[2] * sub_roll(c[d + 2], 1)
            if d & 1:
                t = t + weights[5] * pltpu.roll(c[d - 1], 127, 1)
            else:
                t = t + weights[4] * pltpu.roll(c[d + 1], 1, 1)
            out_ref[rows(d, plane), :] = c[d] + 0.2 * t

    for plane in range(first, last):
        step(plane)


def coarse_kernel(whole, r3, r4, kc, idx, coef, m, g, pay, s1, s2, one, two):
    place_first(g, whole, r3, r4, coef, idx)
    one[...] = 0.2 * g[...]
    coarse_sweep(one, two, g, coef, kc, 1, 9)
    coarse_sweep(two, one, g, coef, kc, 2, 8)
    coarse_sweep(one, two, g, coef, kc, 3, 7)
    for c in range(COLS):
        row = window_row(3 + c // 4, c % 4)
        pay[QC * c : QC * c + QC, :] = two[pl.ds(row, QC, stride=WROWS), :]
    far, near = [pay[32:128, :]], [pay[0:96, :]]
    for y in range(4):
        far.append(m[48:64, (12 + y) * 128 : (13 + y) * 128])
        near.append(m[0:16, y * 128 : y * 128 + 128])
    far_near(idx, jnp.concatenate(far, axis=0), jnp.concatenate(near, axis=0), s1, s2)


def correct_kernel(
    own, r1, r2, r3, r4, kc, idx, g, coef, spread, m, gm, csr, km,
    out, s1, s2, s3, s4, one, two, x_ref, t_ref, m_ref,
):
    place_second(one, own, r1, r2, r3, r4, idx)
    coarse_sweep(one, two, g, coef, kc, 1, 9)
    coarse_sweep(two, one, g, coef, kc, 2, 8)

    def lifted(x, y, rows):
        total = None
        for d in range(QC):
            row = d * WROWS + (3 + x) * 16 + 4 + y
            part = spread[d, rows, :] * one[row : row + 1, :]
            total = part if total is None else total + part
        return total

    whole = slice(0, QM)
    for c in range(COLS):
        lanes = slice(c * 128, c * 128 + 128)
        m_ref[:, lanes] = m[:, lanes] + lifted(c // 4, c % 4, whole)
    below_x, above_x, below_y, above_y = second_edges(idx, r1, r2, r3, r4)
    below_x = below_x + jnp.concatenate([lifted(-1, y, slice(48, 64)) for y in range(4)], axis=1)
    above_x = above_x + jnp.concatenate([lifted(4, y, slice(0, 16)) for y in range(4)], axis=1)
    below_rows, above_rows = [], []
    for i in range(4):
        last, first = slice(16 * i + 8, 16 * i + 16), slice(16 * i, 16 * i + 8)
        below_rows.append(jnp.concatenate([lifted(x, -1, last) for x in range(4)], axis=1))
        above_rows.append(jnp.concatenate([lifted(x, 4, first) for x in range(4)], axis=1))
    below_y = below_y + jnp.concatenate(below_rows, axis=0)
    above_y = above_y + jnp.concatenate(above_rows, axis=0)
    mid_local(m_ref, gm, csr, km, t_ref, x_ref)
    mid_edge_terms(csr, (below_x, above_x, below_y, above_y), t_ref)
    out[...] = m_ref[...] + 0.2 * t_ref[...]
    mid_sends(out, idx, s1, s2, s3, s4)


def partners(step):
    nx, ny = lax.axis_size("gx"), lax.axis_size("yz")
    pairs = []
    for a in range(nx):
        for b in range(ny):
            to = (a, b)
            if step < 2:
                at = ((a + step) ^ 1) - step
                to = (at, b) if 0 <= at < nx else (a, b ^ 1)
            else:
                at = ((b + step - 2) ^ 1) - (step - 2)
                to = (a, at) if 0 <= at < ny else (a ^ 1, b)
            pairs.append((a * ny + b, to[0] * ny + to[1]))
    return pairs


def swap(values, step):
    return lax.ppermute(values, ("gx", "yz"), partners(step))


def exchange(sends):
    s1, s2, s3, s4 = sends
    r2, r1, r4, r3 = swap(s2, 1), swap(s1, 0), swap(s4, 3), swap(s3, 2)
    return r1, r2, r3, r4


def exchange_rows(kernel, rows, outs, idx, own, s1, s2, extra):
    r2, r1 = swap(s2, 1), swap(s1, 0)
    s3, s4, *rest = call(kernel, [((rows, 128), F32)] * 2 + outs, (), (0,))(
        idx, own, r1, r2, extra
    )
    r4, r3 = swap(s4, 3), swap(s3, 2)
    return r1, r2, r3, r4, rest


def body(seed, scale, coef, fine, smooth, mid, coarse, pmid, plow, noise, inc):
    idx = jnp.stack(
        [
            lax.axis_index("gx"),
            lax.axis_index("yz"),
            jnp.int32(lax.axis_size("gx")),
            jnp.int32(lax.axis_size("yz")),
        ]
    ).astype(jnp.int32)
    slots = slot_matrix()
    to_slot, from_slot = jnp.asarray(slots, BF16), jnp.asarray(slots.T, BF16)

    fine_field = ((SF, LANES), F32)
    fine_faces = [((40, 512), F32)] * 2 + [((48, 512), F32)] * 2
    mid_field = ((QM, LANES), F32)
    mid_faces = [((16, 512), F32)] * 2 + [((32, 512), F32)] * 2
    xf = pltpu.VMEM((512, LANES), BF16)
    xm, tm = pltpu.VMEM((256, LANES), BF16), pltpu.VMEM((QM, LANES), F32)
    window = ((QC * WROWS, 128), F32)
    windows = [pltpu.VMEM((QC * WROWS, 128), F32)] * 2

    operands = (
        seed.reshape(QF * COLS, 128),
        scale.reshape(COLS, 128),
        coef.reshape(3 * COLS, 128),
        to_slot,
        smooth,
        fine,
        mid,
        pmid.T,
        plow.T,
    )
    g, u, csx, csr, s1, s2, s3, s4, kf, sf, pmt, km, plt, plv = call(
        first_kernel,
        [fine_field, fine_field, ((16, 512), F32), ((8, LANES), F32)]
        + [((56, 512), F32)] * 2
        + [((48, 512), F32)] * 2
        + [
            ((SF, 768), BF16),
            ((SF, 768), BF16),
            ((QM, 768), BF16),
            ((QM, 256), BF16),
            ((16, 256), BF16),
            ((32, 256), BF16),
        ],
        [pltpu.VMEM(operand.shape, operand.dtype) for operand in operands]
        + [pltpu.SemaphoreType.DMA((len(operands),))],
        (9,),
        range(9),
    )(*operands, idx)
    nf, pm, spread = call(
        late_kernel, [((QF, 768), BF16), ((SF, 256), BF16), ((QC, QM, 128), F32)]
    )(to_slot, noise, pmid.T, plow.T)

    def fine_local(u):
        (t,) = call(fine_local_kernel, [fine_field], [xf])(u, g, csr, kf)
        return t

    def mid_local_part(m):
        (t,) = call(mid_local_kernel, [mid_field], [xm])(m, gm, csr, km)
        return t

    first = exchange((s1, s2, s3, s4))
    u, *sends = call(
        spread_kernel,
        [fine_field] + fine_faces[:2] + [((88, 512), F32)] * 2,
        (),
        (3,),
    )(u, fine_local(u), csr, idx, *first, sf, csx)
    edges = exchange(sends)
    (coefw,) = call(coefficient_kernel, [((6, WROWS, 128), F32)], (), (0,))(
        idx, csx, first[0], first[1], edges[2], edges[3]
    )
    gm, m, *sends = call(restrict_kernel, [mid_field, mid_field] + mid_faces, (), (2,))(
        fine_local(u), csr, idx, *edges, pmt
    )
    edges = exchange(sends)
    m, own, s1, s2 = call(
        smooth_kernel,
        [mid_field, ((256, 128), F32)] + [((176, 128), F32)] * 2,
        [xm, tm],
        (3,),
    )(m, mid_local_part(m), csr, idx, *edges, gm, km, plt, plv)
    _, _, r3, r4, (whole,) = exchange_rows(
        row_kernel, QC * (len(REACH) + WX), [((480, 128), F32)], idx, own, s1, s2, coefw
    )
    gw, own, s1, s2 = call(
        coarse_kernel,
        [window, ((QC * COLS, 128), F32)] + [((160, 128), F32)] * 2,
        windows,
        (3, 4),
    )(whole, r3, r4, coarse, idx, coefw, m)
    r1, r2, r3, r4, _ = exchange_rows(
        second_row_kernel, QC * len(REACH) + 64, [], idx, own, s1, s2, m
    )
    m, *sends = call(
        correct_kernel,
        [mid_field] + mid_faces,
        windows + [xm, tm, pltpu.VMEM((QM, LANES), F32)],
        (5, 6),
    )(own, r1, r2, r3, r4, coarse, idx, gw, coefw, spread, m, gm, csr, km)
    edges = exchange(sends)
    u, *sends = call(lift_kernel, [fine_field] + fine_faces, [xm, tm], (3,))(
        m, mid_local_part(m), csr, idx, *edges, pm, u
    )
    edges = exchange(sends)
    u, *sends = call(sweep_kernel, [fine_field] + fine_faces, (), (3,))(
        u, fine_local(u), csr, idx, *edges, sf
    )
    edges = exchange(sends)
    out, prev = call(
        last_kernel,
        [((QF * COLS, 128), F32)] * 2,
        [
            pltpu.VMEM((SF, LANES), F32),
            pltpu.VMEM((QF, LANES), F32),
            pltpu.VMEM((QF * COLS, 128), F32),
            pltpu.VMEM((QF * COLS, 128), F32),
            pltpu.SemaphoreType.DMA((2,)),
        ],
        (3,),
        hbm_outs=True,
    )(u, fine_local(u), csr, idx, *edges, sf, nf, from_slot, inc.reshape(COLS, 128))
    shape = seed.shape
    return out.reshape(shape), prev.reshape(shape)


def solution(mesh):
    cell, field = P("gx", "yz", None), P(None, "gx", "yz", None)
    return jax.shard_map(
        body,
        mesh=mesh,
        in_specs=(field, cell, field) + (P(),) * 7 + (cell,),
        out_specs=(field, field),
        check_vma=False,
    )
```

```python
import numpy as np
import jax
import jax.numpy as jnp
from jax import lax
from jax.sharding import PartitionSpec as P
from jax.experimental import pallas as pl
from jax.experimental.pallas import tpu as pltpu

NF = 6
QF = 216
SF = 240
QM = 64
QC = 8
COLS = 16
LANES = COLS * 128
F32 = jnp.float32
BF16 = jnp.bfloat16


def fine_slots():
    slots = []
    for i in range(6):
        slots += [(i, 0, k) for k in range(6)] + [None] * 2
        slots += [(i, 5, k) for k in range(6)] + [None] * 2
        slots += [(i, j, 0) for j in range(1, 5)] + [(i, j, 5) for j in range(1, 5)]
        slots += [(i, j, k) for j in range(1, 5) for k in range(1, 5)]
    return slots


def slot_matrix():
    to_slot = np.zeros((SF, QF), np.float32)
    for slot, node in enumerate(fine_slots()):
        if node is not None:
            to_slot[slot, (node[0] * 6 + node[1]) * 6 + node[2]] = 1.0
    return to_slot


def call(kernel, outs, scratch=(), smem=(), hbm=(), hbm_outs=False):
    def run(*operands):
        specs = [
            pl.BlockSpec(
                memory_space=pltpu.SMEM if n in smem else pltpu.HBM if n in hbm else pltpu.VMEM
            )
            for n in range(len(operands))
        ]
        operands = [
            pltpu.with_memory_space_constraint(value, pltpu.HBM) if n in hbm else value
            for n, value in enumerate(operands)
        ]
        return pl.pallas_call(
            kernel,
            out_shape=tuple(jax.ShapeDtypeStruct(s, d) for s, d in outs),
            in_specs=specs,
            out_specs=tuple(
                pl.BlockSpec(memory_space=pltpu.HBM if hbm_outs else pltpu.VMEM) for _ in outs
            ),
            scratch_shapes=list(scratch),
            compiler_params=pltpu.CompilerParams(vmem_limit_bytes=20 * 1024 * 1024),
        )(*operands)

    return run


def dot(a, b):
    return lax.dot_general(a, b, (((1,), (0,)), ((), ())), preferred_element_type=F32)


def dot_nt(a, b):
    return lax.dot_general(a, b, (((1,), (1,)), ((), ())), preferred_element_type=F32)


def halves(values):
    high = values.astype(BF16)
    return high, (values - high.astype(F32)).astype(BF16)


def lane_roll(values, shift):
    return jnp.concatenate(
        [
            pltpu.roll(values[:, c * 128 : (c + 1) * 128], shift % 128, 1)
            for c in range(values.shape[1] // 128)
        ],
        axis=1,
    )


def sub_roll(values, shift):
    return pltpu.roll(values, shift % values.shape[0], 0)


def sublane(shape):
    return lax.broadcasted_iota(jnp.int32, shape, 0)


def y_from_lower(values):
    parts, edge = [], jnp.zeros((values.shape[0], 128), F32)
    for x in range(4):
        parts += [edge, values[:, x * 512 : x * 512 + 384]]
    return jnp.concatenate(parts, axis=1)


def y_from_upper(values):
    parts, edge = [], jnp.zeros((values.shape[0], 128), F32)
    for x in range(4):
        parts += [values[:, x * 512 + 128 : x * 512 + 512], edge]
    return jnp.concatenate(parts, axis=1)


def y_column(values, y):
    return jnp.concatenate(
        [values[:, x * 512 + y * 128 : x * 512 + y * 128 + 128] for x in range(4)], axis=1
    )


def even(idx_ref, axis):
    return idx_ref[axis] % 2 == 0


def grid(rows, columns):
    return tuple(lax.broadcasted_iota(jnp.int32, (rows, columns), n) for n in range(2))


def one_hot(n):
    row, col = grid(n, n)
    return jnp.where(row == col, 1.0, 0.0).astype(BF16)


def wide(out, rows, high, low):
    gap = jnp.zeros((rows, 16), BF16)
    out[:, 0:256] = jnp.concatenate([high, gap], axis=1)
    out[:, 256:512] = jnp.concatenate([high, gap], axis=1)
    out[:, 512:768] = jnp.concatenate([low, gap], axis=1)


def narrow(out, high, low):
    row, col = grid(64, 128)
    twice = jnp.where((row == col) | (row == col - 64), 1.0, 0.0).astype(BF16)
    once = jnp.where(row == col, 1.0, 0.0).astype(BF16)
    out[:, 0:128] = dot(high, twice).astype(BF16)
    out[:, 128:256] = dot(low, once).astype(BF16)


def turned(left, part):
    return dot_nt(left, part).astype(BF16)


def prepare_kernel(slot_in, fine_in, mid_in, pmid_in, plow_in, kf, pmt, km, plt, plv):
    slot, fine, mid = slot_in[...], fine_in[...], mid_in[...]
    pmid_t, plow_t = pmid_in[...], plow_in[...]
    wide(kf, SF, *[turned(turned(slot, part), slot) for part in halves(fine)])
    wide(pmt, QM, *[turned(part, slot) for part in halves(pmid_t)])
    turn = one_hot(QM)
    narrow(km, *[turned(turn, part) for part in halves(mid)])
    gap = jnp.zeros((8, QM), BF16)
    narrow(plt, *[jnp.concatenate([part, gap], axis=0) for part in halves(plow_t)])
    row, col = grid(QM, QM)
    moves = (
        col == row + 48,
        col == row - 48,
        (col == row + 12) & (row // 4 % 4 == 0),
        (col == row - 12) & (row // 4 % 4 == 3),
    )
    moves = [jnp.where(move, 1.0, 0.0).astype(BF16) for move in moves]
    narrow(
        plv,
        *[
            jnp.concatenate([dot(part, move).astype(BF16) for move in moves], axis=0)
            for part in halves(plow_t)
        ],
    )


def late_kernel(slot, noise, pmid_t, plow_t, nf, pm, spread):
    turn = one_hot(QF)
    wide(nf, QF, *[turned(turned(turn, part), slot[...]) for part in halves(noise[...])])
    narrow(pm, *[turned(slot[...], part) for part in halves(pmid_t[...])])
    turn = one_hot(QM)
    values = plow_t[...]
    high, low = halves(values)
    rest = (values - high.astype(F32) - low.astype(F32)).astype(BF16)
    columns = dot_nt(turn, high) + dot_nt(turn, low) + dot_nt(turn, rest)
    for d in range(QC):
        spread[d] = jnp.broadcast_to(columns[:, d : d + 1], (QM, 128))


def split_fine(values, x_ref, lanes):
    high, low = halves(values)
    x_ref[0:SF, lanes] = high
    x_ref[256 : 256 + SF, lanes] = low


def clear_fine(x_ref):
    x_ref[SF:256, :] = jnp.zeros((256 - SF, LANES), BF16)
    x_ref[256 + SF : 512, :] = jnp.zeros((256 - SF, LANES), BF16)


def split_product(w_ref, values):
    high, low = halves(values)
    w = w_ref[:, 0:SF]
    return dot(w, high) + dot(w, low) + dot(w_ref[:, 512 : 512 + SF], high)


def fine_product(w_ref, x_ref, lanes):
    return dot(w_ref[:, 0:512], x_ref[:, lanes]) + dot(w_ref[:, 512:768], x_ref[0:256, lanes])


def mid_product(w_ref, values, x_ref):
    high, low = halves(values)
    x_ref[0:64, :] = high
    x_ref[64:128, :] = low
    x_ref[128:192, :] = high
    x_ref[192:256, :] = jnp.zeros((64, LANES), BF16)
    return dot(w_ref[...], x_ref[...])


def chunk(n):
    return slice(n * 512, n * 512 + 512)


FACE_ROWS = [slice(8 * r, min(8 * r + 8, 36)) for r in range(5)]


def x_face(u_ref, base, lanes):
    parts = [u_ref[base + 8 * r : base + 8 * r + 8, lanes] for r in range(5)]
    row = sublane(parts[0].shape)
    parts[0] = jnp.where(row < 6, parts[0], sub_roll(parts[4], 2))
    parts[1] = jnp.where(row < 6, parts[1], parts[4])
    parts[4] = parts[4][0:4]
    return parts


def x_face_tile(ref, r, lanes):
    if r < 4:
        return ref[8 * r : 8 * r + 8, lanes]
    return jnp.concatenate([ref[32:36, lanes], ref[6:8, lanes], ref[14:16, lanes]], axis=0)


def fine_sends(u_ref, idx, s1, s2, s3, s4):
    x_even, y_even = even(idx, 0), even(idx, 1)
    upper, lower = x_face(u_ref, 200, slice(1536, 2048)), x_face(u_ref, 0, slice(0, 512))
    for rows, up, low in zip(FACE_ROWS, upper, lower):
        s1[rows, :] = jnp.where(x_even, up, low)
        s2[rows, :] = jnp.where(x_even, low, up)
    for i in range(6):
        upper = y_column(u_ref[40 * i + 8 : 40 * i + 16, :], 3)
        lower = y_column(u_ref[40 * i : 40 * i + 8, :], 0)
        s3[8 * i : 8 * i + 8, :] = jnp.where(y_even, upper, lower)
        s4[8 * i : 8 * i + 8, :] = jnp.where(y_even, lower, upper)


def fine_local_kernel(u_ref, g_ref, csr, kf, t_ref, x_ref):
    clear_fine(x_ref)
    for n in range(4):
        u = u_ref[:, chunk(n)]
        split_fine(u, x_ref, chunk(n))
        t_ref[:, chunk(n)] = g_ref[:, chunk(n)] - 4.0 * u - fine_product(kf, x_ref, chunk(n))
    t_ref[0:40, 512:2048] += csr[0:1, 512:2048] * u_ref[200:240, 0:1536]
    t_ref[200:240, 0:1536] += csr[1:2, 0:1536] * u_ref[0:40, 512:2048]
    row = sublane((8, LANES))
    for i in range(6):
        base = 40 * i
        first, last, sides = (u_ref[base + 8 * n : base + 8 * n + 8, :] for n in range(3))
        t0 = csr[2:3, :] * y_from_lower(last)
        t1 = csr[3:4, :] * y_from_upper(first)
        for n, tile, extra in ((0, first, t0), (1, last, t1)):
            lower = csr[4:5, :] * sub_roll(lane_roll(tile, 1), 3)
            upper = csr[5:6, :] * sub_roll(lane_roll(tile, -1), 5)
            t_ref[base + 8 * n : base + 8 * n + 8, :] += (
                extra + jnp.where(row == 0, lower, 0.0) + jnp.where(row == 5, upper, 0.0)
            )
        lower = csr[4:5, :] * sub_roll(lane_roll(sides, 1), 4)
        upper = csr[5:6, :] * sub_roll(lane_roll(sides, -1), 4)
        t_ref[base + 16 : base + 24, :] += jnp.where(row < 4, lower, upper)


def fine_edges(n, t_in, csr, idx, r1, r2, r3, r4):
    x_even, y_even = even(idx, 0), even(idx, 1)
    columns = []
    for y in range(4):
        lanes = slice(n * 512 + y * 128, n * 512 + y * 128 + 128)
        side, edge = slice(y * 128, y * 128 + 128), slice(n * 128, n * 128 + 128)
        tiles = []
        for r in range(SF // 8):
            tile = t_in[8 * r : 8 * r + 8, lanes]
            if n == 0 and r < 5:
                one, two = x_face_tile(r1, r, side), x_face_tile(r2, r, side)
                tile = tile + csr[0:1, lanes] * jnp.where(x_even, two, one)
            if n == 3 and r >= 25:
                one, two = x_face_tile(r1, r - 25, side), x_face_tile(r2, r - 25, side)
                tile = tile + csr[1:2, lanes] * jnp.where(x_even, one, two)
            rows = slice(r // 5 * 8, r // 5 * 8 + 8)
            if y == 0 and r % 5 == 0:
                tile = tile + csr[2:3, lanes] * jnp.where(y_even, r4[rows, edge], r3[rows, edge])
            if y == 3 and r % 5 == 1:
                tile = tile + csr[3:4, lanes] * jnp.where(y_even, r3[rows, edge], r4[rows, edge])
            tiles.append(tile)
        columns.append(jnp.concatenate(tiles, axis=0))
    return jnp.concatenate(columns, axis=1)


def fine_update(u_ref, t_in, csr, idx, received, out_ref, sf):
    for n in range(4):
        t = fine_edges(n, t_in, csr, idx, *received)
        out_ref[:, chunk(n)] = u_ref[:, chunk(n)] + split_product(sf, t)


def first_kernel(
    seed_in, scale_in, coef_in, slot_in, smooth_in, fine_in, mid_in, pmid_in, plow_in, idx,
    g, u1, csx, csr, s1, s2, s3, s4, sf, slot, fine, mid, pmid, plow,
    seed, scale, coef, smooth, done,
):
    copies = {}
    for n, (name, source, target) in enumerate(
        (
            ("scale", scale_in, scale),
            ("coef", coef_in, coef),
            ("slot", slot_in, slot),
            ("smooth", smooth_in, smooth),
            ("seed", seed_in, seed),
            ("fine", fine_in, fine),
            ("pmid", pmid_in, pmid),
            ("plow", plow_in, plow),
            ("mid", mid_in, mid),
        )
    ):
        copies[name] = pltpu.make_async_copy(source, target, done.at[n])
        copies[name].start()
    csr[6:8, :] = jnp.zeros((2, LANES), F32)
    csx[...] = jnp.zeros((16, 512), F32)
    copies["scale"].wait()
    copies["coef"].wait()
    over = 1.0 / scale[...]
    lane = lax.broadcasted_iota(jnp.int32, (COLS, 128), 1)
    column = lax.broadcasted_iota(jnp.int32, (COLS, 128), 0)
    for d in range(3):
        value = coef[16 * d : 16 * d + 16, :] * over
        low, high = 0.9 * value, 0.3 * value
        if d == 0:
            low = jnp.where((column < 4) & (idx[0] == 0), 0.0, low)
            high = jnp.where((column >= 12) & (idx[0] == idx[2] - 1), 0.0, high)
        if d == 1:
            low = jnp.where((column % 4 == 0) & (idx[1] == 0), 0.0, low)
            high = jnp.where((column % 4 == 3) & (idx[1] == idx[3] - 1), 0.0, high)
        if d == 2:
            low = jnp.where(lane == 0, 0.0, low)
            high = jnp.where(lane == 127, 0.0, high)
        for c in range(COLS):
            x, y = c // 4, c % 4
            lanes = slice(c * 128, c * 128 + 128)
            csx[4 * x + d : 4 * x + d + 1, y * 128 : y * 128 + 128] = value[c : c + 1, :]
            csr[2 * d : 2 * d + 1, lanes] = low[c : c + 1, :]
            csr[2 * d + 1 : 2 * d + 2, lanes] = high[c : c + 1, :]
    x_even = even(idx, 0)
    far, near = csx[4:16, :], csx[0:12, :]
    s1[36:48, :] = jnp.where(x_even, far, near)
    s2[36:48, :] = jnp.where(x_even, near, far)
    copies["slot"].wait()
    copies["smooth"].wait()
    row, col = grid(QF, QF)
    first = [
        turned(slot[...], part)
        for part in halves(smooth[...] + jnp.where(row == col, 0.25, 0.0))
    ]
    wide(sf, SF, *[turned(part, slot[...]) for part in first])
    copies["seed"].wait()
    both = jnp.concatenate([first[0], slot[...]], axis=0)
    for n in range(4):
        values = jnp.concatenate(
            [
                seed[pl.ds(c, QF, stride=COLS), :] * over[c : c + 1, :]
                for c in range(4 * n, 4 * n + 4)
            ],
            axis=1,
        )
        high, low = halves(values)
        result = dot(both, high) + dot(both, low)
        g[:, chunk(n)] = result[SF:, :]
        u1[:, chunk(n)] = result[:SF, :] + dot(first[1], high)
    fine_sends(u1, idx, s1, s2, s3, s4)
    for name in ("fine", "pmid", "plow", "mid"):
        copies[name].wait()


def spread_kernel(u, t_in, csr, idx, r1, r2, r3, r4, sf, csx, out, s1, s2, s3, s4):
    fine_update(u, t_in, csr, idx, (r1, r2, r3, r4), out, sf)
    fine_sends(out, idx, s1, s2, s3, s4)
    x_even, y_even = even(idx, 0), even(idx, 1)
    left = jnp.where(x_even, r2[36:48, :], r1[36:48, :])
    right = jnp.where(x_even, r1[36:48, :], r2[36:48, :])
    planes = jnp.concatenate([left, csx[...], right], axis=0)
    gap = jnp.zeros((40, 128), F32)
    far, near = planes[:, 128:512], planes[:, 0:384]
    s3[48:88, :] = jnp.concatenate([jnp.where(y_even, far, near), gap], axis=1)
    s4[48:88, :] = jnp.concatenate([jnp.where(y_even, near, far), gap], axis=1)


def coefficient_kernel(idx, csx, r1, r2, r3, r4, coef):
    x_even, y_even = even(idx, 0), even(idx, 1)
    left = jnp.where(x_even, r2[36:48, :], r1[36:48, :])
    right = jnp.where(x_even, r1[36:48, :], r2[36:48, :])
    planes = jnp.concatenate([left, csx[...], right], axis=0)
    below = jnp.where(y_even, r4[48:88, :], r3[48:88, :])
    above = jnp.where(y_even, r3[48:88, :], r4[48:88, :])
    first_x, last_x = idx[0] == 0, idx[0] == idx[2] - 1
    first_y, last_y = idx[1] == 0, idx[1] == idx[3] - 1
    lane = lax.broadcasted_iota(jnp.int32, (1, 128), 1)
    coef[...] = jnp.zeros((6, WROWS, 128), F32)
    for plane in range(WX):
        for y in range(-3, 7):
            source, at = (below, y + 3) if y < 0 else (planes, y) if y < 4 else (above, y - 4)
            row = slice(plane * 16 + 4 + y, plane * 16 + 5 + y)
            for d in range(3):
                value = source[4 * plane + d : 4 * plane + d + 1, at * 128 : at * 128 + 128]
                low, high = 0.9 * value, 0.3 * value
                if d == 0 and plane == 3:
                    low = jnp.where(first_x, 0.0, low)
                if d == 0 and plane == 6:
                    high = jnp.where(last_x, 0.0, high)
                if d == 1 and y == 0:
                    low = jnp.where(first_y, 0.0, low)
                if d == 1 and y == 3:
                    high = jnp.where(last_y, 0.0, high)
                if d == 2:
                    low = jnp.where(lane == 0, 0.0, low)
                    high = jnp.where(lane == 127, 0.0, high)
                coef[2 * d, row, :] = low
                coef[2 * d + 1, row, :] = high


def sweep_kernel(u, t_in, csr, idx, r1, r2, r3, r4, sf, out, s1, s2, s3, s4):
    fine_update(u, t_in, csr, idx, (r1, r2, r3, r4), out, sf)
    fine_sends(out, idx, s1, s2, s3, s4)


def restrict_kernel(t_in, csr, idx, r1, r2, r3, r4, pmt, gm, m1, s1, s2, s3, s4):
    for n in range(4):
        value = split_product(pmt, fine_edges(n, t_in, csr, idx, r1, r2, r3, r4))
        gm[:, chunk(n)] = value
        m1[:, chunk(n)] = 0.2 * value
    mid_sends(m1, idx, s1, s2, s3, s4)


def last_kernel(
    u, t_in, csr, idx, r1, r2, r3, r4, sf, nf, from_slot, inc, out, prev,
    u_ref, natural, out_rows, prev_rows, done,
):
    fine_update(u, t_in, csr, idx, (r1, r2, r3, r4), u_ref, sf)
    slot = from_slot[...]
    for n in range(4):
        high, low = halves(u_ref[:, chunk(n)])
        natural[:, chunk(n)] = dot(slot, high) + dot(slot, low)
        for c in range(4 * n, 4 * n + 4):
            out_rows[pl.ds(c, QF, stride=COLS), :] = natural[:, c * 128 : c * 128 + 128]
    first = pltpu.make_async_copy(out_rows, out, done.at[0])
    first.start()
    for n in range(4):
        noise = split_product(nf, u_ref[:, chunk(n)])
        for y in range(4):
            c = 4 * n + y
            prev_rows[pl.ds(c, QF, stride=COLS), :] = (
                natural[:, c * 128 : c * 128 + 128]
                + inc[c : c + 1, :] * noise[:, y * 128 : y * 128 + 128]
            )
    second = pltpu.make_async_copy(prev_rows, prev, done.at[1])
    second.start()
    first.wait()
    second.wait()


def mid_sends(m_ref, idx, s1, s2, s3, s4):
    x_even, y_even = even(idx, 0), even(idx, 1)
    upper, lower = m_ref[48:64, 1536:2048], m_ref[0:16, 0:512]
    s1[...] = jnp.where(x_even, upper, lower)
    s2[...] = jnp.where(x_even, lower, upper)
    for i in range(4):
        upper = y_column(m_ref[16 * i + 8 : 16 * i + 16, :], 3)
        lower = y_column(m_ref[16 * i : 16 * i + 8, :], 0)
        s3[8 * i : 8 * i + 8, :] = jnp.where(y_even, upper, lower)
        s4[8 * i : 8 * i + 8, :] = jnp.where(y_even, lower, upper)


def mid_edges(idx, r1, r2, r3, r4):
    x_even, y_even = even(idx, 0), even(idx, 1)
    return (
        jnp.where(x_even, r2[...], r1[...]),
        jnp.where(x_even, r1[...], r2[...]),
        jnp.where(y_even, r4[...], r3[...]),
        jnp.where(y_even, r3[...], r4[...]),
    )


def mid_local(m_ref, g_ref, csr, km, t_ref, x_ref):
    m = m_ref[...]
    t_ref[...] = g_ref[...] - 4.0 * m - mid_product(km, m, x_ref)
    t_ref[0:16, 512:2048] += csr[0:1, 512:2048] * m_ref[48:64, 0:1536]
    t_ref[48:64, 0:1536] += csr[1:2, 0:1536] * m_ref[0:16, 512:2048]
    row = sublane((8, LANES))
    for i in range(4):
        base = 16 * i
        first, last = m_ref[base : base + 8, :], m_ref[base + 8 : base + 16, :]
        extra0 = csr[2:3, :] * sub_roll(y_from_lower(last), 4)
        extra1 = csr[3:4, :] * sub_roll(y_from_upper(first), 4)
        for n, tile, extra in (
            (0, first, jnp.where(row < 4, extra0, 0.0)),
            (1, last, jnp.where(row >= 4, extra1, 0.0)),
        ):
            lower = csr[4:5, :] * sub_roll(lane_roll(tile, 1), 5)
            upper = csr[5:6, :] * sub_roll(lane_roll(tile, -1), 3)
            t_ref[base + 8 * n : base + 8 * n + 8, :] += (
                extra + jnp.where(row % 4 == 0, lower, 0.0) + jnp.where(row % 4 == 3, upper, 0.0)
            )


def mid_edge_terms(csr, edges, t_ref):
    below_x, above_x, below_y, above_y = edges
    t_ref[0:16, 0:512] += csr[0:1, 0:512] * below_x
    t_ref[48:64, 1536:2048] += csr[1:2, 1536:2048] * above_x
    row = sublane((8, 128))
    for i in range(4):
        rows = slice(8 * i, 8 * i + 8)
        for x in range(4):
            edge = slice(x * 128, x * 128 + 128)
            first, last = (slice(x * 512 + y * 128, x * 512 + y * 128 + 128) for y in (0, 3))
            below = csr[2:3, first] * sub_roll(below_y[rows, edge], 4)
            above = csr[3:4, last] * sub_roll(above_y[rows, edge], 4)
            t_ref[16 * i : 16 * i + 8, first] += jnp.where(row < 4, below, 0.0)
            t_ref[16 * i + 8 : 16 * i + 16, last] += jnp.where(row >= 4, above, 0.0)


def mid_local_kernel(m_ref, g_ref, csr, km, t_ref, x_ref):
    mid_local(m_ref, g_ref, csr, km, t_ref, x_ref)


def far_near(idx, far, near, s1, s2):
    x_even = even(idx, 0)
    s1[...] = jnp.where(x_even, far, near)
    s2[...] = jnp.where(x_even, near, far)


def smooth_kernel(
    m, t_in, csr, idx, r1, r2, r3, r4, gm, km, plt, plv, out, own, s1, s2, x_ref, t_ref
):
    t_ref[...] = t_in[...]
    mid_edge_terms(csr, mid_edges(idx, r1, r2, r3, r4), t_ref)
    out[...] = m[...] + 0.2 * t_ref[...]
    mid_local(out, gm, csr, km, t_ref, x_ref)
    faces = dot(plv[...], x_ref[...])
    value = mid_product(plt, t_ref[...], x_ref)
    for c in range(COLS):
        own[QC * c : QC * c + QC, :] = value[0:8, c * 128 : c * 128 + 128]
    for n in range(4):
        upper, lower = slice((12 + n) * 128, (13 + n) * 128), slice(n * 128, n * 128 + 128)
        own[128 + 8 * n : 136 + 8 * n, :] = faces[0:8, upper]
        own[160 + 8 * n : 168 + 8 * n, :] = faces[8:16, lower]
        upper = slice((4 * n + 3) * 128, (4 * n + 4) * 128)
        lower = slice(4 * n * 128, (4 * n + 1) * 128)
        own[192 + 8 * n : 200 + 8 * n, :] = faces[16:24, upper]
        own[224 + 8 * n : 232 + 8 * n, :] = faces[24:32, lower]
    far = (own[32:128, :], own[128:160, :], own[200:224, :], own[232:256, :])
    near = (own[0:96, :], own[160:192, :], own[192:216, :], own[224:248, :])
    far_near(idx, jnp.concatenate(far, axis=0), jnp.concatenate(near, axis=0), s1, s2)


WX = 10
WROWS = WX * 16
REACH = [(p, d) for p in range(WX) for d in range(1, 4 - max(0, 3 - p, p - 6))]


def window_row(plane, y):
    return plane * 16 + 4 + y


def tile(ref, n):
    return ref[QC * n : QC * n + QC, :]


def window_tiles(idx, own, r1, r2):
    x_even = even(idx, 0)
    planes = []
    for plane in range(WX):
        if 3 <= plane < 7:
            planes.append([tile(own, 4 * (plane - 3) + y) for y in range(4)])
        else:
            n = 4 * (plane % 7)
            left = plane < 3
            planes.append(
                [
                    jnp.where(x_even == left, tile(r2, n + y), tile(r1, n + y))
                    for y in range(4)
                ]
            )
    return planes


def row_sends(idx, planes, s3, s4):
    y_even = even(idx, 1)
    for n, (p, d) in enumerate(REACH):
        far, near = planes[p][4 - d], planes[p][d - 1]
        s3[QC * n : QC * n + QC, :] = jnp.where(y_even, far, near)
        s4[QC * n : QC * n + QC, :] = jnp.where(y_even, near, far)


def row_kernel(idx, own, r1, r2, coef, s3, s4, whole):
    x_even, y_even = even(idx, 0), even(idx, 1)
    planes = window_tiles(idx, own, r1, r2)

    def left(n):
        return jnp.where(x_even, tile(r2, n), tile(r1, n))

    def right(n):
        return jnp.where(x_even, tile(r1, n), tile(r2, n))

    def weight(n, plane, y):
        row = window_row(plane, y)
        return coef[n, row : row + 1, :]

    for y in range(4):
        planes[3][y] = planes[3][y] + weight(0, 3, y) * left(12 + y)
        planes[6][y] = planes[6][y] + weight(1, 6, y) * right(12 + y)
        planes[2][y] = planes[2][y] + weight(1, 2, y) * tile(own, 20 + y)
        planes[7][y] = planes[7][y] + weight(0, 7, y) * tile(own, 16 + y)
    row_sends(idx, planes, s3, s4)
    for p in range(WX):
        for y in range(4):
            n = 4 * p + y
            whole[QC * n : QC * n + QC, :] = planes[p][y]
        if p < 3:
            upper, lower = left(16 + p), left(19 + p)
        elif p < 7:
            upper, lower = tile(own, 24 + p - 3), tile(own, 28 + p - 3)
        else:
            upper, lower = right(16 + p - 7), right(19 + p - 7)
        whole[320 + QC * p : 328 + QC * p, :] = upper
        whole[400 + QC * p : 408 + QC * p, :] = lower
        at = QC * (len(REACH) + p)
        s3[at : at + QC, :] = jnp.where(y_even, upper, lower)
        s4[at : at + QC, :] = jnp.where(y_even, lower, upper)


def half_rows(first, second, upper):
    low = sublane(first.shape) < 4
    if upper:
        return jnp.where(low, sub_roll(first, 4), second)
    return jnp.where(low, first, sub_roll(second, 4))


def second_row_kernel(idx, own, r1, r2, m, s3, s4):
    y_even = even(idx, 1)
    row_sends(idx, window_tiles(idx, own, r1, r2), s3, s4)
    at = QC * len(REACH)
    for x in range(4):
        for pair in range(2):
            base = 32 * pair
            up, low = (
                slice((4 * x + y) * 128, (4 * x + y) * 128 + 128) for y in (3, 0)
            )
            upper = half_rows(m[base + 8 : base + 16, up], m[base + 24 : base + 32, up], True)
            lower = half_rows(m[base : base + 8, low], m[base + 16 : base + 24, low], False)
            s3[at : at + 8, :] = jnp.where(y_even, upper, lower)
            s4[at : at + 8, :] = jnp.where(y_even, lower, upper)
            at += 8


def second_edges(idx, r1, r2, r3, r4):
    x_even, y_even = even(idx, 0), even(idx, 1)

    def x_face(ref):
        return jnp.concatenate([ref[96 + 16 * y : 112 + 16 * y, :] for y in range(4)], axis=1)

    def y_face(ref, upper):
        base = QC * len(REACH)
        rows = []
        for i in range(4):
            parts = []
            for x in range(4):
                at = base + 16 * x + 8 * (i // 2)
                part = ref[at : at + 8, :]
                parts.append(sub_roll(part, 4) if (i % 2 == 0) == upper else part)
            rows.append(jnp.concatenate(parts, axis=1))
        return jnp.concatenate(rows, axis=0)

    return (
        jnp.where(x_even, x_face(r2), x_face(r1)),
        jnp.where(x_even, x_face(r1), x_face(r2)),
        jnp.where(y_even, y_face(r4, True), y_face(r3, True)),
        jnp.where(y_even, y_face(r3, False), y_face(r4, False)),
    )


def lift_kernel(m, t_in, csr, idx, r1, r2, r3, r4, pm, u, out, s1, s2, s3, s4, x_ref, t_ref):
    t_ref[...] = t_in[...]
    mid_edge_terms(csr, mid_edges(idx, r1, r2, r3, r4), t_ref)
    high, low = halves(m[...] + 0.2 * t_ref[...])
    x_ref[0:64, :] = high
    x_ref[64:128, :] = low
    x_ref[128:192, :] = high
    x_ref[192:256, :] = jnp.zeros((64, LANES), BF16)
    for n in range(4):
        out[:, chunk(n)] = u[:, chunk(n)] + dot(pm[...], x_ref[:, chunk(n)])
    fine_sends(out, idx, s1, s2, s3, s4)


def spot(x, y):
    n = QC * (WX * (x + 3) + y + 3)
    return slice(n, n + QC)


def within(steps):
    for x in range(-3, 7):
        for y in range(-3, 7):
            if max(0, -x, x - 3) + max(0, -y, y - 3) <= steps:
                yield x, y


def place_first(window, whole, r3, r4, coef, idx):
    y_even = even(idx, 1)

    def below(n):
        return jnp.where(y_even, tile(r4, n), tile(r3, n))

    def above(n):
        return jnp.where(y_even, tile(r3, n), tile(r4, n))

    def weight(n, plane, y):
        row = window_row(plane, y)
        return coef[n, row : row + 1, :]

    count = len(REACH)
    for p in range(WX):
        for y in range(4):
            value = tile(whole, 4 * p + y)
            if y == 0:
                value = value + weight(2, p, 0) * below(count + p)
            if y == 3:
                value = value + weight(3, p, 3) * above(count + p)
            window[spot(p - 3, y), :] = 0.2 * value
    for n, (p, d) in enumerate(REACH):
        lower, upper = below(n), above(n)
        if d == 1:
            lower = lower + weight(3, p, -1) * tile(whole, 50 + p)
            upper = upper + weight(2, p, 4) * tile(whole, 40 + p)
        window[spot(p - 3, -d), :] = 0.2 * lower
        window[spot(p - 3, 3 + d), :] = 0.2 * upper


def place_second(window, own, r1, r2, r3, r4, idx):
    y_even = even(idx, 1)
    planes = window_tiles(idx, own, r1, r2)
    for p in range(WX):
        for y in range(4):
            window[spot(p - 3, y), :] = planes[p][y]
    for n, (p, d) in enumerate(REACH):
        window[spot(p - 3, -d), :] = jnp.where(y_even, tile(r4, n), tile(r3, n))
        window[spot(p - 3, 3 + d), :] = jnp.where(y_even, tile(r3, n), tile(r4, n))


def coarse_columns(kc):
    row = sublane((QC, 128))
    columns = []
    for j in range(QC):
        column = jnp.zeros((QC, 128), F32)
        for d in range(QC):
            entry = (0.2 if j == d else 0.0) - 0.2 * kc[j, d]
            column = jnp.where(row == d, entry, column)
        columns.append(column)
    return columns


def coarse_sweep(c_ref, out_ref, g_ref, coef, columns, steps):
    row = sublane((QC, 128))
    x_low, y_low, z_low = row < 4, row % 4 < 2, row % 2 == 0
    for x, y in within(steps):
        at = spot(x, y)
        c = c_ref[at, :]
        value = g_ref[at, :]
        for j in range(QC):
            value = value + columns[j] * c_ref[at.start + j : at.start + j + 1, :]
        place = window_row(x + 3, y)
        w = [coef[n, place : place + 1, :] for n in range(6)]
        along_x = jnp.where(x_low, c_ref[spot(x + 1, y), :], c_ref[spot(x - 1, y), :])
        along_y = jnp.where(y_low, c_ref[spot(x, y + 1), :], c_ref[spot(x, y - 1), :])
        along_z = jnp.where(z_low, pltpu.roll(c, 127, 1), pltpu.roll(c, 1, 1))
        faces = jnp.where(x_low, w[0], w[1]) * sub_roll(along_x, 4)
        faces = faces + jnp.where(y_low, w[2], w[3]) * jnp.where(
            y_low, sub_roll(along_y, 6), sub_roll(along_y, 2)
        )
        faces = faces + jnp.where(z_low, w[4], w[5]) * jnp.where(
            z_low, sub_roll(along_z, 7), sub_roll(along_z, 1)
        )
        out_ref[at, :] = value + 0.2 * faces


def coarse_kernel(whole, r3, r4, kc, idx, coef, m, g, pay, s1, s2, one, two):
    place_first(g, whole, r3, r4, coef, idx)
    columns = coarse_columns(kc)
    coarse_sweep(g, one, g, coef, columns, 2)
    coarse_sweep(one, two, g, coef, columns, 1)
    coarse_sweep(two, one, g, coef, columns, 0)
    for c in range(COLS):
        pay[QC * c : QC * c + QC, :] = one[spot(c // 4, c % 4), :]
    far, near = [pay[32:128, :]], [pay[0:96, :]]
    for y in range(4):
        far.append(m[48:64, (12 + y) * 128 : (13 + y) * 128])
        near.append(m[0:16, y * 128 : y * 128 + 128])
    far_near(idx, jnp.concatenate(far, axis=0), jnp.concatenate(near, axis=0), s1, s2)


def correct_kernel(
    own, r1, r2, r3, r4, kc, idx, g, coef, spread, m, gm, csr, km,
    out, s1, s2, s3, s4, one, two, x_ref, t_ref, m_ref,
):
    place_second(one, own, r1, r2, r3, r4, idx)
    columns = coarse_columns(kc)
    coarse_sweep(one, two, g, coef, columns, 2)
    coarse_sweep(two, one, g, coef, columns, 1)

    def lifted(x, y, rows):
        total = None
        for d in range(QC):
            row = spot(x, y).start + d
            part = spread[d, rows, :] * one[row : row + 1, :]
            total = part if total is None else total + part
        return total

    whole = slice(0, QM)
    for c in range(COLS):
        lanes = slice(c * 128, c * 128 + 128)
        m_ref[:, lanes] = m[:, lanes] + lifted(c // 4, c % 4, whole)
    below_x, above_x, below_y, above_y = second_edges(idx, r1, r2, r3, r4)
    below_x = below_x + jnp.concatenate([lifted(-1, y, slice(48, 64)) for y in range(4)], axis=1)
    above_x = above_x + jnp.concatenate([lifted(4, y, slice(0, 16)) for y in range(4)], axis=1)
    below_rows, above_rows = [], []
    for i in range(4):
        last, first = slice(16 * i + 8, 16 * i + 16), slice(16 * i, 16 * i + 8)
        below_rows.append(jnp.concatenate([lifted(x, -1, last) for x in range(4)], axis=1))
        above_rows.append(jnp.concatenate([lifted(x, 4, first) for x in range(4)], axis=1))
    below_y = below_y + jnp.concatenate(below_rows, axis=0)
    above_y = above_y + jnp.concatenate(above_rows, axis=0)
    mid_local(m_ref, gm, csr, km, t_ref, x_ref)
    mid_edge_terms(csr, (below_x, above_x, below_y, above_y), t_ref)
    out[...] = m_ref[...] + 0.2 * t_ref[...]
    mid_sends(out, idx, s1, s2, s3, s4)


def partners(step):
    nx, ny = lax.axis_size("gx"), lax.axis_size("yz")
    pairs = []
    for a in range(nx):
        for b in range(ny):
            to = (a, b)
            if step < 2:
                at = ((a + step) ^ 1) - step
                to = (at, b) if 0 <= at < nx else (a, b ^ 1)
            else:
                at = ((b + step - 2) ^ 1) - (step - 2)
                to = (a, at) if 0 <= at < ny else (a ^ 1, b)
            pairs.append((a * ny + b, to[0] * ny + to[1]))
    return pairs


def swap(values, step):
    return lax.ppermute(values, ("gx", "yz"), partners(step))


def exchange(sends):
    s1, s2, s3, s4 = sends
    r2, r1, r4, r3 = swap(s2, 1), swap(s1, 0), swap(s4, 3), swap(s3, 2)
    return r1, r2, r3, r4


def exchange_rows(kernel, rows, outs, idx, own, s1, s2, extra):
    r2, r1 = swap(s2, 1), swap(s1, 0)
    s3, s4, *rest = call(kernel, [((rows, 128), F32)] * 2 + outs, (), (0,))(
        idx, own, r1, r2, extra
    )
    r4, r3 = swap(s4, 3), swap(s3, 2)
    return r1, r2, r3, r4, rest


def body(seed, scale, coef, fine, smooth, mid, coarse, pmid, plow, noise, inc):
    idx = jnp.stack(
        [
            lax.axis_index("gx"),
            lax.axis_index("yz"),
            jnp.int32(lax.axis_size("gx")),
            jnp.int32(lax.axis_size("yz")),
        ]
    ).astype(jnp.int32)
    slots = slot_matrix()
    to_slot, from_slot = jnp.asarray(slots, BF16), jnp.asarray(slots.T, BF16)

    fine_field = ((SF, LANES), F32)
    fine_faces = [((36, 512), F32)] * 2 + [((48, 512), F32)] * 2
    mid_field = ((QM, LANES), F32)
    mid_faces = [((16, 512), F32)] * 2 + [((32, 512), F32)] * 2
    xf = pltpu.VMEM((512, LANES), BF16)
    xm, tm = pltpu.VMEM((256, LANES), BF16), pltpu.VMEM((QM, LANES), F32)
    window = ((QC * WX * WX, 128), F32)
    windows = [pltpu.VMEM((QC * WX * WX, 128), F32)] * 2

    operands = (
        seed.reshape(QF * COLS, 128),
        scale.reshape(COLS, 128),
        coef.reshape(3 * COLS, 128),
        to_slot,
        smooth,
        fine,
        mid,
        pmid.T,
        plow.T,
    )
    g, u, csx, csr, s1, s2, s3, s4, sf, *matrices = call(
        first_kernel,
        [fine_field, fine_field, ((16, 512), F32), ((8, LANES), F32)]
        + [((48, 512), F32)] * 2
        + [((48, 512), F32)] * 2
        + [
            ((SF, 768), BF16),
            ((SF, QF), BF16),
            ((QF, QF), F32),
            ((QM, QM), F32),
            ((QM, QF), F32),
            ((QC, QM), F32),
        ],
        [pltpu.VMEM(operands[n].shape, F32) for n in (0, 1, 2, 4)]
        + [pltpu.SemaphoreType.DMA((len(operands),))],
        (9,),
        range(9),
    )(*operands, idx)
    kf, pmt, km, plt, plv = call(
        prepare_kernel,
        [
            ((SF, 768), BF16),
            ((QM, 768), BF16),
            ((QM, 256), BF16),
            ((16, 256), BF16),
            ((32, 256), BF16),
        ],
    )(*matrices)
    nf, pm, spread = call(
        late_kernel, [((QF, 768), BF16), ((SF, 256), BF16), ((QC, QM, 128), F32)]
    )(matrices[0], noise, matrices[3], matrices[4])

    def fine_local(u):
        (t,) = call(fine_local_kernel, [fine_field], [xf])(u, g, csr, kf)
        return t

    def mid_local_part(m):
        (t,) = call(mid_local_kernel, [mid_field], [xm])(m, gm, csr, km)
        return t

    first = exchange((s1, s2, s3, s4))
    u, *sends = call(
        spread_kernel,
        [fine_field] + fine_faces[:2] + [((88, 512), F32)] * 2,
        (),
        (3,),
    )(u, fine_local(u), csr, idx, *first, sf, csx)
    edges = exchange(sends)
    (coefw,) = call(coefficient_kernel, [((6, WROWS, 128), F32)], (), (0,))(
        idx, csx, first[0], first[1], edges[2], edges[3]
    )
    gm, m, *sends = call(restrict_kernel, [mid_field, mid_field] + mid_faces, (), (2,))(
        fine_local(u), csr, idx, *edges, pmt
    )
    edges = exchange(sends)
    m, own, s1, s2 = call(
        smooth_kernel,
        [mid_field, ((256, 128), F32)] + [((176, 128), F32)] * 2,
        [xm, tm],
        (3,),
    )(m, mid_local_part(m), csr, idx, *edges, gm, km, plt, plv)
    _, _, r3, r4, (whole,) = exchange_rows(
        row_kernel, QC * (len(REACH) + WX), [((480, 128), F32)], idx, own, s1, s2, coefw
    )
    gw, own, s1, s2 = call(
        coarse_kernel,
        [window, ((QC * COLS, 128), F32)] + [((160, 128), F32)] * 2,
        windows,
        (3, 4),
    )(whole, r3, r4, coarse, idx, coefw, m)
    r1, r2, r3, r4, _ = exchange_rows(
        second_row_kernel, QC * len(REACH) + 64, [], idx, own, s1, s2, m
    )
    m, *sends = call(
        correct_kernel,
        [mid_field] + mid_faces,
        windows + [xm, tm, pltpu.VMEM((QM, LANES), F32)],
        (5, 6),
    )(own, r1, r2, r3, r4, coarse, idx, gw, coefw, spread, m, gm, csr, km)
    edges = exchange(sends)
    u, *sends = call(lift_kernel, [fine_field] + fine_faces, [xm, tm], (3,))(
        m, mid_local_part(m), csr, idx, *edges, pm, u
    )
    edges = exchange(sends)
    u, *sends = call(sweep_kernel, [fine_field] + fine_faces, (), (3,))(
        u, fine_local(u), csr, idx, *edges, sf
    )
    edges = exchange(sends)
    out, prev = call(
        last_kernel,
        [((QF * COLS, 128), F32)] * 2,
        [
            pltpu.VMEM((SF, LANES), F32),
            pltpu.VMEM((QF, LANES), F32),
            pltpu.VMEM((QF * COLS, 128), F32),
            pltpu.VMEM((QF * COLS, 128), F32),
            pltpu.SemaphoreType.DMA((2,)),
        ],
        (3,),
        hbm_outs=True,
    )(u, fine_local(u), csr, idx, *edges, sf, nf, from_slot, inc.reshape(COLS, 128))
    shape = seed.shape
    return out.reshape(shape), prev.reshape(shape)


def solution(mesh):
    cell, field = P("gx", "yz", None), P(None, "gx", "yz", None)
    return jax.shard_map(
        body,
        mesh=mesh,
        in_specs=(field, cell, field) + (P(),) * 7 + (cell,),
        out_specs=(field, field),
        check_vma=False,
    )
```

```python
import numpy as np
import jax
import jax.numpy as jnp
from jax import lax
from jax.sharding import PartitionSpec as P
from jax.experimental import pallas as pl
from jax.experimental.pallas import tpu as pltpu

NF = 6
QF = 216
SF = 240
QM = 64
QC = 8
COLS = 16
LANES = COLS * 128
F32 = jnp.float32
BF16 = jnp.bfloat16


def fine_slots():
    slots = []
    for i in range(6):
        slots += [(i, 0, k) for k in range(6)] + [None] * 2
        slots += [(i, 5, k) for k in range(6)] + [None] * 2
        slots += [(i, j, 0) for j in range(1, 5)] + [(i, j, 5) for j in range(1, 5)]
        slots += [(i, j, k) for j in range(1, 5) for k in range(1, 5)]
    return slots


def slot_matrix():
    to_slot = np.zeros((SF, QF), np.float32)
    for slot, node in enumerate(fine_slots()):
        if node is not None:
            to_slot[slot, (node[0] * 6 + node[1]) * 6 + node[2]] = 1.0
    return to_slot


def call(kernel, outs, scratch=(), smem=(), hbm=(), hbm_outs=False):
    def run(*operands):
        specs = [
            pl.BlockSpec(
                memory_space=pltpu.SMEM if n in smem else pltpu.HBM if n in hbm else pltpu.VMEM
            )
            for n in range(len(operands))
        ]
        operands = [
            pltpu.with_memory_space_constraint(value, pltpu.HBM) if n in hbm else value
            for n, value in enumerate(operands)
        ]
        return pl.pallas_call(
            kernel,
            out_shape=tuple(jax.ShapeDtypeStruct(s, d) for s, d in outs),
            in_specs=specs,
            out_specs=tuple(
                pl.BlockSpec(memory_space=pltpu.HBM if hbm_outs else pltpu.VMEM) for _ in outs
            ),
            scratch_shapes=list(scratch),
            compiler_params=pltpu.CompilerParams(vmem_limit_bytes=20 * 1024 * 1024),
        )(*operands)

    return run


def dot(a, b):
    return lax.dot_general(a, b, (((1,), (0,)), ((), ())), preferred_element_type=F32)


def dot_nt(a, b):
    return lax.dot_general(a, b, (((1,), (1,)), ((), ())), preferred_element_type=F32)


def halves(values):
    high = values.astype(BF16)
    return high, (values - high.astype(F32)).astype(BF16)


def lane_roll(values, shift):
    return jnp.concatenate(
        [
            pltpu.roll(values[:, c * 128 : (c + 1) * 128], shift % 128, 1)
            for c in range(values.shape[1] // 128)
        ],
        axis=1,
    )


def sub_roll(values, shift):
    return pltpu.roll(values, shift % values.shape[0], 0)


def sublane(shape):
    return lax.broadcasted_iota(jnp.int32, shape, 0)


def y_from_lower(values):
    parts, edge = [], jnp.zeros((values.shape[0], 128), F32)
    for x in range(4):
        parts += [edge, values[:, x * 512 : x * 512 + 384]]
    return jnp.concatenate(parts, axis=1)


def y_from_upper(values):
    parts, edge = [], jnp.zeros((values.shape[0], 128), F32)
    for x in range(4):
        parts += [values[:, x * 512 + 128 : x * 512 + 512], edge]
    return jnp.concatenate(parts, axis=1)


def y_column(values, y):
    return jnp.concatenate(
        [values[:, x * 512 + y * 128 : x * 512 + y * 128 + 128] for x in range(4)], axis=1
    )


def even(idx_ref, axis):
    return idx_ref[axis] % 2 == 0


def grid(rows, columns):
    return tuple(lax.broadcasted_iota(jnp.int32, (rows, columns), n) for n in range(2))


def one_hot(n):
    row, col = grid(n, n)
    return jnp.where(row == col, 1.0, 0.0).astype(BF16)


def wide(out, rows, high, low):
    gap = jnp.zeros((rows, 16), BF16)
    out[:, 0:256] = jnp.concatenate([high, gap], axis=1)
    out[:, 256:512] = jnp.concatenate([high, gap], axis=1)
    out[:, 512:768] = jnp.concatenate([low, gap], axis=1)


def narrow(out, high, low):
    row, col = grid(64, 128)
    twice = jnp.where((row == col) | (row == col - 64), 1.0, 0.0).astype(BF16)
    once = jnp.where(row == col, 1.0, 0.0).astype(BF16)
    out[:, 0:128] = dot(high, twice).astype(BF16)
    out[:, 128:256] = dot(low, once).astype(BF16)


def turned(left, part):
    return dot_nt(left, part).astype(BF16)


def prepare_kernel(slot_in, fine_in, mid_in, pmid_in, plow_in, kf, pmt, km, plt, plv):
    slot, fine, mid = slot_in[...], fine_in[...], mid_in[...]
    pmid_t, plow_t = pmid_in[...], plow_in[...]
    wide(kf, SF, *[turned(turned(slot, part), slot) for part in halves(fine)])
    wide(pmt, QM, *[turned(part, slot) for part in halves(pmid_t)])
    turn = one_hot(QM)
    narrow(km, *[turned(turn, part) for part in halves(mid)])
    gap = jnp.zeros((8, QM), BF16)
    narrow(plt, *[jnp.concatenate([part, gap], axis=0) for part in halves(plow_t)])
    row, col = grid(QM, QM)
    moves = (
        col == row + 48,
        col == row - 48,
        (col == row + 12) & (row // 4 % 4 == 0),
        (col == row - 12) & (row // 4 % 4 == 3),
    )
    moves = [jnp.where(move, 1.0, 0.0).astype(BF16) for move in moves]
    narrow(
        plv,
        *[
            jnp.concatenate([dot(part, move).astype(BF16) for move in moves], axis=0)
            for part in halves(plow_t)
        ],
    )


def late_kernel(slot, noise, pmid_t, plow_t, nf, pm, spread):
    turn = one_hot(QF)
    wide(nf, QF, *[turned(turned(turn, part), slot[...]) for part in halves(noise[...])])
    narrow(pm, *[turned(slot[...], part) for part in halves(pmid_t[...])])
    turn = one_hot(QM)
    values = plow_t[...]
    high, low = halves(values)
    rest = (values - high.astype(F32) - low.astype(F32)).astype(BF16)
    columns = dot_nt(turn, high) + dot_nt(turn, low) + dot_nt(turn, rest)
    for d in range(QC):
        spread[d] = jnp.broadcast_to(columns[:, d : d + 1], (QM, 128))


def split_fine(values, x_ref, lanes):
    high, low = halves(values)
    x_ref[0:SF, lanes] = high
    x_ref[256 : 256 + SF, lanes] = low


def clear_fine(x_ref):
    x_ref[SF:256, :] = jnp.zeros((256 - SF, LANES), BF16)
    x_ref[256 + SF : 512, :] = jnp.zeros((256 - SF, LANES), BF16)


def split_product(w_ref, values):
    high, low = halves(values)
    w = w_ref[:, 0:SF]
    return dot(w, high) + dot(w, low) + dot(w_ref[:, 512 : 512 + SF], high)


def fine_product(w_ref, x_ref, lanes):
    return dot(w_ref[:, 0:512], x_ref[:, lanes]) + dot(w_ref[:, 512:768], x_ref[0:256, lanes])


def mid_product(w_ref, values, x_ref):
    high, low = halves(values)
    x_ref[0:64, :] = high
    x_ref[64:128, :] = low
    x_ref[128:192, :] = high
    x_ref[192:256, :] = jnp.zeros((64, LANES), BF16)
    return dot(w_ref[...], x_ref[...])


def chunk(n):
    return slice(n * 512, n * 512 + 512)


FACE_ROWS = [slice(8 * r, min(8 * r + 8, 36)) for r in range(5)]


def x_face(u_ref, base, lanes):
    parts = [u_ref[base + 8 * r : base + 8 * r + 8, lanes] for r in range(5)]
    row = sublane(parts[0].shape)
    parts[0] = jnp.where(row < 6, parts[0], sub_roll(parts[4], 2))
    parts[1] = jnp.where(row < 6, parts[1], parts[4])
    parts[4] = parts[4][0:4]
    return parts


def x_face_tile(ref, r, lanes):
    if r < 4:
        return ref[8 * r : 8 * r + 8, lanes]
    return jnp.concatenate([ref[32:36, lanes], ref[6:8, lanes], ref[14:16, lanes]], axis=0)


def fine_sends(u_ref, idx, s1, s2, s3, s4):
    x_even, y_even = even(idx, 0), even(idx, 1)
    upper, lower = x_face(u_ref, 200, slice(1536, 2048)), x_face(u_ref, 0, slice(0, 512))
    for rows, up, low in zip(FACE_ROWS, upper, lower):
        s1[rows, :] = jnp.where(x_even, up, low)
        s2[rows, :] = jnp.where(x_even, low, up)
    for i in range(6):
        upper = y_column(u_ref[40 * i + 8 : 40 * i + 16, :], 3)
        lower = y_column(u_ref[40 * i : 40 * i + 8, :], 0)
        s3[8 * i : 8 * i + 8, :] = jnp.where(y_even, upper, lower)
        s4[8 * i : 8 * i + 8, :] = jnp.where(y_even, lower, upper)


def fine_local_kernel(u_ref, g_ref, csr, kf, t_ref, x_ref):
    clear_fine(x_ref)
    for n in range(4):
        u = u_ref[:, chunk(n)]
        split_fine(u, x_ref, chunk(n))
        t_ref[:, chunk(n)] = g_ref[:, chunk(n)] - 4.0 * u - fine_product(kf, x_ref, chunk(n))
    t_ref[0:40, 512:2048] += csr[0:1, 512:2048] * u_ref[200:240, 0:1536]
    t_ref[200:240, 0:1536] += csr[1:2, 0:1536] * u_ref[0:40, 512:2048]
    row = sublane((8, LANES))
    for i in range(6):
        base = 40 * i
        first, last, sides = (u_ref[base + 8 * n : base + 8 * n + 8, :] for n in range(3))
        t0 = csr[2:3, :] * y_from_lower(last)
        t1 = csr[3:4, :] * y_from_upper(first)
        for n, tile, extra in ((0, first, t0), (1, last, t1)):
            lower = csr[4:5, :] * sub_roll(lane_roll(tile, 1), 3)
            upper = csr[5:6, :] * sub_roll(lane_roll(tile, -1), 5)
            t_ref[base + 8 * n : base + 8 * n + 8, :] += (
                extra + jnp.where(row == 0, lower, 0.0) + jnp.where(row == 5, upper, 0.0)
            )
        lower = csr[4:5, :] * sub_roll(lane_roll(sides, 1), 4)
        upper = csr[5:6, :] * sub_roll(lane_roll(sides, -1), 4)
        t_ref[base + 16 : base + 24, :] += jnp.where(row < 4, lower, upper)


def fine_edges(n, t_in, csr, idx, r1, r2, r3, r4):
    x_even, y_even = even(idx, 0), even(idx, 1)
    columns = []
    for y in range(4):
        lanes = slice(n * 512 + y * 128, n * 512 + y * 128 + 128)
        side, edge = slice(y * 128, y * 128 + 128), slice(n * 128, n * 128 + 128)
        tiles = []
        for r in range(SF // 8):
            tile = t_in[8 * r : 8 * r + 8, lanes]
            if n == 0 and r < 5:
                one, two = x_face_tile(r1, r, side), x_face_tile(r2, r, side)
                tile = tile + csr[0:1, lanes] * jnp.where(x_even, two, one)
            if n == 3 and r >= 25:
                one, two = x_face_tile(r1, r - 25, side), x_face_tile(r2, r - 25, side)
                tile = tile + csr[1:2, lanes] * jnp.where(x_even, one, two)
            rows = slice(r // 5 * 8, r // 5 * 8 + 8)
            if y == 0 and r % 5 == 0:
                tile = tile + csr[2:3, lanes] * jnp.where(y_even, r4[rows, edge], r3[rows, edge])
            if y == 3 and r % 5 == 1:
                tile = tile + csr[3:4, lanes] * jnp.where(y_even, r3[rows, edge], r4[rows, edge])
            tiles.append(tile)
        columns.append(jnp.concatenate(tiles, axis=0))
    return jnp.concatenate(columns, axis=1)


def fine_update(u_ref, t_in, csr, idx, received, out_ref, sf):
    for n in range(4):
        t = fine_edges(n, t_in, csr, idx, *received)
        out_ref[:, chunk(n)] = u_ref[:, chunk(n)] + split_product(sf, t)


def first_kernel(
    seed_in, scale_in, coef_in, slot_in, smooth_in, fine_in, mid_in, pmid_in, plow_in, idx,
    g, u1, csx, csr, s1, s2, s3, s4, sf, slot, fine, mid, pmid, plow,
    seed, scale, coef, smooth, done,
):
    copies = {}
    for n, (name, source, target) in enumerate(
        (
            ("scale", scale_in, scale),
            ("coef", coef_in, coef),
            ("slot", slot_in, slot),
            ("smooth", smooth_in, smooth),
            ("seed", seed_in, seed),
            ("fine", fine_in, fine),
            ("pmid", pmid_in, pmid),
            ("plow", plow_in, plow),
            ("mid", mid_in, mid),
        )
    ):
        copies[name] = pltpu.make_async_copy(source, target, done.at[n])
        copies[name].start()
    csr[6:8, :] = jnp.zeros((2, LANES), F32)
    csx[...] = jnp.zeros((16, 512), F32)
    copies["scale"].wait()
    copies["coef"].wait()
    over = 1.0 / scale[...]
    lane = lax.broadcasted_iota(jnp.int32, (COLS, 128), 1)
    column = lax.broadcasted_iota(jnp.int32, (COLS, 128), 0)
    for d in range(3):
        value = coef[16 * d : 16 * d + 16, :] * over
        low, high = 0.9 * value, 0.3 * value
        if d == 0:
            low = jnp.where((column < 4) & (idx[0] == 0), 0.0, low)
            high = jnp.where((column >= 12) & (idx[0] == idx[2] - 1), 0.0, high)
        if d == 1:
            low = jnp.where((column % 4 == 0) & (idx[1] == 0), 0.0, low)
            high = jnp.where((column % 4 == 3) & (idx[1] == idx[3] - 1), 0.0, high)
        if d == 2:
            low = jnp.where(lane == 0, 0.0, low)
            high = jnp.where(lane == 127, 0.0, high)
        for c in range(COLS):
            x, y = c // 4, c % 4
            lanes = slice(c * 128, c * 128 + 128)
            csx[4 * x + d : 4 * x + d + 1, y * 128 : y * 128 + 128] = value[c : c + 1, :]
            csr[2 * d : 2 * d + 1, lanes] = low[c : c + 1, :]
            csr[2 * d + 1 : 2 * d + 2, lanes] = high[c : c + 1, :]
    x_even = even(idx, 0)
    far, near = csx[4:16, :], csx[0:12, :]
    s1[36:48, :] = jnp.where(x_even, far, near)
    s2[36:48, :] = jnp.where(x_even, near, far)
    copies["slot"].wait()
    copies["smooth"].wait()
    row, col = grid(QF, QF)
    first = [
        turned(slot[...], part)
        for part in halves(smooth[...] + jnp.where(row == col, 0.25, 0.0))
    ]
    wide(sf, SF, *[turned(part, slot[...]) for part in first])
    copies["seed"].wait()
    both = jnp.concatenate([first[0], slot[...]], axis=0)
    for n in range(4):
        values = jnp.concatenate(
            [
                seed[pl.ds(c, QF, stride=COLS), :] * over[c : c + 1, :]
                for c in range(4 * n, 4 * n + 4)
            ],
            axis=1,
        )
        high, low = halves(values)
        result = dot(both, high) + dot(both, low)
        g[:, chunk(n)] = result[SF:, :]
        u1[:, chunk(n)] = result[:SF, :] + dot(first[1], high)
    fine_sends(u1, idx, s1, s2, s3, s4)
    for name in ("fine", "pmid", "plow", "mid"):
        copies[name].wait()


def spread_kernel(u, t_in, csr, idx, r1, r2, r3, r4, sf, csx, out, s1, s2, s3, s4):
    fine_update(u, t_in, csr, idx, (r1, r2, r3, r4), out, sf)
    fine_sends(out, idx, s1, s2, s3, s4)
    x_even, y_even = even(idx, 0), even(idx, 1)
    left = jnp.where(x_even, r2[36:48, :], r1[36:48, :])
    right = jnp.where(x_even, r1[36:48, :], r2[36:48, :])
    planes = jnp.concatenate([left, csx[...], right], axis=0)
    gap = jnp.zeros((40, 128), F32)
    far, near = planes[:, 128:512], planes[:, 0:384]
    s3[48:88, :] = jnp.concatenate([jnp.where(y_even, far, near), gap], axis=1)
    s4[48:88, :] = jnp.concatenate([jnp.where(y_even, near, far), gap], axis=1)


def coefficient_kernel(idx, csx, r1, r2, r3, r4, coef):
    x_even, y_even = even(idx, 0), even(idx, 1)
    left = jnp.where(x_even, r2[36:48, :], r1[36:48, :])
    right = jnp.where(x_even, r1[36:48, :], r2[36:48, :])
    planes = jnp.concatenate([left, csx[...], right], axis=0)
    below = jnp.where(y_even, r4[48:88, :], r3[48:88, :])
    above = jnp.where(y_even, r3[48:88, :], r4[48:88, :])
    first_x, last_x = idx[0] == 0, idx[0] == idx[2] - 1
    first_y, last_y = idx[1] == 0, idx[1] == idx[3] - 1
    lane = lax.broadcasted_iota(jnp.int32, (1, 128), 1)
    coef[...] = jnp.zeros((6, WROWS, 128), F32)
    for plane in range(WX):
        for y in range(-3, 7):
            source, at = (below, y + 3) if y < 0 else (planes, y) if y < 4 else (above, y - 4)
            row = slice(plane * 16 + 4 + y, plane * 16 + 5 + y)
            for d in range(3):
                value = source[4 * plane + d : 4 * plane + d + 1, at * 128 : at * 128 + 128]
                low, high = 0.9 * value, 0.3 * value
                if d == 0 and plane == 3:
                    low = jnp.where(first_x, 0.0, low)
                if d == 0 and plane == 6:
                    high = jnp.where(last_x, 0.0, high)
                if d == 1 and y == 0:
                    low = jnp.where(first_y, 0.0, low)
                if d == 1 and y == 3:
                    high = jnp.where(last_y, 0.0, high)
                if d == 2:
                    low = jnp.where(lane == 0, 0.0, low)
                    high = jnp.where(lane == 127, 0.0, high)
                coef[2 * d, row, :] = low
                coef[2 * d + 1, row, :] = high


def sweep_kernel(u, t_in, csr, idx, r1, r2, r3, r4, sf, out, s1, s2, s3, s4):
    fine_update(u, t_in, csr, idx, (r1, r2, r3, r4), out, sf)
    fine_sends(out, idx, s1, s2, s3, s4)


def restrict_kernel(t_in, csr, idx, r1, r2, r3, r4, pmt, gm, m1, s1, s2, s3, s4):
    for n in range(4):
        value = split_product(pmt, fine_edges(n, t_in, csr, idx, r1, r2, r3, r4))
        gm[:, chunk(n)] = value
        m1[:, chunk(n)] = 0.2 * value
    mid_sends(m1, idx, s1, s2, s3, s4)


def last_kernel(
    u, t_in, csr, idx, r1, r2, r3, r4, sf, nf, from_slot, inc, out, prev,
    u_ref, natural, out_rows, prev_rows, done,
):
    fine_update(u, t_in, csr, idx, (r1, r2, r3, r4), u_ref, sf)
    slot = from_slot[...]
    for n in range(4):
        high, low = halves(u_ref[:, chunk(n)])
        natural[:, chunk(n)] = dot(slot, high) + dot(slot, low)
        for c in range(4 * n, 4 * n + 4):
            out_rows[pl.ds(c, QF, stride=COLS), :] = natural[:, c * 128 : c * 128 + 128]
    first = pltpu.make_async_copy(out_rows, out, done.at[0])
    first.start()
    copies = [first]
    for low, high in ((0, 112), (112, QF)):
        for n in range(4):
            noise = split_product(nf.at[low:high], u_ref[:, chunk(n)])
            for y in range(4):
                c = 4 * n + y
                prev_rows[pl.ds(low * COLS + c, high - low, stride=COLS), :] = (
                    natural[low:high, c * 128 : c * 128 + 128]
                    + inc[c : c + 1, :] * noise[:, y * 128 : y * 128 + 128]
                )
        rows = slice(low * COLS, high * COLS)
        copies.append(
            pltpu.make_async_copy(prev_rows.at[rows], prev.at[rows], done.at[len(copies)])
        )
        copies[-1].start()
    for copy in copies:
        copy.wait()


def mid_sends(m_ref, idx, s1, s2, s3, s4):
    x_even, y_even = even(idx, 0), even(idx, 1)
    upper, lower = m_ref[48:64, 1536:2048], m_ref[0:16, 0:512]
    s1[...] = jnp.where(x_even, upper, lower)
    s2[...] = jnp.where(x_even, lower, upper)
    for i in range(4):
        upper = y_column(m_ref[16 * i + 8 : 16 * i + 16, :], 3)
        lower = y_column(m_ref[16 * i : 16 * i + 8, :], 0)
        s3[8 * i : 8 * i + 8, :] = jnp.where(y_even, upper, lower)
        s4[8 * i : 8 * i + 8, :] = jnp.where(y_even, lower, upper)


def mid_edges(idx, r1, r2, r3, r4):
    x_even, y_even = even(idx, 0), even(idx, 1)
    return (
        jnp.where(x_even, r2[...], r1[...]),
        jnp.where(x_even, r1[...], r2[...]),
        jnp.where(y_even, r4[...], r3[...]),
        jnp.where(y_even, r3[...], r4[...]),
    )


def mid_local(m_ref, g_ref, csr, km, t_ref, x_ref):
    m = m_ref[...]
    t_ref[...] = g_ref[...] - 4.0 * m - mid_product(km, m, x_ref)
    t_ref[0:16, 512:2048] += csr[0:1, 512:2048] * m_ref[48:64, 0:1536]
    t_ref[48:64, 0:1536] += csr[1:2, 0:1536] * m_ref[0:16, 512:2048]
    row = sublane((8, LANES))
    for i in range(4):
        base = 16 * i
        first, last = m_ref[base : base + 8, :], m_ref[base + 8 : base + 16, :]
        extra0 = csr[2:3, :] * sub_roll(y_from_lower(last), 4)
        extra1 = csr[3:4, :] * sub_roll(y_from_upper(first), 4)
        for n, tile, extra in (
            (0, first, jnp.where(row < 4, extra0, 0.0)),
            (1, last, jnp.where(row >= 4, extra1, 0.0)),
        ):
            lower = csr[4:5, :] * sub_roll(lane_roll(tile, 1), 5)
            upper = csr[5:6, :] * sub_roll(lane_roll(tile, -1), 3)
            t_ref[base + 8 * n : base + 8 * n + 8, :] += (
                extra + jnp.where(row % 4 == 0, lower, 0.0) + jnp.where(row % 4 == 3, upper, 0.0)
            )


def mid_edge_terms(csr, edges, t_ref):
    below_x, above_x, below_y, above_y = edges
    t_ref[0:16, 0:512] += csr[0:1, 0:512] * below_x
    t_ref[48:64, 1536:2048] += csr[1:2, 1536:2048] * above_x
    row = sublane((8, 128))
    for i in range(4):
        rows = slice(8 * i, 8 * i + 8)
        for x in range(4):
            edge = slice(x * 128, x * 128 + 128)
            first, last = (slice(x * 512 + y * 128, x * 512 + y * 128 + 128) for y in (0, 3))
            below = csr[2:3, first] * sub_roll(below_y[rows, edge], 4)
            above = csr[3:4, last] * sub_roll(above_y[rows, edge], 4)
            t_ref[16 * i : 16 * i + 8, first] += jnp.where(row < 4, below, 0.0)
            t_ref[16 * i + 8 : 16 * i + 16, last] += jnp.where(row >= 4, above, 0.0)


def mid_local_kernel(m_ref, g_ref, csr, km, t_ref, x_ref):
    mid_local(m_ref, g_ref, csr, km, t_ref, x_ref)


def far_near(idx, far, near, s1, s2):
    x_even = even(idx, 0)
    s1[...] = jnp.where(x_even, far, near)
    s2[...] = jnp.where(x_even, near, far)


def smooth_kernel(
    m, t_in, csr, idx, r1, r2, r3, r4, gm, km, plt, plv, out, own, s1, s2, x_ref, t_ref
):
    t_ref[...] = t_in[...]
    mid_edge_terms(csr, mid_edges(idx, r1, r2, r3, r4), t_ref)
    out[...] = m[...] + 0.2 * t_ref[...]
    mid_local(out, gm, csr, km, t_ref, x_ref)
    faces = dot(plv[...], x_ref[...])
    value = mid_product(plt, t_ref[...], x_ref)
    for c in range(COLS):
        own[QC * c : QC * c + QC, :] = value[0:8, c * 128 : c * 128 + 128]
    for n in range(4):
        upper, lower = slice((12 + n) * 128, (13 + n) * 128), slice(n * 128, n * 128 + 128)
        own[128 + 8 * n : 136 + 8 * n, :] = faces[0:8, upper]
        own[160 + 8 * n : 168 + 8 * n, :] = faces[8:16, lower]
        upper = slice((4 * n + 3) * 128, (4 * n + 4) * 128)
        lower = slice(4 * n * 128, (4 * n + 1) * 128)
        own[192 + 8 * n : 200 + 8 * n, :] = faces[16:24, upper]
        own[224 + 8 * n : 232 + 8 * n, :] = faces[24:32, lower]
    far = (own[32:128, :], own[128:160, :], own[200:224, :], own[232:256, :])
    near = (own[0:96, :], own[160:192, :], own[192:216, :], own[224:248, :])
    far_near(idx, jnp.concatenate(far, axis=0), jnp.concatenate(near, axis=0), s1, s2)


WX = 10
WROWS = WX * 16
REACH = [(p, d) for p in range(WX) for d in range(1, 4 - max(0, 3 - p, p - 6))]


def window_row(plane, y):
    return plane * 16 + 4 + y


def tile(ref, n):
    return ref[QC * n : QC * n + QC, :]


def window_tiles(idx, own, r1, r2):
    x_even = even(idx, 0)
    planes = []
    for plane in range(WX):
        if 3 <= plane < 7:
            planes.append([tile(own, 4 * (plane - 3) + y) for y in range(4)])
        else:
            n = 4 * (plane % 7)
            left = plane < 3
            planes.append(
                [
                    jnp.where(x_even == left, tile(r2, n + y), tile(r1, n + y))
                    for y in range(4)
                ]
            )
    return planes


def row_sends(idx, planes, s3, s4):
    y_even = even(idx, 1)
    s4[s3.shape[0] :, :] = jnp.zeros((8, 128), F32)
    for n, (p, d) in enumerate(REACH):
        far, near = planes[p][4 - d], planes[p][d - 1]
        s3[QC * n : QC * n + QC, :] = jnp.where(y_even, far, near)
        s4[QC * n : QC * n + QC, :] = jnp.where(y_even, near, far)


def row_kernel(idx, own, r1, r2, coef, s3, s4, whole):
    x_even, y_even = even(idx, 0), even(idx, 1)
    planes = window_tiles(idx, own, r1, r2)

    def left(n):
        return jnp.where(x_even, tile(r2, n), tile(r1, n))

    def right(n):
        return jnp.where(x_even, tile(r1, n), tile(r2, n))

    def weight(n, plane, y):
        row = window_row(plane, y)
        return coef[n, row : row + 1, :]

    for y in range(4):
        planes[3][y] = planes[3][y] + weight(0, 3, y) * left(12 + y)
        planes[6][y] = planes[6][y] + weight(1, 6, y) * right(12 + y)
        planes[2][y] = planes[2][y] + weight(1, 2, y) * tile(own, 20 + y)
        planes[7][y] = planes[7][y] + weight(0, 7, y) * tile(own, 16 + y)
    row_sends(idx, planes, s3, s4)
    for p in range(WX):
        for y in range(4):
            n = 4 * p + y
            whole[QC * n : QC * n + QC, :] = planes[p][y]
        if p < 3:
            upper, lower = left(16 + p), left(19 + p)
        elif p < 7:
            upper, lower = tile(own, 24 + p - 3), tile(own, 28 + p - 3)
        else:
            upper, lower = right(16 + p - 7), right(19 + p - 7)
        whole[320 + QC * p : 328 + QC * p, :] = upper
        whole[400 + QC * p : 408 + QC * p, :] = lower
        at = QC * (len(REACH) + p)
        s3[at : at + QC, :] = jnp.where(y_even, upper, lower)
        s4[at : at + QC, :] = jnp.where(y_even, lower, upper)


def half_rows(first, second, upper):
    low = sublane(first.shape) < 4
    if upper:
        return jnp.where(low, sub_roll(first, 4), second)
    return jnp.where(low, first, sub_roll(second, 4))


def second_row_kernel(idx, own, r1, r2, m, s3, s4):
    y_even = even(idx, 1)
    row_sends(idx, window_tiles(idx, own, r1, r2), s3, s4)
    at = QC * len(REACH)
    for x in range(4):
        for pair in range(2):
            base = 32 * pair
            up, low = (
                slice((4 * x + y) * 128, (4 * x + y) * 128 + 128) for y in (3, 0)
            )
            upper = half_rows(m[base + 8 : base + 16, up], m[base + 24 : base + 32, up], True)
            lower = half_rows(m[base : base + 8, low], m[base + 16 : base + 24, low], False)
            s3[at : at + 8, :] = jnp.where(y_even, upper, lower)
            s4[at : at + 8, :] = jnp.where(y_even, lower, upper)
            at += 8


def second_edges(idx, r1, r2, r3, r4):
    x_even, y_even = even(idx, 0), even(idx, 1)

    def x_face(ref):
        return jnp.concatenate([ref[96 + 16 * y : 112 + 16 * y, :] for y in range(4)], axis=1)

    def y_face(ref, upper):
        base = QC * len(REACH)
        rows = []
        for i in range(4):
            parts = []
            for x in range(4):
                at = base + 16 * x + 8 * (i // 2)
                part = ref[at : at + 8, :]
                parts.append(sub_roll(part, 4) if (i % 2 == 0) == upper else part)
            rows.append(jnp.concatenate(parts, axis=1))
        return jnp.concatenate(rows, axis=0)

    return (
        jnp.where(x_even, x_face(r2), x_face(r1)),
        jnp.where(x_even, x_face(r1), x_face(r2)),
        jnp.where(y_even, y_face(r4, True), y_face(r3, True)),
        jnp.where(y_even, y_face(r3, False), y_face(r4, False)),
    )


def lift_kernel(m, t_in, csr, idx, r1, r2, r3, r4, pm, u, out, s1, s2, s3, s4, x_ref, t_ref):
    t_ref[...] = t_in[...]
    mid_edge_terms(csr, mid_edges(idx, r1, r2, r3, r4), t_ref)
    high, low = halves(m[...] + 0.2 * t_ref[...])
    x_ref[0:64, :] = high
    x_ref[64:128, :] = low
    x_ref[128:192, :] = high
    x_ref[192:256, :] = jnp.zeros((64, LANES), BF16)
    for n in range(4):
        out[:, chunk(n)] = u[:, chunk(n)] + dot(pm[...], x_ref[:, chunk(n)])
    fine_sends(out, idx, s1, s2, s3, s4)


def spot(x, y):
    n = QC * (WX * (x + 3) + y + 3)
    return slice(n, n + QC)


def within(steps):
    for x in range(-3, 7):
        for y in range(-3, 7):
            if max(0, -x, x - 3) + max(0, -y, y - 3) <= steps:
                yield x, y


def place_first(window, whole, r3, r4, coef, idx):
    y_even = even(idx, 1)

    def below(n):
        return jnp.where(y_even, tile(r4, n), tile(r3, n))

    def above(n):
        return jnp.where(y_even, tile(r3, n), tile(r4, n))

    def weight(n, plane, y):
        row = window_row(plane, y)
        return coef[n, row : row + 1, :]

    count = len(REACH)
    for p in range(WX):
        for y in range(4):
            value = tile(whole, 4 * p + y)
            if y == 0:
                value = value + weight(2, p, 0) * below(count + p)
            if y == 3:
                value = value + weight(3, p, 3) * above(count + p)
            window[spot(p - 3, y), :] = 0.2 * value
    for n, (p, d) in enumerate(REACH):
        lower, upper = below(n), above(n)
        if d == 1:
            lower = lower + weight(3, p, -1) * tile(whole, 50 + p)
            upper = upper + weight(2, p, 4) * tile(whole, 40 + p)
        window[spot(p - 3, -d), :] = 0.2 * lower
        window[spot(p - 3, 3 + d), :] = 0.2 * upper


def place_second(window, own, r1, r2, r3, r4, idx):
    y_even = even(idx, 1)
    planes = window_tiles(idx, own, r1, r2)
    for p in range(WX):
        for y in range(4):
            window[spot(p - 3, y), :] = planes[p][y]
    for n, (p, d) in enumerate(REACH):
        window[spot(p - 3, -d), :] = jnp.where(y_even, tile(r4, n), tile(r3, n))
        window[spot(p - 3, 3 + d), :] = jnp.where(y_even, tile(r3, n), tile(r4, n))


def coarse_columns(kc):
    row = sublane((QC, 128))
    columns = []
    for j in range(QC):
        column = jnp.zeros((QC, 128), F32)
        for d in range(QC):
            entry = (0.2 if j == d else 0.0) - 0.2 * kc[j, d]
            column = jnp.where(row == d, entry, column)
        columns.append(column)
    return columns


def coarse_sweep(c_ref, out_ref, g_ref, coef, columns, steps):
    row = sublane((QC, 128))
    x_low, y_low, z_low = row < 4, row % 4 < 2, row % 2 == 0
    for x, y in within(steps):
        at = spot(x, y)
        c = c_ref[at, :]
        value = g_ref[at, :]
        for j in range(QC):
            value = value + columns[j] * c_ref[at.start + j : at.start + j + 1, :]
        place = window_row(x + 3, y)
        w = [coef[n, place : place + 1, :] for n in range(6)]
        along_x = jnp.where(x_low, c_ref[spot(x + 1, y), :], c_ref[spot(x - 1, y), :])
        along_y = jnp.where(y_low, c_ref[spot(x, y + 1), :], c_ref[spot(x, y - 1), :])
        along_z = jnp.where(z_low, pltpu.roll(c, 127, 1), pltpu.roll(c, 1, 1))
        faces = jnp.where(x_low, w[0], w[1]) * sub_roll(along_x, 4)
        faces = faces + jnp.where(y_low, w[2], w[3]) * jnp.where(
            y_low, sub_roll(along_y, 6), sub_roll(along_y, 2)
        )
        faces = faces + jnp.where(z_low, w[4], w[5]) * jnp.where(
            z_low, sub_roll(along_z, 7), sub_roll(along_z, 1)
        )
        out_ref[at, :] = value + 0.2 * faces


def coarse_kernel(whole, r3, r4, kc, idx, coef, m, g, pay, s1, s2, one, two):
    place_first(g, whole, r3, r4, coef, idx)
    columns = coarse_columns(kc)
    coarse_sweep(g, one, g, coef, columns, 2)
    coarse_sweep(one, two, g, coef, columns, 1)
    coarse_sweep(two, one, g, coef, columns, 0)
    for c in range(COLS):
        pay[QC * c : QC * c + QC, :] = one[spot(c // 4, c % 4), :]
    far, near = [pay[32:128, :]], [pay[0:96, :]]
    for y in range(4):
        far.append(m[48:64, (12 + y) * 128 : (13 + y) * 128])
        near.append(m[0:16, y * 128 : y * 128 + 128])
    far_near(idx, jnp.concatenate(far, axis=0), jnp.concatenate(near, axis=0), s1, s2)


def correct_kernel(
    own, r1, r2, r3, r4, kc, idx, g, coef, spread, m, gm, csr, km,
    out, s1, s2, s3, s4, one, two, x_ref, t_ref, m_ref,
):
    place_second(one, own, r1, r2, r3, r4, idx)
    columns = coarse_columns(kc)
    coarse_sweep(one, two, g, coef, columns, 2)
    coarse_sweep(two, one, g, coef, columns, 1)

    def lifted(x, y, rows):
        total = None
        for d in range(QC):
            row = spot(x, y).start + d
            part = spread[d, rows, :] * one[row : row + 1, :]
            total = part if total is None else total + part
        return total

    whole = slice(0, QM)
    for c in range(COLS):
        lanes = slice(c * 128, c * 128 + 128)
        m_ref[:, lanes] = m[:, lanes] + lifted(c // 4, c % 4, whole)
    below_x, above_x, below_y, above_y = second_edges(idx, r1, r2, r3, r4)
    below_x = below_x + jnp.concatenate([lifted(-1, y, slice(48, 64)) for y in range(4)], axis=1)
    above_x = above_x + jnp.concatenate([lifted(4, y, slice(0, 16)) for y in range(4)], axis=1)
    below_rows, above_rows = [], []
    for i in range(4):
        last, first = slice(16 * i + 8, 16 * i + 16), slice(16 * i, 16 * i + 8)
        below_rows.append(jnp.concatenate([lifted(x, -1, last) for x in range(4)], axis=1))
        above_rows.append(jnp.concatenate([lifted(x, 4, first) for x in range(4)], axis=1))
    below_y = below_y + jnp.concatenate(below_rows, axis=0)
    above_y = above_y + jnp.concatenate(above_rows, axis=0)
    mid_local(m_ref, gm, csr, km, t_ref, x_ref)
    mid_edge_terms(csr, (below_x, above_x, below_y, above_y), t_ref)
    out[...] = m_ref[...] + 0.2 * t_ref[...]
    mid_sends(out, idx, s1, s2, s3, s4)


def partners(step):
    nx, ny = lax.axis_size("gx"), lax.axis_size("yz")
    pairs = []
    for a in range(nx):
        for b in range(ny):
            to = (a, b)
            if step < 2:
                at = ((a + step) ^ 1) - step
                to = (at, b) if 0 <= at < nx else (a, b ^ 1)
            else:
                at = ((b + step - 2) ^ 1) - (step - 2)
                to = (a, at) if 0 <= at < ny else (a ^ 1, b)
            pairs.append((a * ny + b, to[0] * ny + to[1]))
    return pairs


def swap(values, step):
    return lax.ppermute(values, ("gx", "yz"), partners(step))


def exchange(sends):
    s1, s2, s3, s4 = sends
    r2, r1, r4, r3 = swap(s2, 1), swap(s1, 0), swap(s4, 3), swap(s3, 2)
    return r1, r2, r3, r4


def exchange_rows(kernel, rows, outs, idx, own, s1, s2, extra):
    r2, r1 = swap(s2, 1), swap(s1, 0)
    faces = [((rows, 128), F32), ((rows + 8, 128), F32)]
    s3, s4, *rest = call(kernel, faces + outs, (), (0,))(
        idx, own, r1, r2, extra
    )
    r3, r4 = swap(s3, 2), swap(s4, 3)
    return r1, r2, r3, r4, rest


def body(seed, scale, coef, fine, smooth, mid, coarse, pmid, plow, noise, inc):
    idx = jnp.stack(
        [
            lax.axis_index("gx"),
            lax.axis_index("yz"),
            jnp.int32(lax.axis_size("gx")),
            jnp.int32(lax.axis_size("yz")),
        ]
    ).astype(jnp.int32)
    slots = slot_matrix()
    to_slot, from_slot = jnp.asarray(slots, BF16), jnp.asarray(slots.T, BF16)

    fine_field = ((SF, LANES), F32)
    fine_faces = [((36, 512), F32)] * 2 + [((48, 512), F32)] * 2
    mid_field = ((QM, LANES), F32)
    mid_faces = [((16, 512), F32)] * 2 + [((32, 512), F32)] * 2
    xf = pltpu.VMEM((512, LANES), BF16)
    xm, tm = pltpu.VMEM((256, LANES), BF16), pltpu.VMEM((QM, LANES), F32)
    window = ((QC * WX * WX, 128), F32)
    windows = [pltpu.VMEM((QC * WX * WX, 128), F32)] * 2

    operands = (
        seed.reshape(QF * COLS, 128),
        scale.reshape(COLS, 128),
        coef.reshape(3 * COLS, 128),
        to_slot,
        smooth,
        fine,
        mid,
        pmid.T,
        plow.T,
    )
    g, u, csx, csr, s1, s2, s3, s4, sf, *matrices = call(
        first_kernel,
        [fine_field, fine_field, ((16, 512), F32), ((8, LANES), F32)]
        + [((48, 512), F32)] * 2
        + [((48, 512), F32)] * 2
        + [
            ((SF, 768), BF16),
            ((SF, QF), BF16),
            ((QF, QF), F32),
            ((QM, QM), F32),
            ((QM, QF), F32),
            ((QC, QM), F32),
        ],
        [pltpu.VMEM(operands[n].shape, F32) for n in (0, 1, 2, 4)]
        + [pltpu.SemaphoreType.DMA((len(operands),))],
        (9,),
        range(9),
    )(*operands, idx)
    kf, pmt, km, plt, plv = call(
        prepare_kernel,
        [
            ((SF, 768), BF16),
            ((QM, 768), BF16),
            ((QM, 256), BF16),
            ((16, 256), BF16),
            ((32, 256), BF16),
        ],
    )(*matrices)
    nf, pm, spread = call(
        late_kernel, [((QF, 768), BF16), ((SF, 256), BF16), ((QC, QM, 128), F32)]
    )(matrices[0], noise, matrices[3], matrices[4])

    def fine_local(u):
        (t,) = call(fine_local_kernel, [fine_field], [xf])(u, g, csr, kf)
        return t

    def mid_local_part(m):
        (t,) = call(mid_local_kernel, [mid_field], [xm])(m, gm, csr, km)
        return t

    first = exchange((s1, s2, s3, s4))
    u, *sends = call(
        spread_kernel,
        [fine_field] + fine_faces[:2] + [((88, 512), F32)] * 2,
        (),
        (3,),
    )(u, fine_local(u), csr, idx, *first, sf, csx)
    edges = exchange(sends)
    (coefw,) = call(coefficient_kernel, [((6, WROWS, 128), F32)], (), (0,))(
        idx, csx, first[0], first[1], edges[2], edges[3]
    )
    gm, m, *sends = call(restrict_kernel, [mid_field, mid_field] + mid_faces, (), (2,))(
        fine_local(u), csr, idx, *edges, pmt
    )
    edges = exchange(sends)
    m, own, s1, s2 = call(
        smooth_kernel,
        [mid_field, ((256, 128), F32)] + [((176, 128), F32)] * 2,
        [xm, tm],
        (3,),
    )(m, mid_local_part(m), csr, idx, *edges, gm, km, plt, plv)
    _, _, r3, r4, (whole,) = exchange_rows(
        row_kernel, QC * (len(REACH) + WX), [((480, 128), F32)], idx, own, s1, s2, coefw
    )
    gw, own, s1, s2 = call(
        coarse_kernel,
        [window, ((QC * COLS, 128), F32)] + [((160, 128), F32)] * 2,
        windows,
        (3, 4),
    )(whole, r3, r4, coarse, idx, coefw, m)
    r1, r2, r3, r4, _ = exchange_rows(
        second_row_kernel, QC * len(REACH) + 64, [], idx, own, s1, s2, m
    )
    m, *sends = call(
        correct_kernel,
        [mid_field] + mid_faces,
        windows + [xm, tm, pltpu.VMEM((QM, LANES), F32)],
        (5, 6),
    )(own, r1, r2, r3, r4, coarse, idx, gw, coefw, spread, m, gm, csr, km)
    edges = exchange(sends)
    u, *sends = call(lift_kernel, [fine_field] + fine_faces, [xm, tm], (3,))(
        m, mid_local_part(m), csr, idx, *edges, pm, u
    )
    edges = exchange(sends)
    u, *sends = call(sweep_kernel, [fine_field] + fine_faces, (), (3,))(
        u, fine_local(u), csr, idx, *edges, sf
    )
    edges = exchange(sends)
    out, prev = call(
        last_kernel,
        [((QF * COLS, 128), F32)] * 2,
        [
            pltpu.VMEM((SF, LANES), F32),
            pltpu.VMEM((QF, LANES), F32),
            pltpu.VMEM((QF * COLS, 128), F32),
            pltpu.VMEM((QF * COLS, 128), F32),
            pltpu.SemaphoreType.DMA((3,)),
        ],
        (3,),
        hbm_outs=True,
    )(u, fine_local(u), csr, idx, *edges, sf, nf, from_slot, inc.reshape(COLS, 128))
    shape = seed.shape
    return out.reshape(shape), prev.reshape(shape)


def solution(mesh):
    cell, field = P("gx", "yz", None), P(None, "gx", "yz", None)
    return jax.shard_map(
        body,
        mesh=mesh,
        in_specs=(field, cell, field) + (P(),) * 7 + (cell,),
        out_specs=(field, field),
        check_vma=False,
    )
```

```python
import numpy as np
import jax
import jax.numpy as jnp
from jax import lax
from jax.sharding import PartitionSpec as P
from jax.experimental import pallas as pl
from jax.experimental.pallas import tpu as pltpu

NF = 6
QF = 216
SF = 240
QM = 64
QC = 8
COLS = 16
LANES = COLS * 128
F32 = jnp.float32
BF16 = jnp.bfloat16


def fine_slots():
    slots = []
    for i in range(6):
        slots += [(i, 0, k) for k in range(6)] + [None] * 2
        slots += [(i, 5, k) for k in range(6)] + [None] * 2
        slots += [(i, j, 0) for j in range(1, 5)] + [(i, j, 5) for j in range(1, 5)]
        slots += [(i, j, k) for j in range(1, 5) for k in range(1, 5)]
    return slots


def slot_matrix():
    to_slot = np.zeros((SF, QF), np.float32)
    for slot, node in enumerate(fine_slots()):
        if node is not None:
            to_slot[slot, (node[0] * 6 + node[1]) * 6 + node[2]] = 1.0
    return to_slot


def call(kernel, outs, scratch=(), smem=(), hbm=(), hbm_outs=False):
    def run(*operands):
        specs = [
            pl.BlockSpec(
                memory_space=pltpu.SMEM if n in smem else pltpu.HBM if n in hbm else pltpu.VMEM
            )
            for n in range(len(operands))
        ]
        operands = [
            pltpu.with_memory_space_constraint(value, pltpu.HBM) if n in hbm else value
            for n, value in enumerate(operands)
        ]
        return pl.pallas_call(
            kernel,
            out_shape=tuple(jax.ShapeDtypeStruct(s, d) for s, d in outs),
            in_specs=specs,
            out_specs=tuple(
                pl.BlockSpec(memory_space=pltpu.HBM if hbm_outs else pltpu.VMEM) for _ in outs
            ),
            scratch_shapes=list(scratch),
            compiler_params=pltpu.CompilerParams(vmem_limit_bytes=20 * 1024 * 1024),
        )(*operands)

    return run


def dot(a, b):
    return lax.dot_general(a, b, (((1,), (0,)), ((), ())), preferred_element_type=F32)


def dot_nt(a, b):
    return lax.dot_general(a, b, (((1,), (1,)), ((), ())), preferred_element_type=F32)


def halves(values):
    high = values.astype(BF16)
    return high, (values - high.astype(F32)).astype(BF16)


def lane_roll(values, shift):
    return jnp.concatenate(
        [
            pltpu.roll(values[:, c * 128 : (c + 1) * 128], shift % 128, 1)
            for c in range(values.shape[1] // 128)
        ],
        axis=1,
    )


def sub_roll(values, shift):
    return pltpu.roll(values, shift % values.shape[0], 0)


def sublane(shape):
    return lax.broadcasted_iota(jnp.int32, shape, 0)


def y_from_lower(values):
    parts, edge = [], jnp.zeros((values.shape[0], 128), F32)
    for x in range(4):
        parts += [edge, values[:, x * 512 : x * 512 + 384]]
    return jnp.concatenate(parts, axis=1)


def y_from_upper(values):
    parts, edge = [], jnp.zeros((values.shape[0], 128), F32)
    for x in range(4):
        parts += [values[:, x * 512 + 128 : x * 512 + 512], edge]
    return jnp.concatenate(parts, axis=1)


def y_column(values, y):
    return jnp.concatenate(
        [values[:, x * 512 + y * 128 : x * 512 + y * 128 + 128] for x in range(4)], axis=1
    )


def even(idx_ref, axis):
    return idx_ref[axis] % 2 == 0


def grid(rows, columns):
    return tuple(lax.broadcasted_iota(jnp.int32, (rows, columns), n) for n in range(2))


def one_hot(n):
    row, col = grid(n, n)
    return jnp.where(row == col, 1.0, 0.0).astype(BF16)


def wide(out, rows, high, low):
    gap = jnp.zeros((rows, 16), BF16)
    out[:, 0:256] = jnp.concatenate([high, gap], axis=1)
    out[:, 256:512] = jnp.concatenate([high, gap], axis=1)
    out[:, 512:768] = jnp.concatenate([low, gap], axis=1)


def narrow(out, high, low):
    row, col = grid(64, 128)
    twice = jnp.where((row == col) | (row == col - 64), 1.0, 0.0).astype(BF16)
    once = jnp.where(row == col, 1.0, 0.0).astype(BF16)
    out[:, 0:128] = dot(high, twice).astype(BF16)
    out[:, 128:256] = dot(low, once).astype(BF16)


def turned(left, part):
    return dot_nt(left, part).astype(BF16)


def prepare_kernel(slot_in, fine_in, mid_in, pmid_in, plow_in, kf, pmt, km, plt, plv):
    slot, fine, mid = slot_in[...], fine_in[...], mid_in[...]
    pmid_t, plow_t = pmid_in[...], plow_in[...]
    wide(kf, SF, *[turned(turned(slot, part), slot) for part in halves(fine)])
    wide(pmt, QM, *[turned(part, slot) for part in halves(pmid_t)])
    turn = one_hot(QM)
    narrow(km, *[turned(turn, part) for part in halves(mid)])
    gap = jnp.zeros((8, QM), BF16)
    narrow(plt, *[jnp.concatenate([part, gap], axis=0) for part in halves(plow_t)])
    row, col = grid(QM, QM)
    moves = (
        col == row + 48,
        col == row - 48,
        (col == row + 12) & (row // 4 % 4 == 0),
        (col == row - 12) & (row // 4 % 4 == 3),
    )
    moves = [jnp.where(move, 1.0, 0.0).astype(BF16) for move in moves]
    narrow(
        plv,
        *[
            jnp.concatenate([dot(part, move).astype(BF16) for move in moves], axis=0)
            for part in halves(plow_t)
        ],
    )


def late_kernel(slot, noise, pmid_t, plow_t, nf, pm, spread):
    turn = one_hot(QF)
    wide(nf, QF, *[turned(turned(turn, part), slot[...]) for part in halves(noise[...])])
    narrow(pm, *[turned(slot[...], part) for part in halves(pmid_t[...])])
    turn = one_hot(QM)
    values = plow_t[...]
    high, low = halves(values)
    rest = (values - high.astype(F32) - low.astype(F32)).astype(BF16)
    columns = dot_nt(turn, high) + dot_nt(turn, low) + dot_nt(turn, rest)
    for d in range(QC):
        spread[d] = jnp.broadcast_to(columns[:, d : d + 1], (QM, 128))


def split_fine(values, x_ref, lanes):
    high, low = halves(values)
    x_ref[0:SF, lanes] = high
    x_ref[256 : 256 + SF, lanes] = low


def clear_fine(x_ref):
    x_ref[SF:256, :] = jnp.zeros((256 - SF, LANES), BF16)
    x_ref[256 + SF : 512, :] = jnp.zeros((256 - SF, LANES), BF16)


def split_product(w_ref, values):
    high, low = halves(values)
    w = w_ref[:, 0:SF]
    return dot(w, high) + dot(w, low) + dot(w_ref[:, 512 : 512 + SF], high)


def fine_product(w_ref, x_ref, lanes):
    return dot(w_ref[:, 0:512], x_ref[:, lanes]) + dot(w_ref[:, 512:768], x_ref[0:256, lanes])


def mid_product(w_ref, values, x_ref):
    high, low = halves(values)
    x_ref[0:64, :] = high
    x_ref[64:128, :] = low
    x_ref[128:192, :] = high
    x_ref[192:256, :] = jnp.zeros((64, LANES), BF16)
    return dot(w_ref[...], x_ref[...])


def chunk(n):
    return slice(n * 512, n * 512 + 512)


FACE_ROWS = [slice(8 * r, min(8 * r + 8, 36)) for r in range(5)]


def x_face(u_ref, base, lanes):
    parts = [u_ref[base + 8 * r : base + 8 * r + 8, lanes] for r in range(5)]
    row = sublane(parts[0].shape)
    parts[0] = jnp.where(row < 6, parts[0], sub_roll(parts[4], 2))
    parts[1] = jnp.where(row < 6, parts[1], parts[4])
    parts[4] = parts[4][0:4]
    return parts


def x_face_tile(ref, r, lanes):
    if r < 4:
        return ref[8 * r : 8 * r + 8, lanes]
    return jnp.concatenate([ref[32:36, lanes], ref[6:8, lanes], ref[14:16, lanes]], axis=0)


def fine_sends(u_ref, idx, s1, s2, s3, s4):
    x_even, y_even = even(idx, 0), even(idx, 1)
    upper, lower = x_face(u_ref, 200, slice(1536, 2048)), x_face(u_ref, 0, slice(0, 512))
    for rows, up, low in zip(FACE_ROWS, upper, lower):
        s1[rows, :] = jnp.where(x_even, up, low)
        s2[rows, :] = jnp.where(x_even, low, up)
    if s4.shape[0] == 56:
        s4[48:56, :] = jnp.zeros((8, 512), F32)
    for i in range(6):
        upper = y_column(u_ref[40 * i + 8 : 40 * i + 16, :], 3)
        lower = y_column(u_ref[40 * i : 40 * i + 8, :], 0)
        s3[8 * i : 8 * i + 8, :] = jnp.where(y_even, upper, lower)
        s4[8 * i : 8 * i + 8, :] = jnp.where(y_even, lower, upper)


def fine_local_kernel(u_ref, g_ref, csr, kf, t_ref, x_ref):
    clear_fine(x_ref)
    for n in range(4):
        u = u_ref[:, chunk(n)]
        split_fine(u, x_ref, chunk(n))
        t_ref[:, chunk(n)] = g_ref[:, chunk(n)] - 4.0 * u - fine_product(kf, x_ref, chunk(n))
    t_ref[0:40, 512:2048] += csr[0:1, 512:2048] * u_ref[200:240, 0:1536]
    t_ref[200:240, 0:1536] += csr[1:2, 0:1536] * u_ref[0:40, 512:2048]
    row = sublane((8, LANES))
    for i in range(6):
        base = 40 * i
        first, last, sides = (u_ref[base + 8 * n : base + 8 * n + 8, :] for n in range(3))
        t0 = csr[2:3, :] * y_from_lower(last)
        t1 = csr[3:4, :] * y_from_upper(first)
        for n, tile, extra in ((0, first, t0), (1, last, t1)):
            lower = csr[4:5, :] * sub_roll(lane_roll(tile, 1), 3)
            upper = csr[5:6, :] * sub_roll(lane_roll(tile, -1), 5)
            t_ref[base + 8 * n : base + 8 * n + 8, :] += (
                extra + jnp.where(row == 0, lower, 0.0) + jnp.where(row == 5, upper, 0.0)
            )
        lower = csr[4:5, :] * sub_roll(lane_roll(sides, 1), 4)
        upper = csr[5:6, :] * sub_roll(lane_roll(sides, -1), 4)
        t_ref[base + 16 : base + 24, :] += jnp.where(row < 4, lower, upper)


def fine_edges(n, t_in, csr, idx, r1, r2, r3, r4):
    x_even, y_even = even(idx, 0), even(idx, 1)
    columns = []
    for y in range(4):
        lanes = slice(n * 512 + y * 128, n * 512 + y * 128 + 128)
        side, edge = slice(y * 128, y * 128 + 128), slice(n * 128, n * 128 + 128)
        tiles = []
        for r in range(SF // 8):
            tile = t_in[8 * r : 8 * r + 8, lanes]
            if n == 0 and r < 5:
                one, two = x_face_tile(r1, r, side), x_face_tile(r2, r, side)
                tile = tile + csr[0:1, lanes] * jnp.where(x_even, two, one)
            if n == 3 and r >= 25:
                one, two = x_face_tile(r1, r - 25, side), x_face_tile(r2, r - 25, side)
                tile = tile + csr[1:2, lanes] * jnp.where(x_even, one, two)
            rows = slice(r // 5 * 8, r // 5 * 8 + 8)
            if y == 0 and r % 5 == 0:
                tile = tile + csr[2:3, lanes] * jnp.where(y_even, r4[rows, edge], r3[rows, edge])
            if y == 3 and r % 5 == 1:
                tile = tile + csr[3:4, lanes] * jnp.where(y_even, r3[rows, edge], r4[rows, edge])
            tiles.append(tile)
        columns.append(jnp.concatenate(tiles, axis=0))
    return jnp.concatenate(columns, axis=1)


def fine_update(u_ref, t_in, csr, idx, received, out_ref, sf):
    for n in range(4):
        t = fine_edges(n, t_in, csr, idx, *received)
        out_ref[:, chunk(n)] = u_ref[:, chunk(n)] + split_product(sf, t)


def first_kernel(
    seed_in, scale_in, coef_in, slot_in, smooth_in, fine_in, mid_in, pmid_in, plow_in, idx,
    g, u1, csx, csr, s1, s2, s3, s4, sf, slot, fine, mid, pmid, plow,
    seed, scale, coef, smooth, done,
):
    copies = {}
    for n, (name, source, target) in enumerate(
        (
            ("scale", scale_in, scale),
            ("coef", coef_in, coef),
            ("slot", slot_in, slot),
            ("smooth", smooth_in, smooth),
            ("seed", seed_in, seed),
            ("fine", fine_in, fine),
            ("pmid", pmid_in, pmid),
            ("plow", plow_in, plow),
            ("mid", mid_in, mid),
        )
    ):
        copies[name] = pltpu.make_async_copy(source, target, done.at[n])
        copies[name].start()
    csr[6:8, :] = jnp.zeros((2, LANES), F32)
    csx[...] = jnp.zeros((16, 512), F32)
    copies["scale"].wait()
    copies["coef"].wait()
    over = 1.0 / scale[...]
    lane = lax.broadcasted_iota(jnp.int32, (COLS, 128), 1)
    column = lax.broadcasted_iota(jnp.int32, (COLS, 128), 0)
    for d in range(3):
        value = coef[16 * d : 16 * d + 16, :] * over
        low, high = 0.9 * value, 0.3 * value
        if d == 0:
            low = jnp.where((column < 4) & (idx[0] == 0), 0.0, low)
            high = jnp.where((column >= 12) & (idx[0] == idx[2] - 1), 0.0, high)
        if d == 1:
            low = jnp.where((column % 4 == 0) & (idx[1] == 0), 0.0, low)
            high = jnp.where((column % 4 == 3) & (idx[1] == idx[3] - 1), 0.0, high)
        if d == 2:
            low = jnp.where(lane == 0, 0.0, low)
            high = jnp.where(lane == 127, 0.0, high)
        for c in range(COLS):
            x, y = c // 4, c % 4
            lanes = slice(c * 128, c * 128 + 128)
            csx[4 * x + d : 4 * x + d + 1, y * 128 : y * 128 + 128] = value[c : c + 1, :]
            csr[2 * d : 2 * d + 1, lanes] = low[c : c + 1, :]
            csr[2 * d + 1 : 2 * d + 2, lanes] = high[c : c + 1, :]
    x_even = even(idx, 0)
    far, near = csx[4:16, :], csx[0:12, :]
    s1[36:48, :] = jnp.where(x_even, far, near)
    s2[36:48, :] = jnp.where(x_even, near, far)
    copies["slot"].wait()
    copies["smooth"].wait()
    row, col = grid(QF, QF)
    first = [
        turned(slot[...], part)
        for part in halves(smooth[...] + jnp.where(row == col, 0.25, 0.0))
    ]
    wide(sf, SF, *[turned(part, slot[...]) for part in first])
    copies["seed"].wait()
    both = jnp.concatenate([first[0], slot[...]], axis=0)
    for n in range(4):
        values = jnp.concatenate(
            [
                seed[pl.ds(c, QF, stride=COLS), :] * over[c : c + 1, :]
                for c in range(4 * n, 4 * n + 4)
            ],
            axis=1,
        )
        high, low = halves(values)
        result = dot(both, high) + dot(both, low)
        g[:, chunk(n)] = result[SF:, :]
        u1[:, chunk(n)] = result[:SF, :] + dot(first[1], high)
    fine_sends(u1, idx, s1, s2, s3, s4)
    for name in ("fine", "pmid", "plow", "mid"):
        copies[name].wait()


def spread_kernel(u, t_in, csr, idx, r1, r2, r3, r4, sf, csx, out, s1, s2, s3, s4):
    fine_update(u, t_in, csr, idx, (r1, r2, r3, r4), out, sf)
    fine_sends(out, idx, s1, s2, s3, s4)
    x_even, y_even = even(idx, 0), even(idx, 1)
    left = jnp.where(x_even, r2[36:48, :], r1[36:48, :])
    right = jnp.where(x_even, r1[36:48, :], r2[36:48, :])
    planes = jnp.concatenate([left, csx[...], right], axis=0)
    gap = jnp.zeros((40, 128), F32)
    far, near = planes[:, 128:512], planes[:, 0:384]
    s3[48:88, :] = jnp.concatenate([jnp.where(y_even, far, near), gap], axis=1)
    s4[48:88, :] = jnp.concatenate([jnp.where(y_even, near, far), gap], axis=1)


def coefficient_kernel(idx, csx, r1, r2, r3, r4, coef):
    x_even, y_even = even(idx, 0), even(idx, 1)
    left = jnp.where(x_even, r2[36:48, :], r1[36:48, :])
    right = jnp.where(x_even, r1[36:48, :], r2[36:48, :])
    planes = jnp.concatenate([left, csx[...], right], axis=0)
    below = jnp.where(y_even, r4[48:88, :], r3[48:88, :])
    above = jnp.where(y_even, r3[48:88, :], r4[48:88, :])
    first_x, last_x = idx[0] == 0, idx[0] == idx[2] - 1
    first_y, last_y = idx[1] == 0, idx[1] == idx[3] - 1
    lane = lax.broadcasted_iota(jnp.int32, (1, 128), 1)
    coef[...] = jnp.zeros((6, WROWS, 128), F32)
    for plane in range(WX):
        for y in range(-3, 7):
            source, at = (below, y + 3) if y < 0 else (planes, y) if y < 4 else (above, y - 4)
            row = slice(plane * 16 + 4 + y, plane * 16 + 5 + y)
            for d in range(3):
                value = source[4 * plane + d : 4 * plane + d + 1, at * 128 : at * 128 + 128]
                low, high = 0.9 * value, 0.3 * value
                if d == 0 and plane == 3:
                    low = jnp.where(first_x, 0.0, low)
                if d == 0 and plane == 6:
                    high = jnp.where(last_x, 0.0, high)
                if d == 1 and y == 0:
                    low = jnp.where(first_y, 0.0, low)
                if d == 1 and y == 3:
                    high = jnp.where(last_y, 0.0, high)
                if d == 2:
                    low = jnp.where(lane == 0, 0.0, low)
                    high = jnp.where(lane == 127, 0.0, high)
                coef[2 * d, row, :] = low
                coef[2 * d + 1, row, :] = high


def sweep_kernel(u, t_in, csr, idx, r1, r2, r3, r4, sf, out, s1, s2, s3, s4):
    fine_update(u, t_in, csr, idx, (r1, r2, r3, r4), out, sf)
    fine_sends(out, idx, s1, s2, s3, s4)


def restrict_kernel(t_in, csr, idx, r1, r2, r3, r4, pmt, gm, m1, s1, s2, s3, s4):
    for n in range(4):
        value = split_product(pmt, fine_edges(n, t_in, csr, idx, r1, r2, r3, r4))
        gm[:, chunk(n)] = value
        m1[:, chunk(n)] = 0.2 * value
    mid_sends(m1, idx, s1, s2, s3, s4)


def last_kernel(
    u, t_in, csr, idx, r1, r2, r3, r4, sf, nf, from_slot, inc, out, prev,
    u_ref, natural, out_rows, prev_rows, done,
):
    fine_update(u, t_in, csr, idx, (r1, r2, r3, r4), u_ref, sf)
    slot = from_slot[...]
    for n in range(4):
        high, low = halves(u_ref[:, chunk(n)])
        natural[:, chunk(n)] = dot(slot, high) + dot(slot, low)
        for c in range(4 * n, 4 * n + 4):
            out_rows[pl.ds(c, QF, stride=COLS), :] = natural[:, c * 128 : c * 128 + 128]
    first = pltpu.make_async_copy(out_rows, out, done.at[0])
    first.start()
    copies = [first]
    for low, high in ((0, 112), (112, QF)):
        for n in range(4):
            noise = split_product(nf.at[low:high], u_ref[:, chunk(n)])
            for y in range(4):
                c = 4 * n + y
                prev_rows[pl.ds(low * COLS + c, high - low, stride=COLS), :] = (
                    natural[low:high, c * 128 : c * 128 + 128]
                    + inc[c : c + 1, :] * noise[:, y * 128 : y * 128 + 128]
                )
        rows = slice(low * COLS, high * COLS)
        copies.append(
            pltpu.make_async_copy(prev_rows.at[rows], prev.at[rows], done.at[len(copies)])
        )
        copies[-1].start()
    for copy in copies:
        copy.wait()


def mid_sends(m_ref, idx, s1, s2, s3, s4):
    x_even, y_even = even(idx, 0), even(idx, 1)
    upper, lower = m_ref[48:64, 1536:2048], m_ref[0:16, 0:512]
    s1[...] = jnp.where(x_even, upper, lower)
    s2[...] = jnp.where(x_even, lower, upper)
    s4[32:40, :] = jnp.zeros((8, 512), F32)
    for i in range(4):
        upper = y_column(m_ref[16 * i + 8 : 16 * i + 16, :], 3)
        lower = y_column(m_ref[16 * i : 16 * i + 8, :], 0)
        s3[8 * i : 8 * i + 8, :] = jnp.where(y_even, upper, lower)
        s4[8 * i : 8 * i + 8, :] = jnp.where(y_even, lower, upper)


def mid_edges(idx, r1, r2, r3, r4):
    x_even, y_even = even(idx, 0), even(idx, 1)
    return (
        jnp.where(x_even, r2[...], r1[...]),
        jnp.where(x_even, r1[...], r2[...]),
        jnp.where(y_even, r4[0:32, :], r3[0:32, :]),
        jnp.where(y_even, r3[0:32, :], r4[0:32, :]),
    )


def mid_local(m_ref, g_ref, csr, km, t_ref, x_ref):
    m = m_ref[...]
    t_ref[...] = g_ref[...] - 4.0 * m - mid_product(km, m, x_ref)
    t_ref[0:16, 512:2048] += csr[0:1, 512:2048] * m_ref[48:64, 0:1536]
    t_ref[48:64, 0:1536] += csr[1:2, 0:1536] * m_ref[0:16, 512:2048]
    row = sublane((8, LANES))
    for i in range(4):
        base = 16 * i
        first, last = m_ref[base : base + 8, :], m_ref[base + 8 : base + 16, :]
        extra0 = csr[2:3, :] * sub_roll(y_from_lower(last), 4)
        extra1 = csr[3:4, :] * sub_roll(y_from_upper(first), 4)
        for n, tile, extra in (
            (0, first, jnp.where(row < 4, extra0, 0.0)),
            (1, last, jnp.where(row >= 4, extra1, 0.0)),
        ):
            lower = csr[4:5, :] * sub_roll(lane_roll(tile, 1), 5)
            upper = csr[5:6, :] * sub_roll(lane_roll(tile, -1), 3)
            t_ref[base + 8 * n : base + 8 * n + 8, :] += (
                extra + jnp.where(row % 4 == 0, lower, 0.0) + jnp.where(row % 4 == 3, upper, 0.0)
            )


def mid_edge_terms(csr, edges, t_ref):
    below_x, above_x, below_y, above_y = edges
    t_ref[0:16, 0:512] += csr[0:1, 0:512] * below_x
    t_ref[48:64, 1536:2048] += csr[1:2, 1536:2048] * above_x
    row = sublane((8, 128))
    for i in range(4):
        rows = slice(8 * i, 8 * i + 8)
        for x in range(4):
            edge = slice(x * 128, x * 128 + 128)
            first, last = (slice(x * 512 + y * 128, x * 512 + y * 128 + 128) for y in (0, 3))
            below = csr[2:3, first] * sub_roll(below_y[rows, edge], 4)
            above = csr[3:4, last] * sub_roll(above_y[rows, edge], 4)
            t_ref[16 * i : 16 * i + 8, first] += jnp.where(row < 4, below, 0.0)
            t_ref[16 * i + 8 : 16 * i + 16, last] += jnp.where(row >= 4, above, 0.0)


def mid_local_kernel(m_ref, g_ref, csr, km, t_ref, x_ref):
    mid_local(m_ref, g_ref, csr, km, t_ref, x_ref)


def far_near(idx, far, near, s1, s2):
    x_even = even(idx, 0)
    s1[...] = jnp.where(x_even, far, near)
    s2[...] = jnp.where(x_even, near, far)


def smooth_kernel(
    m, t_in, csr, idx, r1, r2, r3, r4, gm, km, plt, plv, out, own, s1, s2, x_ref, t_ref
):
    t_ref[...] = t_in[...]
    mid_edge_terms(csr, mid_edges(idx, r1, r2, r3, r4), t_ref)
    out[...] = m[...] + 0.2 * t_ref[...]
    mid_local(out, gm, csr, km, t_ref, x_ref)
    faces = dot(plv[...], x_ref[...])
    value = mid_product(plt, t_ref[...], x_ref)
    for c in range(COLS):
        own[QC * c : QC * c + QC, :] = value[0:8, c * 128 : c * 128 + 128]
    for n in range(4):
        upper, lower = slice((12 + n) * 128, (13 + n) * 128), slice(n * 128, n * 128 + 128)
        own[128 + 8 * n : 136 + 8 * n, :] = faces[0:8, upper]
        own[160 + 8 * n : 168 + 8 * n, :] = faces[8:16, lower]
        upper = slice((4 * n + 3) * 128, (4 * n + 4) * 128)
        lower = slice(4 * n * 128, (4 * n + 1) * 128)
        own[192 + 8 * n : 200 + 8 * n, :] = faces[16:24, upper]
        own[224 + 8 * n : 232 + 8 * n, :] = faces[24:32, lower]
    far = (own[32:128, :], own[128:160, :], own[200:224, :], own[232:256, :])
    near = (own[0:96, :], own[160:192, :], own[192:216, :], own[224:248, :])
    far_near(idx, jnp.concatenate(far, axis=0), jnp.concatenate(near, axis=0), s1, s2)


WX = 10
WROWS = WX * 16
REACH = [(p, d) for p in range(WX) for d in range(1, 4 - max(0, 3 - p, p - 6))]


def window_row(plane, y):
    return plane * 16 + 4 + y


def tile(ref, n):
    return ref[QC * n : QC * n + QC, :]


def window_tiles(idx, own, r1, r2):
    x_even = even(idx, 0)
    planes = []
    for plane in range(WX):
        if 3 <= plane < 7:
            planes.append([tile(own, 4 * (plane - 3) + y) for y in range(4)])
        else:
            n = 4 * (plane % 7)
            left = plane < 3
            planes.append(
                [
                    jnp.where(x_even == left, tile(r2, n + y), tile(r1, n + y))
                    for y in range(4)
                ]
            )
    return planes


def row_sends(idx, planes, s3, s4):
    y_even = even(idx, 1)
    s4[s3.shape[0] :, :] = jnp.zeros((8, 128), F32)
    for n, (p, d) in enumerate(REACH):
        far, near = planes[p][4 - d], planes[p][d - 1]
        s3[QC * n : QC * n + QC, :] = jnp.where(y_even, far, near)
        s4[QC * n : QC * n + QC, :] = jnp.where(y_even, near, far)


def row_kernel(idx, own, r1, r2, coef, s3, s4, whole):
    x_even, y_even = even(idx, 0), even(idx, 1)
    planes = window_tiles(idx, own, r1, r2)

    def left(n):
        return jnp.where(x_even, tile(r2, n), tile(r1, n))

    def right(n):
        return jnp.where(x_even, tile(r1, n), tile(r2, n))

    def weight(n, plane, y):
        row = window_row(plane, y)
        return coef[n, row : row + 1, :]

    for y in range(4):
        planes[3][y] = planes[3][y] + weight(0, 3, y) * left(12 + y)
        planes[6][y] = planes[6][y] + weight(1, 6, y) * right(12 + y)
        planes[2][y] = planes[2][y] + weight(1, 2, y) * tile(own, 20 + y)
        planes[7][y] = planes[7][y] + weight(0, 7, y) * tile(own, 16 + y)
    row_sends(idx, planes, s3, s4)
    for p in range(WX):
        for y in range(4):
            n = 4 * p + y
            whole[QC * n : QC * n + QC, :] = planes[p][y]
        if p < 3:
            upper, lower = left(16 + p), left(19 + p)
        elif p < 7:
            upper, lower = tile(own, 24 + p - 3), tile(own, 28 + p - 3)
        else:
            upper, lower = right(16 + p - 7), right(19 + p - 7)
        whole[320 + QC * p : 328 + QC * p, :] = upper
        whole[400 + QC * p : 408 + QC * p, :] = lower
        at = QC * (len(REACH) + p)
        s3[at : at + QC, :] = jnp.where(y_even, upper, lower)
        s4[at : at + QC, :] = jnp.where(y_even, lower, upper)


def half_rows(first, second, upper):
    low = sublane(first.shape) < 4
    if upper:
        return jnp.where(low, sub_roll(first, 4), second)
    return jnp.where(low, first, sub_roll(second, 4))


def second_row_kernel(idx, own, r1, r2, m, s3, s4):
    y_even = even(idx, 1)
    row_sends(idx, window_tiles(idx, own, r1, r2), s3, s4)
    at = QC * len(REACH)
    for x in range(4):
        for pair in range(2):
            base = 32 * pair
            up, low = (
                slice((4 * x + y) * 128, (4 * x + y) * 128 + 128) for y in (3, 0)
            )
            upper = half_rows(m[base + 8 : base + 16, up], m[base + 24 : base + 32, up], True)
            lower = half_rows(m[base : base + 8, low], m[base + 16 : base + 24, low], False)
            s3[at : at + 8, :] = jnp.where(y_even, upper, lower)
            s4[at : at + 8, :] = jnp.where(y_even, lower, upper)
            at += 8


def second_edges(idx, r1, r2, r3, r4):
    x_even, y_even = even(idx, 0), even(idx, 1)

    def x_face(ref):
        return jnp.concatenate([ref[96 + 16 * y : 112 + 16 * y, :] for y in range(4)], axis=1)

    def y_face(ref, upper):
        base = QC * len(REACH)
        rows = []
        for i in range(4):
            parts = []
            for x in range(4):
                at = base + 16 * x + 8 * (i // 2)
                part = ref[at : at + 8, :]
                parts.append(sub_roll(part, 4) if (i % 2 == 0) == upper else part)
            rows.append(jnp.concatenate(parts, axis=1))
        return jnp.concatenate(rows, axis=0)

    return (
        jnp.where(x_even, x_face(r2), x_face(r1)),
        jnp.where(x_even, x_face(r1), x_face(r2)),
        jnp.where(y_even, y_face(r4, True), y_face(r3, True)),
        jnp.where(y_even, y_face(r3, False), y_face(r4, False)),
    )


def lift_kernel(m, t_in, csr, idx, r1, r2, r3, r4, pm, u, out, s1, s2, s3, s4, x_ref, t_ref):
    t_ref[...] = t_in[...]
    mid_edge_terms(csr, mid_edges(idx, r1, r2, r3, r4), t_ref)
    high, low = halves(m[...] + 0.2 * t_ref[...])
    x_ref[0:64, :] = high
    x_ref[64:128, :] = low
    x_ref[128:192, :] = high
    x_ref[192:256, :] = jnp.zeros((64, LANES), BF16)
    for n in range(4):
        out[:, chunk(n)] = u[:, chunk(n)] + dot(pm[...], x_ref[:, chunk(n)])
    fine_sends(out, idx, s1, s2, s3, s4)


def spot(x, y):
    n = QC * (WX * (x + 3) + y + 3)
    return slice(n, n + QC)


def within(steps):
    for x in range(-3, 7):
        for y in range(-3, 7):
            if max(0, -x, x - 3) + max(0, -y, y - 3) <= steps:
                yield x, y


def place_first(window, whole, r3, r4, coef, idx):
    y_even = even(idx, 1)

    def below(n):
        return jnp.where(y_even, tile(r4, n), tile(r3, n))

    def above(n):
        return jnp.where(y_even, tile(r3, n), tile(r4, n))

    def weight(n, plane, y):
        row = window_row(plane, y)
        return coef[n, row : row + 1, :]

    count = len(REACH)
    for p in range(WX):
        for y in range(4):
            value = tile(whole, 4 * p + y)
            if y == 0:
                value = value + weight(2, p, 0) * below(count + p)
            if y == 3:
                value = value + weight(3, p, 3) * above(count + p)
            window[spot(p - 3, y), :] = 0.2 * value
    for n, (p, d) in enumerate(REACH):
        lower, upper = below(n), above(n)
        if d == 1:
            lower = lower + weight(3, p, -1) * tile(whole, 50 + p)
            upper = upper + weight(2, p, 4) * tile(whole, 40 + p)
        window[spot(p - 3, -d), :] = 0.2 * lower
        window[spot(p - 3, 3 + d), :] = 0.2 * upper


def place_second(window, own, r1, r2, r3, r4, idx):
    y_even = even(idx, 1)
    planes = window_tiles(idx, own, r1, r2)
    for p in range(WX):
        for y in range(4):
            window[spot(p - 3, y), :] = planes[p][y]
    for n, (p, d) in enumerate(REACH):
        window[spot(p - 3, -d), :] = jnp.where(y_even, tile(r4, n), tile(r3, n))
        window[spot(p - 3, 3 + d), :] = jnp.where(y_even, tile(r3, n), tile(r4, n))


def coarse_columns(kc):
    row = sublane((QC, 128))
    columns = []
    for j in range(QC):
        column = jnp.zeros((QC, 128), F32)
        for d in range(QC):
            entry = (0.2 if j == d else 0.0) - 0.2 * kc[j, d]
            column = jnp.where(row == d, entry, column)
        columns.append(column)
    return columns


def coarse_sweep(c_ref, out_ref, g_ref, coef, columns, steps):
    row = sublane((QC, 128))
    x_low, y_low, z_low = row < 4, row % 4 < 2, row % 2 == 0
    for x, y in within(steps):
        at = spot(x, y)
        c = c_ref[at, :]
        value = g_ref[at, :]
        for j in range(QC):
            value = value + columns[j] * c_ref[at.start + j : at.start + j + 1, :]
        place = window_row(x + 3, y)
        w = [coef[n, place : place + 1, :] for n in range(6)]
        along_x = jnp.where(x_low, c_ref[spot(x + 1, y), :], c_ref[spot(x - 1, y), :])
        along_y = jnp.where(y_low, c_ref[spot(x, y + 1), :], c_ref[spot(x, y - 1), :])
        along_z = jnp.where(z_low, pltpu.roll(c, 127, 1), pltpu.roll(c, 1, 1))
        faces = jnp.where(x_low, w[0], w[1]) * sub_roll(along_x, 4)
        faces = faces + jnp.where(y_low, w[2], w[3]) * jnp.where(
            y_low, sub_roll(along_y, 6), sub_roll(along_y, 2)
        )
        faces = faces + jnp.where(z_low, w[4], w[5]) * jnp.where(
            z_low, sub_roll(along_z, 7), sub_roll(along_z, 1)
        )
        out_ref[at, :] = value + 0.2 * faces


def coarse_kernel(whole, r3, r4, kc, idx, coef, m, g, pay, s1, s2, one, two):
    place_first(g, whole, r3, r4, coef, idx)
    columns = coarse_columns(kc)
    coarse_sweep(g, one, g, coef, columns, 2)
    coarse_sweep(one, two, g, coef, columns, 1)
    coarse_sweep(two, one, g, coef, columns, 0)
    for c in range(COLS):
        pay[QC * c : QC * c + QC, :] = one[spot(c // 4, c % 4), :]
    far, near = [pay[32:128, :]], [pay[0:96, :]]
    for y in range(4):
        far.append(m[48:64, (12 + y) * 128 : (13 + y) * 128])
        near.append(m[0:16, y * 128 : y * 128 + 128])
    far_near(idx, jnp.concatenate(far, axis=0), jnp.concatenate(near, axis=0), s1, s2)


def correct_kernel(
    own, r1, r2, r3, r4, kc, idx, g, coef, spread, m, gm, csr, km,
    out, s1, s2, s3, s4, one, two, x_ref, t_ref, m_ref,
):
    place_second(one, own, r1, r2, r3, r4, idx)
    columns = coarse_columns(kc)
    coarse_sweep(one, two, g, coef, columns, 2)
    coarse_sweep(two, one, g, coef, columns, 1)

    def lifted(x, y, rows):
        total = None
        for d in range(QC):
            row = spot(x, y).start + d
            part = spread[d, rows, :] * one[row : row + 1, :]
            total = part if total is None else total + part
        return total

    whole = slice(0, QM)
    for c in range(COLS):
        lanes = slice(c * 128, c * 128 + 128)
        m_ref[:, lanes] = m[:, lanes] + lifted(c // 4, c % 4, whole)
    below_x, above_x, below_y, above_y = second_edges(idx, r1, r2, r3, r4)
    below_x = below_x + jnp.concatenate([lifted(-1, y, slice(48, 64)) for y in range(4)], axis=1)
    above_x = above_x + jnp.concatenate([lifted(4, y, slice(0, 16)) for y in range(4)], axis=1)
    below_rows, above_rows = [], []
    for i in range(4):
        last, first = slice(16 * i + 8, 16 * i + 16), slice(16 * i, 16 * i + 8)
        below_rows.append(jnp.concatenate([lifted(x, -1, last) for x in range(4)], axis=1))
        above_rows.append(jnp.concatenate([lifted(x, 4, first) for x in range(4)], axis=1))
    below_y = below_y + jnp.concatenate(below_rows, axis=0)
    above_y = above_y + jnp.concatenate(above_rows, axis=0)
    mid_local(m_ref, gm, csr, km, t_ref, x_ref)
    mid_edge_terms(csr, (below_x, above_x, below_y, above_y), t_ref)
    out[...] = m_ref[...] + 0.2 * t_ref[...]
    mid_sends(out, idx, s1, s2, s3, s4)


def partners(step):
    nx, ny = lax.axis_size("gx"), lax.axis_size("yz")
    pairs = []
    for a in range(nx):
        for b in range(ny):
            to = (a, b)
            if step < 2:
                at = ((a + step) ^ 1) - step
                to = (at, b) if 0 <= at < nx else (a, b ^ 1)
            else:
                at = ((b + step - 2) ^ 1) - (step - 2)
                to = (a, at) if 0 <= at < ny else (a ^ 1, b)
            pairs.append((a * ny + b, to[0] * ny + to[1]))
    return pairs


def swap(values, step):
    return lax.ppermute(values, ("gx", "yz"), partners(step))


def exchange(sends):
    s1, s2, s3, s4 = sends
    r2, r1, r4, r3 = swap(s2, 1), swap(s1, 0), swap(s4, 3), swap(s3, 2)
    return r1, r2, r3, r4


def exchange_rows(kernel, rows, outs, idx, own, s1, s2, extra):
    r2, r1 = swap(s2, 1), swap(s1, 0)
    faces = [((rows, 128), F32), ((rows + 8, 128), F32)]
    s3, s4, *rest = call(kernel, faces + outs, (), (0,))(
        idx, own, r1, r2, extra
    )
    r3, r4 = swap(s3, 2), swap(s4, 3)
    return r1, r2, r3, r4, rest


def body(seed, scale, coef, fine, smooth, mid, coarse, pmid, plow, noise, inc):
    idx = jnp.stack(
        [
            lax.axis_index("gx"),
            lax.axis_index("yz"),
            jnp.int32(lax.axis_size("gx")),
            jnp.int32(lax.axis_size("yz")),
        ]
    ).astype(jnp.int32)
    slots = slot_matrix()
    to_slot, from_slot = jnp.asarray(slots, BF16), jnp.asarray(slots.T, BF16)

    fine_field = ((SF, LANES), F32)
    fine_faces = [((36, 512), F32)] * 2 + [((48, 512), F32), ((56, 512), F32)]
    mid_field = ((QM, LANES), F32)
    mid_faces = [((16, 512), F32)] * 2 + [((32, 512), F32), ((40, 512), F32)]
    xf = pltpu.VMEM((512, LANES), BF16)
    xm, tm = pltpu.VMEM((256, LANES), BF16), pltpu.VMEM((QM, LANES), F32)
    window = ((QC * WX * WX, 128), F32)
    windows = [pltpu.VMEM((QC * WX * WX, 128), F32)] * 2

    operands = (
        seed.reshape(QF * COLS, 128),
        scale.reshape(COLS, 128),
        coef.reshape(3 * COLS, 128),
        to_slot,
        smooth,
        fine,
        mid,
        pmid.T,
        plow.T,
    )
    g, u, csx, csr, s1, s2, s3, s4, sf, *matrices = call(
        first_kernel,
        [fine_field, fine_field, ((16, 512), F32), ((8, LANES), F32)]
        + [((48, 512), F32)] * 2
        + [((48, 512), F32)] * 2
        + [
            ((SF, 768), BF16),
            ((SF, QF), BF16),
            ((QF, QF), F32),
            ((QM, QM), F32),
            ((QM, QF), F32),
            ((QC, QM), F32),
        ],
        [pltpu.VMEM(operands[n].shape, F32) for n in (0, 1, 2, 4)]
        + [pltpu.SemaphoreType.DMA((len(operands),))],
        (9,),
        range(9),
    )(*operands, idx)
    kf, pmt, km, plt, plv = call(
        prepare_kernel,
        [
            ((SF, 768), BF16),
            ((QM, 768), BF16),
            ((QM, 256), BF16),
            ((16, 256), BF16),
            ((32, 256), BF16),
        ],
    )(*matrices)
    nf, pm, spread = call(
        late_kernel, [((QF, 768), BF16), ((SF, 256), BF16), ((QC, QM, 128), F32)]
    )(matrices[0], noise, matrices[3], matrices[4])

    def fine_local(u):
        (t,) = call(fine_local_kernel, [fine_field], [xf])(u, g, csr, kf)
        return t

    def mid_local_part(m):
        (t,) = call(mid_local_kernel, [mid_field], [xm])(m, gm, csr, km)
        return t

    first = exchange((s1, s2, s3, s4))
    u, *sends = call(
        spread_kernel,
        [fine_field] + fine_faces[:2] + [((88, 512), F32)] * 2,
        (),
        (3,),
    )(u, fine_local(u), csr, idx, *first, sf, csx)
    edges = exchange(sends)
    (coefw,) = call(coefficient_kernel, [((6, WROWS, 128), F32)], (), (0,))(
        idx, csx, first[0], first[1], edges[2], edges[3]
    )
    gm, m, *sends = call(restrict_kernel, [mid_field, mid_field] + mid_faces, (), (2,))(
        fine_local(u), csr, idx, *edges, pmt
    )
    edges = exchange(sends)
    m, own, s1, s2 = call(
        smooth_kernel,
        [mid_field, ((256, 128), F32)] + [((176, 128), F32)] * 2,
        [xm, tm],
        (3,),
    )(m, mid_local_part(m), csr, idx, *edges, gm, km, plt, plv)
    _, _, r3, r4, (whole,) = exchange_rows(
        row_kernel, QC * (len(REACH) + WX), [((480, 128), F32)], idx, own, s1, s2, coefw
    )
    gw, own, s1, s2 = call(
        coarse_kernel,
        [window, ((QC * COLS, 128), F32)] + [((160, 128), F32)] * 2,
        windows,
        (3, 4),
    )(whole, r3, r4, coarse, idx, coefw, m)
    r1, r2, r3, r4, _ = exchange_rows(
        second_row_kernel, QC * len(REACH) + 64, [], idx, own, s1, s2, m
    )
    m, *sends = call(
        correct_kernel,
        [mid_field] + mid_faces,
        windows + [xm, tm, pltpu.VMEM((QM, LANES), F32)],
        (5, 6),
    )(own, r1, r2, r3, r4, coarse, idx, gw, coefw, spread, m, gm, csr, km)
    edges = exchange(sends)
    u, *sends = call(lift_kernel, [fine_field] + fine_faces, [xm, tm], (3,))(
        m, mid_local_part(m), csr, idx, *edges, pm, u
    )
    edges = exchange(sends)
    u, *sends = call(sweep_kernel, [fine_field] + fine_faces, (), (3,))(
        u, fine_local(u), csr, idx, *edges, sf
    )
    edges = exchange(sends)
    out, prev = call(
        last_kernel,
        [((QF * COLS, 128), F32)] * 2,
        [
            pltpu.VMEM((SF, LANES), F32),
            pltpu.VMEM((QF, LANES), F32),
            pltpu.VMEM((QF * COLS, 128), F32),
            pltpu.VMEM((QF * COLS, 128), F32),
            pltpu.SemaphoreType.DMA((3,)),
        ],
        (3,),
        hbm_outs=True,
    )(u, fine_local(u), csr, idx, *edges, sf, nf, from_slot, inc.reshape(COLS, 128))
    shape = seed.shape
    return out.reshape(shape), prev.reshape(shape)


def solution(mesh):
    cell, field = P("gx", "yz", None), P(None, "gx", "yz", None)
    return jax.shard_map(
        body,
        mesh=mesh,
        in_specs=(field, cell, field) + (P(),) * 7 + (cell,),
        out_specs=(field, field),
        check_vma=False,
    )
```
